256 devices in a mesh: seq: 64 (over z, y, core), mp: 4 (over x).
Axes of the slice: x: 4, y: 4, z: 8, core: 2. Of those that a mesh axis runs over, the one named last changes fastest.
Arguments:
- residual: bfloat16 [8192, 8192], P('seq', 'mp'), may hold values from -6 to 6
- chosen_pos: int32 [3072], P('seq'), may hold values from 0 to 127, as said below
- chosen_count: int32 [64], P('seq'), may hold values from 0 to 48, as said below
- router_weight: float32 [8192], P('mp'), may hold values from -0.0625 to 0.0625
- weight_in: bfloat16 [8192, 53248], P('mp', 'seq')
- weight_out: bfloat16 [22528, 8192], P('seq', 'mp'), may hold values from -0.0390625 to 0.0390625
- cotangent: bfloat16 [8192, 8192], P('seq', 'mp'), may hold values from -6 to 6
Outputs:
- output: bfloat16 [8192, 8192], P('seq', 'mp')
- grad_residual: bfloat16 [8192, 8192], P('seq', 'mp')
The draws below stay inside these ranges and needn't reach their ends.
Inputs may be any that keep to these rules, and one draw needn't show every extreme that they name: `chosen_count`: in each aligned window of 4 consecutive sequence shards the counts sum to exactly 64; some shard holds 48. `chosen_pos`: in shard s's block, the first chosen_count[s] entries are distinct increasing local positions; the remaining entries are 0.
All inputs are finite; a program needn't handle non-finite values.
Results may differ from the reference program's by a relative error of at most 0.01.
Values may be sent and summed in bfloat16 or wider, within the bound.
A program may use at most 64 MiB of HBM per device.

```python
import jax
import jax.numpy as jnp
from jax import lax

D = 8192
HS = 128
FF_HEAD = 224
GROUP = 4
TOK_DEV = 128
HQ = 64
FF = 14336
CAP = 16
MAXSRC = 48
SEQ_LEN = 8192
ROWS = 1024
N_SEQ = 64
N_MP = 4


def shard_loads(key):
    groups = N_SEQ // GROUP
    key_one, key_two, key_three, key_four, key_five, key_six = jax.random.split(key, 6)
    first = jax.random.randint(key_one, (groups,), -CAP, CAP + 1)
    second = jax.random.randint(key_two, (groups,), -CAP, CAP + 1)
    spread = jnp.stack([CAP + first, CAP - first, CAP + second, CAP - second], axis=1)
    lighter = jax.random.randint(key_three, (groups,), 0, CAP + 1)
    heavy = jnp.stack([jnp.full((groups,), 3 * CAP, jnp.int32), jnp.zeros((groups,), jnp.int32), lighter, CAP - lighter], axis=1)
    forced = jax.random.randint(key_four, (), 0, groups)
    is_heavy = (jax.random.randint(key_five, (groups,), 0, 4) == 0) | (jnp.arange(groups) == forced)
    loads = jnp.where(is_heavy[:, None], heavy, spread)
    scores = jax.random.randint(key_six, (groups, GROUP), 0, 1 << 20) * GROUP + jnp.arange(GROUP)
    ranking = jnp.argsort(scores, axis=1)
    return jnp.take_along_axis(loads, ranking, axis=1).reshape(N_SEQ).astype(jnp.int32)


def draw_chosen_count(key, part):
    return shard_loads(key)


def draw_chosen_pos(key, part):
    loads = shard_loads(key)
    key = jax.random.fold_in(key, 5)
    scores = jax.random.randint(key, (N_SEQ, TOK_DEV), 0, 1 << 20) * TOK_DEV + jnp.arange(TOK_DEV)
    ranked = jnp.argsort(-scores, axis=1)[:, :MAXSRC]
    is_live = jnp.arange(MAXSRC)[None, :] < loads[:, None]
    picked = jnp.where(is_live, ranked, TOK_DEV)
    picked = jnp.sort(picked, axis=1)
    picked = jnp.where(picked == TOK_DEV, 0, picked)
    return picked.reshape(-1).astype(jnp.int32)


def column_scales():
    width = 3 * HS + 2 * FF_HEAD
    col = jnp.arange(width)
    scales = jnp.where(col < 2 * HS, 1.0, jnp.where(col < 3 * HS, 4.0, 0.7))
    return scales.astype(jnp.float32)


def draw_weight_in(key, part):
    key = jax.random.fold_in(key, 11)
    width = 3 * HS + 2 * FF_HEAD
    base = jnp.clip(jax.random.normal(key, (D, HQ, width), jnp.float32), -6.0, 6.0)
    scaled = base * column_scales()[None, None, :] * D ** (-0.5)
    return scaled.reshape(D, HQ * width).astype(jnp.bfloat16)


def level_of(own_key, extent, cuts, low, largest):
    factor_of = 1.0
    for position, shards_of in cuts:
        steps = jax.random.uniform(jax.random.fold_in(jax.random.fold_in(own_key, 6), position), (shards_of,), jnp.float32, low / len(cuts), largest / len(cuts))
        factor_of = factor_of * jnp.repeat(jnp.exp(steps), extent[position] // shards_of).reshape((-1,) + (1,) * (len(extent) - 1 - position))
    return factor_of


def gaussian(rng, shape, scale, limit, cuts=(), held_as=jnp.bfloat16):
    result = scale * jax.random.normal(rng, shape, jnp.float32)
    if cuts:
        result = result * level_of(rng, shape, cuts, -0.22, 0.18)
    return jnp.clip(result, -limit, limit).astype(held_as)


def setup_inputs(seed: int = 0) -> dict:
    splits = jax.random.split(jax.random.key(seed), 8)
    residual = gaussian(splits[0], (SEQ_LEN, D), 1.0, 6.0, ((0, 64), (1, 4)))
    chosen_pos = draw_chosen_pos(jax.random.fold_in(splits[7], 71), 0)
    chosen_count = draw_chosen_count(jax.random.fold_in(splits[7], 71), 0)
    router_weight = gaussian(splits[3], (D,), D ** -0.5, 0.0625, ((0, 4),), jnp.float32)
    weight_in = draw_weight_in(jax.random.fold_in(splits[7], 71), 0)
    weight_out = gaussian(splits[5], (HQ * (HS + FF_HEAD), D), (HQ * HS + FF) ** -0.5, 0.0390625, ((0, 64), (1, 4)))
    cotangent = gaussian(splits[6], (SEQ_LEN, D), 1.0, 6.0, ((0, 64), (1, 4)))
    return dict(residual=residual, chosen_pos=chosen_pos, chosen_count=chosen_count, router_weight=router_weight, weight_in=weight_in, weight_out=weight_out, cotangent=cotangent)


def norm_rows(values, epsilon):
    scale = lax.rsqrt(lax.optimization_barrier(jnp.mean(values * values, axis=-1, keepdims=True)) + epsilon)
    return (values * scale, scale)

def norm_back(values, scale, grads):
    return scale * grads - values * scale ** 3 * lax.optimization_barrier(jnp.mean(grads * values, axis=-1, keepdims=True))

def quarter_product(left, right, right_cols):
    quarter = D // N_MP
    total = None
    for part_id in range(N_MP):
        left_part = left[:, part_id * quarter:(part_id + 1) * quarter]
        if right_cols:
            right_part = right[:, part_id * quarter:(part_id + 1) * quarter].T
        else:
            right_part = right[part_id * quarter:(part_id + 1) * quarter]
        term = jnp.dot(left_part, right_part, preferred_element_type=jnp.float32).astype(jnp.bfloat16)
        term = lax.optimization_barrier(term).astype(jnp.float32)
        total = term if total is None else total + term
    return total

def reference(residual, chosen_pos, chosen_count, router_weight, weight_in, weight_out, cotangent):
    shard_ids = jnp.arange(N_SEQ, dtype=jnp.int32)
    slot_ids = jnp.arange(MAXSRC, dtype=jnp.int32)
    chosen = chosen_count.astype(jnp.int32)
    before = (jnp.cumsum(chosen) - chosen).astype(jnp.int32)
    is_valid = slot_ids[None, :] < chosen[:, None]
    target = jnp.where(is_valid, before[:, None] + slot_ids[None, :], ROWS).astype(jnp.int32)
    tokens_at = (shard_ids[:, None] * TOK_DEV + chosen_pos.reshape(N_SEQ, MAXSRC)).astype(jnp.int32)
    compact_tok = jnp.zeros((ROWS,), jnp.int32).at[target.reshape(-1)].set(tokens_at.reshape(-1), mode='drop')
    rows = residual[compact_tok]
    rows_f = rows.astype(jnp.float32)
    gate_value = jax.nn.sigmoid(lax.optimization_barrier(jnp.sum(rows_f * router_weight, axis=-1)))
    normed, in_scale = norm_rows(rows_f, 1e-05)
    project = quarter_product(normed.astype(jnp.bfloat16), weight_in, False)
    ffd = FF // HQ
    block = project.reshape(ROWS, HQ, 3 * HS + 2 * ffd)
    query = block[:, :, :HS]
    keyraw = block[:, :, HS:2 * HS]
    values = block[:, :, 2 * HS:3 * HS].astype(jnp.bfloat16)
    gate_in = block[:, :, 3 * HS:3 * HS + ffd]
    up_in = block[:, :, 3 * HS + ffd:]
    query_n, query_scale = norm_rows(query, 1e-06)
    key_n, key_scale = norm_rows(keyraw, 1e-06)
    query_b = jnp.moveaxis(query_n.astype(jnp.bfloat16), 1, 0)
    key_b = jnp.moveaxis(key_n.astype(jnp.bfloat16), 1, 0)
    value_b = jnp.moveaxis(values, 1, 0)
    positions = jnp.arange(ROWS, dtype=jnp.int32)
    causal = positions[None, :] <= positions[:, None]
    factor = HS ** (-0.5)

    def head_scores(query_h, key_h):
        raw = jnp.dot(query_h, key_h.T, preferred_element_type=jnp.float32)
        return jnp.where(causal, jnp.exp(raw * factor), jnp.float32(0.0))

    def head_forward(operands):
        query_h, key_h, value_h = operands
        expo = head_scores(query_h, key_h)
        denom = lax.optimization_barrier(jnp.sum(expo, axis=-1))
        summed = jnp.dot(expo.astype(jnp.bfloat16), value_h, preferred_element_type=jnp.float32)
        return (summed / denom[:, None]).astype(jnp.bfloat16)
    attended = jnp.moveaxis(lax.map(head_forward, (query_b, key_b, value_b)), 0, 1)
    sigma = jax.nn.sigmoid(gate_in)
    hidden = (gate_in * sigma * up_in).astype(jnp.bfloat16)
    joined = jnp.concatenate([attended, hidden], axis=-1).reshape(ROWS, HQ * (HS + ffd))
    delta = jnp.dot(joined, weight_out, preferred_element_type=jnp.float32).astype(jnp.bfloat16)
    out_rows = (rows_f + gate_value[:, None] * delta.astype(jnp.float32)).astype(jnp.bfloat16)
    output = residual.at[compact_tok].set(out_rows)
    grad_rows = cotangent[compact_tok]
    grad_f = grad_rows.astype(jnp.float32)
    dgate = lax.optimization_barrier(jnp.sum(grad_f * delta.astype(jnp.float32), axis=-1))
    dlogit = dgate * gate_value * (1.0 - gate_value)
    ddelta = (gate_value[:, None] * grad_f).astype(jnp.bfloat16)
    djoined = quarter_product(ddelta, weight_out, True).reshape(ROWS, HQ, HS + ffd)
    dattended = djoined[:, :, :HS].astype(jnp.bfloat16)
    dhidden = djoined[:, :, HS:]
    dup = (dhidden * gate_in * sigma).astype(jnp.bfloat16)
    dgate_in = (dhidden * up_in * sigma * (1.0 + gate_in * (1.0 - sigma))).astype(jnp.bfloat16)

    def head_backward(operands):
        query_h, key_h, value_h, dout_h = operands
        expo = head_scores(query_h, key_h)
        denom = lax.optimization_barrier(jnp.sum(expo, axis=-1))
        prob = expo / denom[:, None]
        dprob = jnp.dot(dout_h, value_h.T, preferred_element_type=jnp.float32)
        inner = lax.optimization_barrier(jnp.sum(prob * dprob, axis=-1))
        dscore = (prob * (dprob - inner[:, None])).astype(jnp.bfloat16)
        dquery_h = jnp.dot(dscore, key_h, preferred_element_type=jnp.float32) * factor
        dkey_h = jnp.dot(dscore.T, query_h, preferred_element_type=jnp.float32) * factor
        dvalue_h = jnp.dot(prob.astype(jnp.bfloat16).T, dout_h, preferred_element_type=jnp.float32)
        return (dquery_h, dkey_h, dvalue_h)
    dout_b = jnp.moveaxis(dattended, 1, 0)
    dquery_n, dkey_n, dvalues = lax.map(head_backward, (query_b, key_b, value_b, dout_b))
    dquery = norm_back(query, query_scale, jnp.moveaxis(dquery_n, 0, 1)).astype(jnp.bfloat16)
    dkey = norm_back(keyraw, key_scale, jnp.moveaxis(dkey_n, 0, 1)).astype(jnp.bfloat16)
    dvalue = jnp.moveaxis(dvalues, 0, 1).astype(jnp.bfloat16)
    dproject = jnp.concatenate([dquery, dkey, dvalue, dgate_in, dup], axis=-1).reshape(ROWS, HQ * (3 * HS + 2 * ffd))
    dnormed = jnp.dot(dproject, weight_in.T, preferred_element_type=jnp.float32)
    dinput = norm_back(rows_f, in_scale, dnormed).astype(jnp.bfloat16)
    grad_out = (grad_f + dinput.astype(jnp.float32) + dlogit[:, None] * router_weight).astype(jnp.bfloat16)
    grad_residual = cotangent.at[compact_tok].set(grad_out)
    return (output, grad_residual)
```

```python
import functools

import jax
import jax.numpy as jnp
from jax import lax
from jax.experimental import pallas as pl
from jax.experimental.pallas import tpu as pltpu
from jax.sharding import PartitionSpec as P

MESH = pl.DeviceIdType.MESH
D = 8192
HS = 128
NZ, NY, NX = 8, 4, 4
CAP = 16
QD = D // NX
FFD = 224
WIN = 3 * HS + 2 * FFD
WINP = 896
WOUT = HS + FFD
WOUTP = 384
ROWS = 1024
BLK = 256
HALF = QD // 2
F32 = jnp.float32
BF16 = jnp.bfloat16
FACTOR = HS ** (-0.5)


def mod(value, n):
    return lax.rem(value + n, n)


def dot_nn(a, b):
    return jnp.dot(a, b, preferred_element_type=F32)


def dot_nt(a, b):
    return lax.dot_general(a, b, (((1,), (1,)), ((), ())), preferred_element_type=F32)


def dot_tn(a, b):
    return lax.dot_general(a, b, (((0,), (0,)), ((), ())), preferred_element_type=F32)


class Net:
    def __init__(self, send_sem, recv_sem):
        self.send_sem, self.recv_sem = send_sem, recv_sem
        self.used = 0
        self.sent = []
        seq = lax.axis_index("seq")
        self.x = lax.axis_index("mp")
        self.z = lax.div(seq, NY * 2)
        self.y = lax.rem(lax.div(seq, 2), NY)
        self.c = lax.rem(seq, 2)
        self.o = 1 - self.c
        self.yw = self.y + 1 - 2 * lax.rem(self.y, 2)
        z, y, c, x = self.z, self.y, self.c, self.x
        self.sib = self.at(z, y, self.o, x)
        self.zp, self.zm = self.at(mod(z + 1, NZ), y, c, x), self.at(mod(z - 1, NZ), y, c, x)
        self.yp, self.ym = self.at(z, mod(y + 1, NY), c, x), self.at(z, mod(y - 1, NY), c, x)
        self.xp, self.xm = (self.at(z, y, c, mod(x + 1, NX)), self.at(z, y, c, mod(x - 1, NX)))
        self.xo = self.at(z, y, c, mod(x + 2, NX))
        self.mate = self.at(z, self.yw, c, x)
        self.diag = self.at(z, self.yw, self.o, x)
        self.w = lax.rem(y, 2) * 2 + c
        self.window = (
            (self.sib, lax.rem(y, 2) * 2 + self.o),
            (self.mate, lax.rem(self.yw, 2) * 2 + c),
            (self.diag, lax.rem(self.yw, 2) * 2 + self.o),
        )

    def at(self, z, y, c, x):
        return ((z * NY + y) * 2 + c, x)

    def enter(self):
        barrier = pltpu.get_barrier_semaphore()
        partners = (self.sib, self.diag, self.zp, self.zm, self.yp, self.ym, self.xp, self.xm, self.xo)
        for partner in partners:
            pl.semaphore_signal(barrier, inc=1, device_id=partner, device_id_type=MESH)
        pl.semaphore_wait(barrier, len(partners))

    def send(self, src, dst, device):
        copy = pltpu.make_async_remote_copy(
            src_ref=src,
            dst_ref=dst,
            send_sem=self.send_sem.at[self.used],
            recv_sem=self.recv_sem.at[self.used],
            device_id=device,
            device_id_type=MESH,
        )
        self.used += 1
        self.sent.append(copy)
        copy.start()
        return copy

    def finish(self):
        for copy in self.sent:
            copy.wait_send()


def arrive(*copies):
    for copy in copies:
        copy.wait_recv()


class MpSum:
    def __init__(self, net, part, first, second):
        self.net, self.part, self.first, self.second = net, part, first, second

    def a(self):
        net, far = self.net, mod(self.net.x + 2, NX)
        self.copies = (
            net.send(self.part.at[far, 0], self.first.at[0], net.xp),
            net.send(self.part.at[far, 1], self.first.at[1], net.xm),
        )

    def b(self):
        net = self.net
        right, left = mod(net.x + 1, NX), mod(net.x - 1, NX)
        arrive(*self.copies)
        self.part[right, 0] = (self.part[right, 0].astype(F32) + self.first[0].astype(F32)).astype(BF16)
        self.part[left, 1] = (self.part[left, 1].astype(F32) + self.first[1].astype(F32)).astype(BF16)
        self.copies = (
            net.send(self.part.at[right], self.second.at[0], net.xp),
            net.send(self.part.at[left], self.second.at[1], net.xm),
        )

    def c(self):
        arrive(*self.copies)
        return self.part[self.net.x].astype(F32) + self.second[0].astype(F32) + self.second[1].astype(F32)


class MpGather:
    def __init__(self, net, full, lanes):
        self.net, self.full, self.lanes = net, full, lanes

    def a(self):
        net, block = self.net, self.full.at[self.net.x, :, self.lanes]
        self.copies = (net.send(block, block, net.xp), net.send(block, block, net.xm))

    def b(self):
        net = self.net
        arrive(*self.copies)
        left = self.full.at[mod(net.x - 1, NX), 0 : BLK // 2, self.lanes]
        right = self.full.at[mod(net.x + 1, NX), BLK // 2 : BLK, self.lanes]
        self.copies = (net.send(left, left, net.xp), net.send(right, right, net.xm))

    def c(self):
        arrive(*self.copies)


def chain(net, n, pos, right, left, block, from_left, from_right):
    hops = n // 2
    half = HALF // 2
    far = mod(pos + hops, n)
    low = net.send(block(far, 0, half), from_left.at[0, ..., 0:half], right)
    high = net.send(block(far, half, HALF), from_right.at[0, ..., half:HALF], left)
    yield
    for step in range(1, hops):
        lo, hi = (0, half) if step == 1 else (0, HALF)
        target = block(mod(pos + hops - step, n), lo, hi)
        arrive(low)
        target[...] = (target[...].astype(F32) + from_left[step - 1, ..., lo:hi].astype(F32)).astype(BF16)
        low = net.send(block(mod(pos + hops - step, n), 0, HALF), from_left.at[step], right)
        lo, hi = (half, HALF) if step == 1 else (0, HALF)
        target = block(mod(pos - hops + step, n), lo, hi)
        arrive(high)
        target[...] = (target[...].astype(F32) + from_right[step - 1, ..., lo:hi].astype(F32)).astype(BF16)
        high = net.send(block(mod(pos - hops + step, n), 0, HALF), from_right.at[step], left)
        yield
    arrive(low, high)


def seq_sum_parts(net, bufs, out):
    part, _, qa, qb, azl, azr, ayl, ayr, byl, byr, bzl, bzr = bufs
    z, y, c = net.z, net.y, net.c

    def half_a():
        block = lambda t, lo, hi: part.at[c, t, :, :, lo:hi]
        yield from chain(net, NZ, z, net.zp, net.zm, block, azl, azr)
        qa[...] = (
            part[c, z, :, :, 0:HALF].astype(F32) + azl[NZ // 2 - 1].astype(F32) + azr[NZ // 2 - 1].astype(F32)
        ).astype(BF16)
        block = lambda t, lo, hi: qa.at[t, :, lo:hi]
        yield from chain(net, NY, y, net.yp, net.ym, block, ayl, ayr)
        out[:, 0:HALF] = qa[y].astype(F32) + ayl[NY // 2 - 1].astype(F32) + ayr[NY // 2 - 1].astype(F32)

    def half_b():
        block = lambda t, lo, hi: part.at[c, :, t, :, HALF + lo : HALF + hi]
        yield from chain(net, NY, y, net.yp, net.ym, block, byl, byr)
        qb[...] = (
            part[c, :, y, :, HALF:QD].astype(F32) + byl[NY // 2 - 1].astype(F32) + byr[NY // 2 - 1].astype(F32)
        ).astype(BF16)
        block = lambda t, lo, hi: qb.at[t, :, lo:hi]
        yield from chain(net, NZ, z, net.zp, net.zm, block, bzl, bzr)
        out[:, HALF:QD] = qb[z].astype(F32) + bzl[NZ // 2 - 1].astype(F32) + bzr[NZ // 2 - 1].astype(F32)

    return [half_b(), half_a()]


def turn(parts):
    left = []
    for part in parts:
        try:
            next(part)
            left.append(part)
        except StopIteration:
            pass
    return left


def sum_cores(net, bufs, product):
    part, other = bufs[0], bufs[1]
    copies = []
    for pair in range(NZ // 2):
        rows = product(pair)
        for owner in range(NX):
            for place in range(2):
                z = 2 * pair + place
                y = (owner - z) % NY
                for core in range(2):
                    at = ((owner * 2 + place) * 2 + core) * CAP
                    part[core, z, y] = rows[at : at + CAP].astype(BF16)
        copies.append(
            net.send(part.at[net.o, 2 * pair : 2 * pair + 2], other.at[2 * pair : 2 * pair + 2], net.sib)
        )
    for pair in range(NZ // 2):
        arrive(copies[pair])
        for z in (2 * pair, 2 * pair + 1):
            part[net.c, z] = (part[net.c, z].astype(F32) + other[z].astype(F32)).astype(BF16)


def kernel(
    count_ref, onehot_ref, res_ref, cot_ref, rw_ref, win_ref, wout_ref,
    output_ref, grad_ref,
    send_sem, recv_sem, winp, woutp, counts, contrib, routed, g0, g1,
    pr, pra, prb, pd, pda, pdb, proj, dj, kv, joined, dproj, kg, kga, kgb,
    delta, dnormed, stats, fin, *chains,
):
    net = Net(send_sem, recv_sem)
    x, y, z, c = net.x, net.y, net.z, net.c
    net.enter()

    counts[net.w] = count_ref[...]
    copies = [net.send(count_ref, counts.at[net.w], partner) for partner, _ in net.window]
    winp[:, 768:896] = jnp.zeros((QD, 128), BF16)
    winp[:, 0:WIN] = win_ref[...]
    woutp[0:WOUT] = wout_ref[...]
    woutp[WOUT:WOUTP] = jnp.zeros((WOUTP - WOUT, QD), BF16)
    arrive(*copies)
    before = jnp.zeros((1, 128), jnp.int32)
    for place in range(4):
        earlier = jnp.where(place < net.w, jnp.int32(1), jnp.int32(0))
        before = before + counts[place, 0:1, :] * earlier
    at_row = lax.broadcasted_iota(jnp.int32, (64, 128), 0)
    at_slot = lax.broadcasted_iota(jnp.int32, (64, 128), 1)
    place_of = jnp.where(at_row - at_slot == before, F32(1.0), F32(0.0)).astype(BF16)
    sel = dot_nn(place_of, onehot_ref[...]).astype(BF16)

    copies = []
    for which, source in enumerate((res_ref, cot_ref)):
        contrib[which] = dot_nn(sel, source[...]).astype(BF16).reshape(4, CAP, QD)
        copies.append(
            [
                net.send(contrib.at[which, theirs], routed.at[which, slot], partner)
                for slot, (partner, theirs) in enumerate(net.window)
            ]
        )
    for which, g in enumerate((g0, g1)):
        arrive(*copies[which])
        total = contrib[which, net.w].astype(F32)
        for slot in range(3):
            total = total + routed[which, slot].astype(F32)
        g[z, y, c] = total.astype(BF16)

    def same(ref, device):
        return net.send(ref, ref, device)

    own = g0.at[z, y, c]
    r_copies = (same(own, net.yp), same(own, net.ym))
    own = g1.at[z, y, c]
    d_copies = (same(own, net.zp), same(own, net.zm))
    arrive(*r_copies)
    r_copies = (
        same(g0.at[z, mod(y - 1, NY), c, :, 0:HALF], net.yp),
        same(g0.at[z, mod(y + 1, NY), c, :, HALF:QD], net.ym),
    )

    def d_ring(step):
        arrive(*d_copies)
        if step < 4:
            return (
                same(g1.at[mod(z - step + 1, NZ), y, c], net.zp),
                same(g1.at[mod(z + step - 1, NZ), y, c], net.zm),
            )
        return (
            same(g1.at[mod(z - 3, NZ), y, c, :, 0:HALF], net.zp),
            same(g1.at[mod(z + 3, NZ), y, c, :, HALF:QD], net.zm),
        )

    d_copies = d_ring(2)
    arrive(*r_copies)
    r_copies = (same(g0.at[z, :, c], net.zp), same(g0.at[z, :, c], net.zm))
    sib_own = same(g0.at[z, :, c], net.sib)
    d_copies = d_ring(3)
    d_copies = d_ring(4)

    lane = lax.broadcasted_iota(jnp.int32, (BLK, 128), 1)

    def in_stage(stage, pair):
        rows = g0[pl.ds(2 * pair, 2)].reshape(BLK, QD)
        result = dot_nn(rows, winp[...])
        rows_f = rows.astype(F32)
        tail = result[:, 768:896]
        at = WIN - 768
        for value in (
            jnp.sum(rows_f * rows_f, axis=-1, keepdims=True),
            jnp.sum(rows_f * rw_ref[...], axis=-1, keepdims=True),
        ):
            for _ in range(3):
                rounded = value.astype(BF16).astype(F32)
                tail = jnp.where(lane == at, rounded, tail)
                value = value - rounded
                at += 1
        result = result.astype(BF16)
        tail = tail.astype(BF16)
        for place in range(2):
            for row in range(NY):
                owner = lax.rem(2 * pair + place + row, NX)
                at = (place * NY + row) * 32
                pr[stage, owner, place, :, 0:768] = result[at : at + 32, 0:768]
                pr[stage, owner, place, :, 768:896] = tail[at : at + 32]
        summed = MpSum(net, pr.at[stage], pra.at[stage], prb.at[stage])
        summed.a()
        return summed, pair

    def in_done(item):
        summed, pair = item
        proj[pl.ds(2 * pair, 2)] = summed.c()

    def back_stage(stage, row):
        rows = g1[:, row].reshape(BLK, QD)
        result = dot_nt(rows, woutp[...]).astype(BF16)
        for place in range(NZ):
            owner = lax.rem(row + place, NX)
            pd[stage, owner, place // 4] = result[place * 32 : place * 32 + 32]
        summed = MpSum(net, pd.at[stage], pda.at[stage], pdb.at[stage])
        summed.a()
        return summed, row

    def back_done(item):
        summed, row = item
        total = summed.c()
        first = mod(x - row, NX)
        dj[first] = total[0]
        dj[first + 4] = total[1]

    pair = lax.div(z, 2)
    turned = 2 * lax.rem(z, 2) - 1
    order = (pair, mod(pair + turned, 4), mod(pair - turned, 4), mod(pair + 2, 4))

    def r_ring(step):
        arrive(*r_copies)
        if step < 4:
            near, far = mod(z - step + 1, NZ), mod(z + step - 1, NZ)
            copies = (same(g0.at[near, :, c], net.zp), same(g0.at[far, :, c], net.zm))
        else:
            near, far = mod(z - 3, NZ), mod(z + 3, NZ)
            copies = (
                same(g0.at[near, :, c, :, 0:HALF], net.zp),
                same(g0.at[far, :, c, :, HALF:QD], net.zm),
            )
        return copies, (same(g0.at[near, :, c], net.sib), same(g0.at[far, :, c], net.sib))

    r_copies, sibs = r_ring(2)
    arrive(*d_copies)
    d_copies = (same(g1.at[:, y, c], net.yp), same(g1.at[:, y, c], net.ym))
    d_sib = same(g1.at[:, y, c], net.sib)
    arrive(sib_own, *sibs)
    in_1 = in_stage(0, order[0])
    r_copies, sibs = r_ring(3)
    arrive(d_sib)
    back_1 = back_stage(0, y)
    in_1[0].b()
    arrive(*sibs)
    in_2 = in_stage(1, order[1])
    r_copies, sibs = r_ring(4)
    back_1[0].b()
    in_2[0].b()
    arrive(*d_copies)
    below, above = mod(y - 1, NY), mod(y + 1, NY)
    d_copies = (
        same(g1.at[:, below, c, :, 0:HALF], net.yp),
        same(g1.at[:, above, c, :, HALF:QD], net.ym),
    )
    d_sibs = (same(g1.at[:, below, c], net.sib), same(g1.at[:, above, c], net.sib))
    arrive(*sibs)
    in_3 = in_stage(2, order[2])
    arrive(*r_copies)
    sib_last = same(g0.at[mod(z + 4, NZ), :, c], net.sib)
    arrive(d_sibs[0])
    back_2 = back_stage(1, below)
    in_3[0].b()
    arrive(sib_last)
    in_4 = in_stage(3, order[3])
    back_2[0].b()
    arrive(d_sibs[1])
    back_3 = back_stage(2, above)
    in_4[0].b()
    arrive(*d_copies)
    opposite = mod(y + 2, NY)
    d_last = same(g1.at[:, opposite, c], net.sib)
    back_3[0].b()
    in_done(in_1)
    in_done(in_2)
    arrive(d_last)
    back_4 = back_stage(3, opposite)
    in_done(in_3)
    in_done(in_4)
    back_4[0].b()

    tail = proj[:, :, 768:896].reshape(BLK, 128)
    at = WIN - 768
    square = jnp.sum(jnp.where((lane >= at) & (lane < at + 3), tail, 0.0), axis=-1, keepdims=True)
    logit = jnp.sum(jnp.where((lane >= at + 3) & (lane < at + 6), tail, 0.0), axis=-1, keepdims=True)
    in_scale = lax.rsqrt(square / D + 1e-05)
    gate = jax.nn.sigmoid(logit)
    query = proj[:, :, 0:HS].reshape(BLK, HS) * in_scale
    keyraw = proj[:, :, HS : 2 * HS].reshape(BLK, HS) * in_scale
    values = proj[:, :, 2 * HS : 3 * HS].reshape(BLK, HS) * in_scale
    query_scale = lax.rsqrt(jnp.mean(query * query, axis=-1, keepdims=True) + 1e-06)
    key_scale = lax.rsqrt(jnp.mean(keyraw * keyraw, axis=-1, keepdims=True) + 1e-06)
    query_b = (query * query_scale).astype(BF16)
    kv[x, :, 0:HS] = (keyraw * key_scale).astype(BF16)
    kv[x, :, HS : 2 * HS] = values.astype(BF16)
    kv_ring = MpGather(net, kv, slice(0, 2 * HS))
    kv_ring.a()

    gate_up = proj[:, :, 384:896].reshape(BLK, 512) * in_scale
    gate_in = gate_up[:, 0:FFD]
    up_in = gate_up[:, FFD : 2 * FFD]
    sigma = jax.nn.sigmoid(gate_in)
    joined[x, :, 256:384] = jnp.zeros((BLK, 128), BF16)
    joined[x, :, HS : HS + FFD] = (gate_in * sigma * up_in).astype(BF16)
    hid_ring = MpGather(net, joined, slice(HS, WOUTP))
    hid_ring.a()

    for item in (back_1, back_2, back_3, back_4):
        back_done(item)
    dattended = (dj[:, :, 0:HS].reshape(BLK, HS) * gate).astype(BF16)
    dhidden = dj[:, :, HS:WOUTP].reshape(BLK, 256)[:, 0:FFD] * gate
    dup = (dhidden * gate_in * sigma).astype(BF16)
    dgate_in = (dhidden * up_in * sigma * (1.0 + gate_in * (1.0 - sigma))).astype(BF16)
    dproj[x, :, 384:896] = jnp.concatenate([dgate_in, dup, jnp.zeros((BLK, 64), BF16)], axis=-1)
    ff_ring = MpGather(net, dproj, slice(384, WINP))
    kv_ring.b()
    ff_ring.a()
    hid_ring.b()
    kv_ring.c()

    keys = kv[:, :, 0:HS].reshape(ROWS, HS)
    vals = kv[:, :, HS : 2 * HS].reshape(ROWS, HS)
    row = lax.broadcasted_iota(jnp.int32, (BLK, 1), 0)
    row_z = row >> 5
    query_order = row_z * 128 + ((x + 8 - row_z) & 3) * 32 + (row & 31)
    col = lax.broadcasted_iota(jnp.int32, (1, ROWS), 1)
    col_z = (col >> 5) & 7
    key_order = col_z * 128 + (((col >> 8) + 8 - col_z) & 3) * 32 + (col & 31)
    visible = key_order <= query_order
    expo = jnp.where(visible, jnp.exp(dot_nt(query_b, keys) * FACTOR), 0.0)
    inverse = 1.0 / jnp.sum(expo, axis=-1, keepdims=True)
    joined[x, :, 0:HS] = (dot_nn(expo.astype(BF16), vals) * inverse).astype(BF16)
    att_ring = MpGather(net, joined, slice(0, HS))
    att_ring.a()

    prob = expo * inverse
    dprob = dot_nt(dattended, vals)
    inner = jnp.sum(prob * dprob, axis=-1, keepdims=True)
    dscore = (prob * (dprob - inner)).astype(BF16)
    prob_b = prob.astype(BF16)
    dkey_part = dot_tn(dscore, query_b) * FACTOR
    dvalue_part = dot_tn(prob_b, dattended)
    for owner in range(NX):
        for place in range(2):
            at = (owner * 2 + place) * 128
            kg[owner, place, :, 0:HS] = dkey_part[at : at + 128].astype(BF16)
            kg[owner, place, :, HS : 2 * HS] = dvalue_part[at : at + 128].astype(BF16)
    kg_sum = MpSum(net, kg, kga, kgb)
    kg_sum.a()
    att_ring.b()
    dquery_n = dot_nn(dscore, keys) * FACTOR
    ff_ring.b()

    def norm_back(values, scale, grads):
        return scale * grads - values * scale**3 * jnp.mean(grads * values, axis=-1, keepdims=True)

    dproj[x, :, 0:HS] = norm_back(query, query_scale, dquery_n).astype(BF16)
    kg_sum.b()
    hid_ring.c()
    att_ring.c()

    delta_bufs, dnormed_bufs = chains[:12], chains[12:]

    def delta_rows(pair):
        return dot_nn(joined[:, pair * 64 : pair * 64 + 64].reshape(BLK, WOUTP), woutp[...])

    sum_cores(net, delta_bufs, delta_rows)
    parts = turn(seq_sum_parts(net, delta_bufs, delta))
    key_grad = kg_sum.c().reshape(BLK, 2 * HS)
    dproj[x, :, HS : 2 * HS] = norm_back(keyraw, key_scale, key_grad[:, 0:HS]).astype(BF16)
    dproj[x, :, 2 * HS : 3 * HS] = key_grad[:, HS : 2 * HS].astype(BF16)
    qkv_ring = MpGather(net, dproj, slice(0, 3 * HS))
    qkv_ring.a()
    parts = turn(parts)
    qkv_ring.b()
    parts = turn(parts)
    ff_ring.c()
    qkv_ring.c()

    def dnormed_rows(pair):
        return dot_nt(dproj[:, pair * 64 : pair * 64 + 64].reshape(BLK, WINP), winp[...])

    sum_cores(net, dnormed_bufs, dnormed_rows)
    more = turn(seq_sum_parts(net, dnormed_bufs, dnormed))
    while parts or more:
        parts = turn(parts)
        more = turn(more)

    rows = g0[z, y, c].astype(F32)
    grads = g1[z, y, c].astype(F32)
    rw = rw_ref[...]
    delta_b = delta[...].astype(BF16).astype(F32)
    dn = dnormed[...]
    small = lax.broadcasted_iota(jnp.int32, (CAP, 128), 1)
    tile = jnp.zeros((CAP, 128), F32)
    for at, product in enumerate((rows * rows, rows * rw, grads * delta_b, dn * rows)):
        tile = jnp.where(small == at, jnp.sum(product, axis=-1, keepdims=True), tile)
    stats[3] = tile
    arrive(*[net.send(stats.at[3], stats.at[slot], device) for slot, device in enumerate((net.xp, net.xo, net.xm))])
    tile = stats[0] + stats[1] + stats[2] + stats[3]

    def pick(at):
        return jnp.sum(jnp.where(small == at, tile, 0.0), axis=-1, keepdims=True)

    in_scale = lax.rsqrt(pick(0) / D + 1e-05)
    gate = jax.nn.sigmoid(pick(1))
    dlogit = pick(2) * gate * (1.0 - gate)
    dinput = (in_scale * dn - rows * in_scale**3 * (pick(3) / D)).astype(BF16).astype(F32)
    fin[0, net.w] = (rows + gate * delta_b).astype(BF16)
    fin[1, net.w] = (grads + dinput + dlogit * rw).astype(BF16)
    copies = [
        net.send(fin.at[which, net.w], fin.at[which, net.w], partner)
        for which in range(2)
        for partner, _ in net.window
    ]
    chosen = dot_tn(sel, jnp.ones((64, 128), BF16))[:, 0:1] > 0.5
    for which, (source, target) in enumerate(((res_ref, output_ref), (cot_ref, grad_ref))):
        arrive(*copies[which * 3 : which * 3 + 3])
        back = dot_tn(sel, fin[which].reshape(64, QD)).astype(BF16)
        target[...] = jnp.where(chosen, back, source[...])
    net.finish()


def chain_scratch():
    return [
        pltpu.VMEM((2, NZ, NY, CAP, QD), BF16),
        pltpu.VMEM((NZ, NY, CAP, QD), BF16),
        pltpu.VMEM((NY, CAP, HALF), BF16),
        pltpu.VMEM((NZ, CAP, HALF), BF16),
        pltpu.VMEM((NZ // 2, NY, CAP, HALF), BF16),
        pltpu.VMEM((NZ // 2, NY, CAP, HALF), BF16),
        pltpu.VMEM((NY // 2, CAP, HALF), BF16),
        pltpu.VMEM((NY // 2, CAP, HALF), BF16),
        pltpu.VMEM((NY // 2, NZ, CAP, HALF), BF16),
        pltpu.VMEM((NY // 2, NZ, CAP, HALF), BF16),
        pltpu.VMEM((NZ // 2, CAP, HALF), BF16),
        pltpu.VMEM((NZ // 2, CAP, HALF), BF16),
    ]


def local(residual, chosen_pos, chosen_count, router_weight, weight_in, weight_out, cotangent):
    slots = jnp.arange(128, dtype=jnp.int32)
    position = jnp.pad(chosen_pos, (0, 128 - chosen_pos.shape[0]))
    onehot = ((position[:, None] == slots[None, :]) & (slots < chosen_count[0])[:, None]).astype(BF16)
    counts = jnp.broadcast_to(chosen_count[0], (8, 128)).astype(jnp.int32)
    n_sem = 192
    scratch = [
        pltpu.SemaphoreType.DMA((n_sem,)),
        pltpu.SemaphoreType.DMA((n_sem,)),
        pltpu.VMEM((QD, WINP), BF16),
        pltpu.VMEM((WOUTP, QD), BF16),
        pltpu.VMEM((4, 8, 128), jnp.int32),
        pltpu.VMEM((2, 4, CAP, QD), BF16),
        pltpu.VMEM((2, 3, CAP, QD), BF16),
        pltpu.VMEM((NZ, NY, 2, CAP, QD), BF16),
        pltpu.VMEM((NZ, NY, 2, CAP, QD), BF16),
        pltpu.VMEM((4, NX, 2, 32, WINP), BF16),
        pltpu.VMEM((4, 2, 32, WINP), BF16),
        pltpu.VMEM((4, 2, 2, 32, WINP), BF16),
        pltpu.VMEM((4, NX, 2, 32, WOUTP), BF16),
        pltpu.VMEM((4, 2, 32, WOUTP), BF16),
        pltpu.VMEM((4, 2, 2, 32, WOUTP), BF16),
        pltpu.VMEM((NZ, 32, WINP), F32),
        pltpu.VMEM((NZ, 32, WOUTP), F32),
        pltpu.VMEM((NX, BLK, 2 * HS), BF16),
        pltpu.VMEM((NX, BLK, WOUTP), BF16),
        pltpu.VMEM((NX, BLK, WINP), BF16),
        pltpu.VMEM((NX, 2, 128, 2 * HS), BF16),
        pltpu.VMEM((2, 128, 2 * HS), BF16),
        pltpu.VMEM((2, 2, 128, 2 * HS), BF16),
        pltpu.VMEM((CAP, QD), F32),
        pltpu.VMEM((CAP, QD), F32),
        pltpu.VMEM((4, CAP, 128), F32),
        pltpu.VMEM((2, 4, CAP, QD), BF16),
    ] + chain_scratch() + chain_scratch()
    vmem = pl.BlockSpec(memory_space=pltpu.VMEM)
    return pl.pallas_call(
        kernel,
        out_shape=[jax.ShapeDtypeStruct(residual.shape, BF16)] * 2,
        in_specs=[vmem] * 7,
        out_specs=[vmem] * 2,
        scratch_shapes=scratch,
        compiler_params=pltpu.CompilerParams(
            collective_id=0, has_side_effects=True, vmem_limit_bytes=62 * 1024 * 1024
        ),
        cost_estimate=pl.CostEstimate(flops=10**10, bytes_accessed=10**7, transcendentals=10**6),
    )(counts, onehot, residual, cotangent, router_weight[None, :], weight_in, weight_out)


def solution(mesh):
    spec = P("seq", "mp")
    return jax.shard_map(
        local,
        mesh=mesh,
        in_specs=(spec, P("seq"), P("seq"), P("mp"), P("mp", "seq"), spec, spec),
        out_specs=(spec, spec),
        check_vma=False,
    )
```

```python
import jax
import jax.numpy as jnp
from jax import lax
from jax.experimental import pallas as pl
from jax.experimental.pallas import tpu as pltpu
from jax.sharding import PartitionSpec as P

MESH = pl.DeviceIdType.MESH
D = 8192
HS = 128
NZ, NY, NX = 8, 4, 4
CAP = 16
QD = D // NX
FFD = 224
WIN = 3 * HS + 2 * FFD
WINP = 896
WOUT = HS + FFD
WOUTP = 384
PRW = WINP + WOUTP
ROWS = 1024
BLK = 256
HALF = QD // 2
F32 = jnp.float32
BF16 = jnp.bfloat16
FACTOR = HS ** (-0.5)


def mod(value, n):
    return lax.rem(value + n, n)


def dot_nn(a, b):
    return jnp.dot(a, b, preferred_element_type=F32)


def dot_nt(a, b):
    return lax.dot_general(a, b, (((1,), (1,)), ((), ())), preferred_element_type=F32)


def dot_tn(a, b):
    return lax.dot_general(a, b, (((0,), (0,)), ((), ())), preferred_element_type=F32)


class Net:
    def __init__(self, send_sem, recv_sem):
        self.send_sem, self.recv_sem = send_sem, recv_sem
        self.used = 0
        self.sent = []
        seq = lax.axis_index("seq")
        x = self.x = lax.axis_index("mp")
        z = self.z = lax.div(seq, NY * 2)
        y = self.y = lax.rem(lax.div(seq, 2), NY)
        c = self.c = lax.rem(seq, 2)
        self.o = 1 - c
        self.upper = lax.rem(y, 2)
        self.w = self.upper * 2 + c
        yw = y + 1 - 2 * self.upper
        yo = mod(y - 1 + 2 * self.upper, NY)
        self.twin = self.at(z, y, self.o, x)
        self.mate = self.at(z, yw, c, x)
        self.cross = self.at(z, yw, self.o, x)
        self.beyond = self.at(z, yo, c, x)
        self.along_x = [self.at(z, y, c, mod(x + d, NX)) for d in range(1, NX)]
        self.along_y = [self.at(z, mod(y + d, NY), c, x) for d in range(1, NY)]
        self.along_z = [self.at(mod(z + d, NZ), y, c, x) for d in range(1, NZ)]
        self.xp, self.xm = self.along_x[0], self.along_x[-1]
        self.yp, self.ym = self.along_y[0], self.along_y[-1]
        self.zp, self.zm = self.along_z[0], self.along_z[-1]

    def at(self, z, y, c, x):
        return ((z * NY + y) * 2 + c, x)

    def enter(self):
        barrier = pltpu.get_barrier_semaphore()
        partners = [self.twin, self.cross] + self.along_x + self.along_y + self.along_z
        for partner in partners:
            pl.semaphore_signal(barrier, inc=1, device_id=partner, device_id_type=MESH)
        pl.semaphore_wait(barrier, len(partners))

    def send(self, src, dst, device):
        copy = pltpu.make_async_remote_copy(
            src_ref=src,
            dst_ref=dst,
            send_sem=self.send_sem.at[self.used],
            recv_sem=self.recv_sem.at[self.used],
            device_id=device,
            device_id_type=MESH,
        )
        self.used += 1
        self.sent.append(copy)
        copy.start()
        return copy

    def same(self, ref, device):
        return self.send(ref, ref, device)

    def finish(self):
        for copy in self.sent:
            copy.wait_send()


def arrive(*copies):
    for copy in copies:
        copy.wait_recv()


class MpSum:
    def __init__(self, net, part, landed):
        self.net, self.part, self.landed = net, part, landed
        self.copies = [
            net.send(part.at[mod(net.x + d, NX)], landed.at[d - 1], net.along_x[d - 1]) for d in range(1, NX)
        ]

    def total(self):
        arrive(*self.copies)
        total = self.part[self.net.x].astype(F32)
        for d in range(NX - 1):
            total = total + self.landed[d].astype(F32)
        return total


class MpGather:
    def __init__(self, net, full, lanes):
        block = full.at[net.x, :, lanes]
        self.copies = [net.same(block, device) for device in net.along_x]

    def done(self):
        arrive(*self.copies)


class MpRing:
    def __init__(self, net, full, lanes):
        self.net, self.full, self.lanes = net, full, lanes
        block = full.at[net.x, :, lanes]
        self.copies = (net.same(block, net.xp), net.same(block, net.xm))

    def pass_on(self):
        net = self.net
        arrive(*self.copies)
        left = self.full.at[mod(net.x - 1, NX), 0 : BLK // 2, self.lanes]
        right = self.full.at[mod(net.x + 1, NX), BLK // 2 : BLK, self.lanes]
        self.copies = (net.same(left, net.xp), net.same(right, net.xm))

    def done(self):
        arrive(*self.copies)


def chain(net, pos, block, from_left, from_right, width):
    hops = NZ // 2
    half = width // 2
    far = mod(pos + hops, NZ)
    low = net.send(block(far, 0, half), from_left.at[0, ..., 0:half], net.zp)
    high = net.send(block(far, half, width), from_right.at[0, ..., half:width], net.zm)
    yield
    for step in range(1, hops):
        lo, hi = (0, half) if step == 1 else (0, width)
        target = block(mod(pos + hops - step, NZ), lo, hi)
        arrive(low)
        target[...] = (target[...].astype(F32) + from_left[step - 1, ..., lo:hi].astype(F32)).astype(BF16)
        low = net.send(block(mod(pos + hops - step, NZ), 0, width), from_left.at[step], net.zp)
        lo, hi = (half, width) if step == 1 else (0, width)
        target = block(mod(pos - hops + step, NZ), lo, hi)
        arrive(high)
        target[...] = (target[...].astype(F32) + from_right[step - 1, ..., lo:hi].astype(F32)).astype(BF16)
        high = net.send(block(mod(pos - hops + step, NZ), 0, width), from_right.at[step], net.zm)
        yield
    arrive(low, high)


class SeqSum:
    def __init__(self, net, bufs, out, product, order):
        self.net, self.bufs, self.out, self.product, self.order = net, bufs, out, product, order
        self.by_copies = []
        self.steps = [self.along_z_first(0), self.along_z_first(1)]

    def multiply(self):
        net, part, other = self.net, self.bufs[0], self.bufs[1]
        self.copies = []
        for k, pair in enumerate(self.order):
            rows = self.product(pair)
            for owner in range(NX):
                for place in range(2):
                    z = 2 * pair + place
                    y = lax.rem(owner - z + 2 * NZ, NY)
                    for core in range(2):
                        at = ((owner * 2 + place) * 2 + core) * CAP
                        part[core, z, y] = rows[at : at + CAP].astype(BF16)
            both = pl.ds(2 * pair, 2)
            self.copies.append(net.send(part.at[net.o, both], other.at[both], net.twin))
            if k:
                self.merge(k - 1)
        self.merge(len(self.order) - 1)
        self.steps.append(self.along_y_first())

    def merge(self, k):
        net, part, other, byl = self.net, self.bufs[0], self.bufs[1], self.bufs[7]
        arrive(self.copies[k])
        pair = self.order[k]
        for place in range(2):
            z = 2 * pair + place
            part[net.c, z] = (part[net.c, z].astype(F32) + other[z].astype(F32)).astype(BF16)
        if k == 0:
            for step in self.steps:
                next(step)
        both = pl.ds(2 * pair, 2)
        for d in range(1, NY):
            source = part.at[net.c, both, mod(net.y + d, NY), :, HALF:QD]
            self.by_copies.append(net.send(source, byl.at[d - 1, both], net.along_y[d - 1]))

    def turn(self):
        left = []
        for step in self.steps:
            try:
                next(step)
                left.append(step)
            except StopIteration:
                pass
        self.steps = left
        return bool(left)

    def along_z_first(self, which):
        net, part, qa, ayl = self.net, self.bufs[0], self.bufs[2], self.bufs[6]
        width = HALF // 2
        first = which * width
        left, right = self.bufs[4].at[which], self.bufs[5].at[which]
        block = lambda t, lo, hi: part.at[net.c, t, :, :, first + lo : first + hi]
        yield from chain(net, net.z, block, left, right, width)
        last = NZ // 2 - 1
        lanes = slice(first, first + width)
        qa[:, :, lanes] = (
            part[net.c, net.z, :, :, lanes].astype(F32) + left[last].astype(F32) + right[last].astype(F32)
        ).astype(BF16)
        copies = [
            net.send(qa.at[mod(net.y + d, NY), :, lanes], ayl.at[d - 1, :, lanes], net.along_y[d - 1])
            for d in range(1, NY)
        ]
        yield
        arrive(*copies)
        total = qa[net.y, :, lanes].astype(F32)
        for d in range(NY - 1):
            total = total + ayl[d, :, lanes].astype(F32)
        self.out[:, lanes] = total

    def along_y_first(self):
        net, part, qb, byl, bzl = self.net, self.bufs[0], self.bufs[3], self.bufs[7], self.bufs[8]
        arrive(*self.by_copies)
        total = part[net.c, :, net.y, :, HALF:QD].astype(F32)
        for d in range(NY - 1):
            total = total + byl[d].astype(F32)
        qb[...] = total.astype(BF16)
        copies = [net.send(qb.at[mod(net.z + d, NZ)], bzl.at[d - 1], net.along_z[d - 1]) for d in range(1, NZ)]
        yield
        arrive(*copies)
        total = qb[net.z].astype(F32)
        for d in range(NZ - 1):
            total = total + bzl[d].astype(F32)
        self.out[:, HALF:QD] = total


def row_sums(tile, columns):
    small = lax.broadcasted_iota(jnp.int32, tile, 1)
    result = jnp.zeros(tile, F32)
    for at, product in enumerate(columns):
        result = jnp.where(small == at, jnp.sum(product, axis=-1, keepdims=True), result)
    return result


def kernel(
    count_ref, pos_ref, res_ref, cot_ref, rw_ref, win_ref, wout_ref,
    fin_out, sel_out,
    send_sem, recv_sem, load_sem, winp, woutp, counts, contrib, from_twin, from_mate, g0, g1,
    pr, prl, proj, kv, joined, dproj, kg, kgl,
    delta, dnormed, stats, fin, *bufs,
):
    net = Net(send_sem, recv_sem)
    x, y, z, c = net.x, net.y, net.z, net.c
    loads = (
        pltpu.make_async_copy(win_ref, winp.at[0:WIN], load_sem.at[0]),
        pltpu.make_async_copy(wout_ref, woutp.at[0:WOUT], load_sem.at[1]),
    )
    for load in loads:
        load.start()
    net.enter()

    counts[0] = jnp.zeros((8, 128), jnp.int32) + count_ref[...]
    arrive(net.send(counts.at[0], counts.at[1], net.twin))
    n_slots = pos_ref.shape[1]
    mine, twins = counts[0, 0:1, 0:n_slots], counts[1, 0:1, 0:n_slots]
    before = twins * c + (4 * CAP - mine - twins) * net.upper
    row = lax.broadcasted_iota(jnp.int32, (4 * CAP, n_slots), 0)
    slot = lax.broadcasted_iota(jnp.int32, (4 * CAP, n_slots), 1)
    place_of = jnp.where(row - slot == before, F32(1.0), F32(0.0)).astype(BF16)
    token = lax.broadcasted_iota(jnp.int32, (128, n_slots), 0)
    slot = lax.broadcasted_iota(jnp.int32, (128, n_slots), 1)
    token_of = jnp.where((token == pos_ref[...]) & (slot < mine), F32(1.0), F32(0.0)).astype(BF16)
    sel = dot_nt(place_of, token_of).astype(BF16)
    sel_out[...] = sel

    copies = []
    for which, source in enumerate((res_ref, cot_ref)):
        rows = dot_nn(sel, source[...]).astype(BF16)
        for chip in range(2):
            for core in range(2):
                at = (chip * 2 + core) * CAP
                contrib[which, core, chip] = rows[at : at + CAP]
        copies.append(net.send(contrib.at[which, net.o], from_twin.at[which], net.twin))
    for which in range(2):
        arrive(copies[which])
        contrib[which, c] = (contrib[which, c].astype(F32) + from_twin[which].astype(F32)).astype(BF16)
        if which == 0:
            r_copy = net.send(contrib.at[0, c], from_mate.at[0:2], net.mate)
        else:
            d_copy = net.send(contrib.at[1, c, 1 - net.upper], from_mate.at[2], net.mate)
    mine_q = lax.div(y, 2)
    arrive(r_copy)
    for place in range(2):
        g0[z, 2 * mine_q + place, c] = (
            contrib[0, c, place].astype(F32) + from_mate[place].astype(F32)
        ).astype(BF16)

    def r_ring(step, q):
        near, far = mod(z - step + 1, NZ), mod(z + step - 1, NZ)
        ys = pl.ds(2 * q, 2)
        if step < 4:
            return (net.same(g0.at[near, ys, c], net.zp), net.same(g0.at[far, ys, c], net.zm))
        return (
            net.same(g0.at[near, ys, c, :, 0:HALF], net.zp),
            net.same(g0.at[far, ys, c, :, HALF:QD], net.zm),
        )

    def d_ring(step):
        near, far = mod(z - step + 1, NZ), mod(z + step - 1, NZ)
        if step < 4:
            return (net.same(g1.at[near, y, c], net.zp), net.same(g1.at[far, y, c], net.zm))
        return (
            net.same(g1.at[near, y, c, :, 0:HALF], net.zp),
            net.same(g1.at[far, y, c, :, HALF:QD], net.zm),
        )

    def d_sides(d):
        at = mod(z + d, NZ)
        return d, (net.same(g1.at[at, y, c], net.yp), net.same(g1.at[at, y, c], net.ym))

    def d_opposite(item):
        d, copies = item
        arrive(*copies)
        at = mod(z + d, NZ)
        return d, (
            net.same(g1.at[at, mod(y - 1, NY), c, :, 0:HALF], net.yp),
            net.same(g1.at[at, mod(y + 1, NY), c, :, HALF:QD], net.ym),
        )

    def d_twin(item):
        d, copies = item
        arrive(*copies)
        return net.same(g1.at[mod(z + d, NZ), :, c], net.twin)

    def r_twin(d):
        return net.same(g0.at[mod(z + d, NZ), :, c], net.twin)

    other_q = 1 - mine_q
    p_ring = r_ring(1, mine_q)
    r_copy = net.same(g0.at[z, pl.ds(2 * mine_q, 2), c], net.beyond)
    arrive(d_copy)
    g1[z, y, c] = (contrib[1, c, net.upper].astype(F32) + from_mate[2].astype(F32)).astype(BF16)
    g_ring = d_ring(1)
    d_0 = d_sides(0)
    rows = g0[z, y, c].astype(F32)
    stats[0, 3] = row_sums((CAP, 128), (rows * rows, rows * rw_ref[...]))
    first_stats = [net.send(stats.at[0, 3], stats.at[0, d], net.along_x[d]) for d in range(3)]
    winp[WIN:WINP] = jnp.zeros((WINP - WIN, QD), BF16)
    woutp[WOUT:WOUTP] = jnp.zeros((WOUTP - WOUT, QD), BF16)
    arrive(r_copy)
    q_ring = r_ring(1, other_q)
    r_0 = r_twin(0)
    arrive(*g_ring)
    g_ring = d_ring(2)
    d_1, d_7 = d_sides(1), d_sides(-1)
    d_0 = d_opposite(d_0)
    arrive(*p_ring)
    p_ring = r_ring(2, mine_q)
    arrive(*q_ring)
    q_ring = r_ring(2, other_q)
    r_1, r_7 = r_twin(1), r_twin(-1)
    arrive(*g_ring)
    g_ring = d_ring(3)
    d_2, d_6 = d_sides(2), d_sides(-2)
    d_0 = d_twin(d_0)
    d_1, d_7 = d_opposite(d_1), d_opposite(d_7)
    arrive(*p_ring)
    p_ring = r_ring(3, mine_q)
    arrive(*q_ring)
    q_ring = r_ring(3, other_q)
    r_2, r_6 = r_twin(2), r_twin(-2)
    d_1, d_7 = d_twin(d_1), d_twin(d_7)
    arrive(*g_ring)
    g_ring = d_ring(4)
    d_3, d_5 = d_sides(3), d_sides(-3)
    d_2, d_6 = d_opposite(d_2), d_opposite(d_6)

    lane = lax.broadcasted_iota(jnp.int32, (BLK, 128), 1)

    def stage(k, pair):
        both = pl.ds(2 * pair, 2)
        rows = g0[both].reshape(BLK, QD)
        result = dot_nt(rows, winp[...])
        rows_f = rows.astype(F32)
        tail = result[:, 768:896]
        at = WIN - 768
        for value in (
            jnp.sum(rows_f * rows_f, axis=-1, keepdims=True),
            jnp.sum(rows_f * rw_ref[...], axis=-1, keepdims=True),
        ):
            for _ in range(3):
                rounded = value.astype(BF16).astype(F32)
                tail = jnp.where(lane == at, rounded, tail)
                value = value - rounded
                at += 1
        result = result.astype(BF16)
        tail = tail.astype(BF16)
        back = dot_nt(g1[both].reshape(BLK, QD), woutp[...]).astype(BF16)
        for place in range(2):
            for row in range(NY):
                owner = lax.rem(2 * pair + place + row, NX)
                at = (place * NY + row) * 32
                pr[k, owner, place, :, 0:768] = result[at : at + 32, 0:768]
                pr[k, owner, place, :, 768:896] = tail[at : at + 32]
                pr[k, owner, place, :, WINP:PRW] = back[at : at + 32]
        return MpSum(net, pr.at[k], prl.at[k]), pair

    def stage_done(item):
        summed, pair = item
        proj[pl.ds(2 * pair, 2)] = summed.total()

    pair = lax.div(z, 2)
    turned = 2 * lax.rem(z, 2) - 1
    order = (pair, mod(pair + turned, 4), mod(pair - turned, 4), mod(pair + 2, 4))

    for load in loads:
        load.wait()
    arrive(r_0, r_1, r_7, d_0, d_1, d_7)
    s_0 = stage(0, order[0])
    arrive(*p_ring)
    p_ring = r_ring(4, mine_q)
    arrive(*q_ring)
    q_ring = r_ring(4, other_q)
    r_3, r_5 = r_twin(3), r_twin(-3)
    d_2, d_6 = d_twin(d_2), d_twin(d_6)
    arrive(*g_ring)
    d_4 = d_sides(4)
    d_3, d_5 = d_opposite(d_3), d_opposite(d_5)
    arrive(r_2, r_6, d_2, d_6)
    s_1 = stage(1, order[1])
    arrive(*p_ring)
    arrive(*q_ring)
    r_4 = r_twin(4)
    d_4 = d_opposite(d_4)
    d_3, d_5 = d_twin(d_3), d_twin(d_5)
    arrive(r_3, r_5, d_3, d_5)
    s_2 = stage(2, order[2])
    d_4 = d_twin(d_4)
    stage_done(s_0)
    arrive(r_4, d_4)
    s_3 = stage(3, order[3])
    stage_done(s_1)
    stage_done(s_2)
    stage_done(s_3)

    tail = proj[:, :, 768:896].reshape(BLK, 128)
    at = WIN - 768
    square = jnp.sum(jnp.where((lane >= at) & (lane < at + 3), tail, 0.0), axis=-1, keepdims=True)
    logit = jnp.sum(jnp.where((lane >= at + 3) & (lane < at + 6), tail, 0.0), axis=-1, keepdims=True)
    in_scale = lax.rsqrt(square / D + 1e-05)
    gate = jax.nn.sigmoid(logit)
    keyraw = proj[:, :, HS : 2 * HS].reshape(BLK, HS) * in_scale
    key_scale = lax.rsqrt(jnp.mean(keyraw * keyraw, axis=-1, keepdims=True) + 1e-06)
    kv[x, :, 0:HS] = (keyraw * key_scale).astype(BF16)
    kv[x, :, HS : 2 * HS] = (proj[:, :, 2 * HS : 3 * HS].reshape(BLK, HS) * in_scale).astype(BF16)
    kv_gather = MpGather(net, kv, slice(0, 2 * HS))

    gate_up = proj[:, :, 384:896].reshape(BLK, 512) * in_scale
    gate_in = gate_up[:, 0:FFD]
    up_in = gate_up[:, FFD : 2 * FFD]
    sigma = jax.nn.sigmoid(gate_in)
    joined[x, :, 256:384] = jnp.zeros((BLK, 128), BF16)
    joined[x, :, HS : HS + FFD] = (gate_in * sigma * up_in).astype(BF16)
    hid_ring = MpRing(net, joined, slice(HS, WOUTP))

    query = proj[:, :, 0:HS].reshape(BLK, HS) * in_scale
    query_scale = lax.rsqrt(jnp.mean(query * query, axis=-1, keepdims=True) + 1e-06)
    query_b = (query * query_scale).astype(BF16)
    dattended = (proj[:, :, WINP : WINP + HS].reshape(BLK, HS) * gate).astype(BF16)
    dhidden = proj[:, :, WINP + HS : PRW].reshape(BLK, 256)[:, 0:FFD] * gate
    dup = (dhidden * gate_in * sigma).astype(BF16)
    dgate_in = (dhidden * up_in * sigma * (1.0 + gate_in * (1.0 - sigma))).astype(BF16)
    dproj[x, :, 384:896] = jnp.concatenate([dgate_in, dup, jnp.zeros((BLK, 64), BF16)], axis=-1)

    row = lax.broadcasted_iota(jnp.int32, (BLK, 1), 0)
    row_z = row >> 5
    query_order = row_z * 128 + ((x + 8 - row_z) & 3) * 32 + (row & 31)
    col = lax.broadcasted_iota(jnp.int32, (1, ROWS), 1)
    col_z = (col >> 5) & 7
    key_order = col_z * 128 + (((col >> 8) + 8 - col_z) & 3) * 32 + (col & 31)
    visible = key_order <= query_order
    kv_gather.done()

    keys = kv[:, :, 0:HS].reshape(ROWS, HS)
    vals = kv[:, :, HS : 2 * HS].reshape(ROWS, HS)
    expo = jnp.where(visible, jnp.exp(dot_nt(query_b, keys) * FACTOR), 0.0)
    inverse = 1.0 / jnp.sum(expo, axis=-1, keepdims=True)
    joined[x, :, 0:HS] = (dot_nn(expo.astype(BF16), vals) * inverse).astype(BF16)
    att_gather = MpGather(net, joined, slice(0, HS))

    prob = expo * inverse
    dprob = dot_nt(dattended, vals)
    inner = jnp.sum(prob * dprob, axis=-1, keepdims=True)
    dscore = (prob * (dprob - inner)).astype(BF16)
    prob_b = prob.astype(BF16)
    dkey_part = (dot_tn(dscore, query_b) * FACTOR).astype(BF16)
    dvalue_part = dot_tn(prob_b, dattended).astype(BF16)
    for owner in range(NX):
        kg[owner, :, 0:HS] = dkey_part[owner * BLK : owner * BLK + BLK]
        kg[owner, :, HS : 2 * HS] = dvalue_part[owner * BLK : owner * BLK + BLK]
    kg_sum = MpSum(net, kg, kgl)
    hid_ring.pass_on()
    ff_ring = MpRing(net, dproj, slice(384, WINP))
    dquery_n = dot_nn(dscore, keys) * FACTOR

    def norm_back(values, scale, grads):
        return scale * grads - values * scale**3 * jnp.mean(grads * values, axis=-1, keepdims=True)

    dproj[x, :, 0:HS] = norm_back(query, query_scale, dquery_n).astype(BF16)
    att_gather.done()
    hid_ring.done()

    def rows_of(full, pair, columns):
        return full[:, pl.ds(pl.multiple_of(pair * 64, 64), 64)].reshape(BLK, columns)

    far_first = order[::-1]
    n_bufs = len(bufs) // 2
    delta_sum = SeqSum(
        net, bufs[:n_bufs], delta, lambda pair: dot_nn(rows_of(joined, pair, WOUTP), woutp[...]), far_first
    )
    dnormed_sum = SeqSum(
        net, bufs[n_bufs:], dnormed, lambda pair: dot_nn(rows_of(dproj, pair, WINP), winp[...]), far_first
    )
    delta_sum.multiply()
    key_grad = kg_sum.total()
    dproj[x, :, HS : 2 * HS] = norm_back(keyraw, key_scale, key_grad[:, 0:HS]).astype(BF16)
    dproj[x, :, 2 * HS : 3 * HS] = key_grad[:, HS : 2 * HS].astype(BF16)
    qkv_gather = MpGather(net, dproj, slice(0, 3 * HS))
    ff_ring.pass_on()
    delta_sum.turn()
    delta_sum.turn()
    ff_ring.done()
    qkv_gather.done()
    dnormed_sum.multiply()
    while delta_sum.turn():
        pass

    rows = g0[z, y, c].astype(F32)
    grads = g1[z, y, c].astype(F32)
    delta_b = delta[...].astype(BF16).astype(F32)
    small = lax.broadcasted_iota(jnp.int32, (CAP, 128), 1)

    def summed(which):
        return stats[which, 0] + stats[which, 1] + stats[which, 2] + stats[which, 3]

    def pick(tile, at):
        return jnp.sum(jnp.where(small == at, tile, 0.0), axis=-1, keepdims=True)

    def spread(which):
        own = fin.at[which, net.w]
        return [net.same(own, device) for device in (net.mate, net.cross, net.twin)]

    stats[1, 3] = row_sums((CAP, 128), (grads * delta_b,))
    arrive(*first_stats)
    tile = summed(0)
    in_scale = lax.rsqrt(pick(tile, 0) / D + 1e-05)
    gate = jax.nn.sigmoid(pick(tile, 1))
    fin[0, net.w] = (rows + gate * delta_b).astype(BF16)
    gate_stats = [net.send(stats.at[1, 3], stats.at[1, d], net.along_x[d]) for d in range(3)]
    copies = spread(0)
    while dnormed_sum.turn():
        pass
    dn = dnormed[...]
    stats[2, 3] = row_sums((CAP, 128), (dn * rows,))
    last_stats = [net.send(stats.at[2, 3], stats.at[2, d], net.along_x[d]) for d in range(3)]
    arrive(*gate_stats)
    dlogit = pick(summed(1), 0) * gate * (1.0 - gate)
    base = grads + dlogit * rw_ref[...]
    dn = in_scale * dn
    arrive(*copies)
    arrive(*last_stats)
    dinput = (dn - rows * in_scale**3 * (pick(summed(2), 0) / D)).astype(BF16).astype(F32)
    fin[1, net.w] = (base + dinput).astype(BF16)
    copies = spread(1)
    fin_out[0] = fin[0]
    arrive(*copies)
    fin_out[1] = fin[1]
    net.finish()


def place_kernel(sel_ref, fin_ref, res_ref, cot_ref, output_ref, grad_ref):
    sel = sel_ref[...]
    chosen = dot_tn(sel, jnp.ones((4 * CAP, 128), BF16))[:, 0:1] > 0.5
    for which, (source, target) in enumerate(((res_ref, output_ref), (cot_ref, grad_ref))):
        back = dot_tn(sel, fin_ref[which]).astype(BF16)
        target[...] = jnp.where(chosen, back, source[...])


def sum_scratch():
    return [
        pltpu.VMEM((2, NZ, NY, CAP, QD), BF16),
        pltpu.VMEM((NZ, NY, CAP, QD), BF16),
        pltpu.VMEM((NY, CAP, HALF), BF16),
        pltpu.VMEM((NZ, CAP, HALF), BF16),
        pltpu.VMEM((2, NZ // 2, NY, CAP, HALF // 2), BF16),
        pltpu.VMEM((2, NZ // 2, NY, CAP, HALF // 2), BF16),
        pltpu.VMEM((NY - 1, CAP, HALF), BF16),
        pltpu.VMEM((NY - 1, NZ, CAP, HALF), BF16),
        pltpu.VMEM((NZ - 1, CAP, HALF), BF16),
    ]


def local(residual, chosen_pos, chosen_count, router_weight, weight_in, weight_out, cotangent):
    n_sem = 320
    scratch = [
        pltpu.SemaphoreType.DMA((n_sem,)),
        pltpu.SemaphoreType.DMA((n_sem,)),
        pltpu.SemaphoreType.DMA((2,)),
        pltpu.VMEM((WINP, QD), BF16),
        pltpu.VMEM((WOUTP, QD), BF16),
        pltpu.VMEM((2, 8, 128), jnp.int32),
        pltpu.VMEM((2, 2, 2, CAP, QD), BF16),
        pltpu.VMEM((2, 2, CAP, QD), BF16),
        pltpu.VMEM((3, CAP, QD), BF16),
        pltpu.VMEM((NZ, NY, 2, CAP, QD), BF16),
        pltpu.VMEM((NZ, NY, 2, CAP, QD), BF16),
        pltpu.VMEM((4, NX, 2, 32, PRW), BF16),
        pltpu.VMEM((4, NX - 1, 2, 32, PRW), BF16),
        pltpu.VMEM((NZ, 32, PRW), F32),
        pltpu.VMEM((NX, BLK, 2 * HS), BF16),
        pltpu.VMEM((NX, BLK, WOUTP), BF16),
        pltpu.VMEM((NX, BLK, WINP), BF16),
        pltpu.VMEM((NX, BLK, 2 * HS), BF16),
        pltpu.VMEM((NX - 1, BLK, 2 * HS), BF16),
        pltpu.VMEM((CAP, QD), F32),
        pltpu.VMEM((CAP, QD), F32),
        pltpu.VMEM((3, 4, CAP, 128), F32),
        pltpu.VMEM((2, 4, CAP, QD), BF16),
    ] + sum_scratch() + sum_scratch()
    vmem = pl.BlockSpec(memory_space=pltpu.VMEM)
    anywhere = pl.BlockSpec(memory_space=pl.ANY)
    fin, sel = pl.pallas_call(
        kernel,
        out_shape=[
            jax.ShapeDtypeStruct((2, 4, CAP, QD), BF16),
            jax.ShapeDtypeStruct((4 * CAP, residual.shape[0]), BF16),
        ],
        in_specs=[vmem] * 5 + [anywhere] * 2,
        out_specs=[vmem] * 2,
        scratch_shapes=scratch,
        compiler_params=pltpu.CompilerParams(
            collective_id=0, has_side_effects=True, vmem_limit_bytes=62 * 1024 * 1024
        ),
        cost_estimate=pl.CostEstimate(flops=10**10, bytes_accessed=10**7, transcendentals=10**6),
    )(
        chosen_count[None, :], chosen_pos[None, :], residual, cotangent, router_weight[None, :],
        weight_in.T, weight_out,
    )
    fin = fin.reshape(2, 4 * CAP, QD)
    n_steps = 4
    tokens = residual.shape[0]
    columns = QD // n_steps
    block = pl.BlockSpec((tokens, columns), lambda i: (0, i))
    return pl.pallas_call(
        place_kernel,
        grid=(n_steps,),
        out_shape=[jax.ShapeDtypeStruct(residual.shape, BF16)] * 2,
        in_specs=[
            pl.BlockSpec((4 * CAP, tokens), lambda i: (0, 0)),
            pl.BlockSpec((2, 4 * CAP, columns), lambda i: (0, 0, i)),
            block,
            block,
        ],
        out_specs=[block, block],
    )(sel, fin, residual, cotangent)


def solution(mesh):
    spec = P("seq", "mp")
    return jax.shard_map(
        local,
        mesh=mesh,
        in_specs=(spec, P("seq"), P("seq"), P("mp"), P("mp", "seq"), spec, spec),
        out_specs=(spec, spec),
        check_vma=False,
    )
```

```python
import jax
import jax.numpy as jnp
from jax import lax
from jax.experimental import pallas as pl
from jax.experimental.pallas import tpu as pltpu
from jax.sharding import PartitionSpec as P

MESH = pl.DeviceIdType.MESH
D = 8192
HS = 128
NZ, NY, NX = 8, 4, 4
CAP = 16
QD = D // NX
FFD = 224
WIN = 3 * HS + 2 * FFD
WINP = 896
WOUT = HS + FFD
WOUTP = 384
ROWS = 1024
BLK = 256
HALF = QD // 2
Z_FIRST = ((0, 512), (512, 256))
AW = 768
F32 = jnp.float32
BF16 = jnp.bfloat16
FACTOR = HS ** (-0.5)


def mod(value, n):
    return lax.rem(value + n, n)


def dot_nn(a, b):
    return jnp.dot(a, b, preferred_element_type=F32)


def dot_nt(a, b):
    return lax.dot_general(a, b, (((1,), (1,)), ((), ())), preferred_element_type=F32)


def dot_tn(a, b):
    return lax.dot_general(a, b, (((0,), (0,)), ((), ())), preferred_element_type=F32)


class Net:
    def __init__(self, send_sem, recv_sem):
        self.send_sem, self.recv_sem = send_sem, recv_sem
        self.used = 0
        self.sent = []
        seq = lax.axis_index("seq")
        x = self.x = lax.axis_index("mp")
        z = self.z = lax.div(seq, NY * 2)
        y = self.y = lax.rem(lax.div(seq, 2), NY)
        c = self.c = lax.rem(seq, 2)
        self.o = 1 - c
        self.upper = lax.rem(y, 2)
        self.w = self.upper * 2 + c
        yw = y + 1 - 2 * self.upper
        yo = mod(y - 1 + 2 * self.upper, NY)
        self.twin = self.at(z, y, self.o, x)
        self.mate = self.at(z, yw, c, x)
        self.cross = self.at(z, yw, self.o, x)
        self.beyond = self.at(z, yo, c, x)
        self.along_x = [self.at(z, y, c, mod(x + d, NX)) for d in range(1, NX)]
        self.along_y = [self.at(z, mod(y + d, NY), c, x) for d in range(1, NY)]
        self.along_z = [self.at(mod(z + d, NZ), y, c, x) for d in range(1, NZ)]
        self.xp, self.xm = self.along_x[0], self.along_x[-1]
        self.yp, self.ym = self.along_y[0], self.along_y[-1]
        self.zp, self.zm = self.along_z[0], self.along_z[-1]

    def at(self, z, y, c, x):
        return ((z * NY + y) * 2 + c, x)

    def enter(self):
        barrier = pltpu.get_barrier_semaphore()
        partners = [self.twin, self.cross] + self.along_x + self.along_y + self.along_z
        for partner in partners:
            pl.semaphore_signal(barrier, inc=1, device_id=partner, device_id_type=MESH)
        pl.semaphore_wait(barrier, len(partners))

    def group(self, copies, whole):
        send_sem, recv_sem = self.send_sem.at[self.used], self.recv_sem.at[self.used]
        self.used += 1
        for src, dst, device in copies:
            pltpu.make_async_remote_copy(
                src_ref=src, dst_ref=dst, send_sem=send_sem, recv_sem=recv_sem, device_id=device, device_id_type=MESH
            ).start()
        self.sent.append(pltpu.make_async_copy(whole, whole, send_sem))
        return pltpu.make_async_copy(whole, whole, recv_sem)

    def send(self, src, dst, device):
        return self.group([(src, dst, device)], dst)

    def same(self, ref, device):
        return self.send(ref, ref, device)

    def finish(self):
        assert self.used == self.send_sem.shape[0], self.used
        for copy in self.sent:
            copy.wait()


def arrive(*copies):
    for copy in copies:
        copy.wait()


class MpSum:
    def __init__(self, net, part, landed):
        self.net, self.part, self.landed = net, part, landed
        self.copy = net.group(
            [(part.at[mod(net.x + d, NX)], landed.at[d - 1], net.along_x[d - 1]) for d in range(1, NX)], landed
        )

    def total(self):
        arrive(self.copy)
        total = self.part[self.net.x].astype(F32)
        for d in range(NX - 1):
            total = total + self.landed[d].astype(F32)
        return total


class MpGather:
    def __init__(self, net, full, lanes):
        block = full.at[net.x, :, lanes]
        self.copy = net.group([(block, block, device) for device in net.along_x], full.at[0 : NX - 1, :, lanes])

    def done(self):
        arrive(self.copy)


class MpRing:
    def __init__(self, net, full, lanes):
        self.net, self.full, self.lanes = net, full, lanes
        block = full.at[net.x, :, lanes]
        self.copy = net.group([(block, block, net.xp), (block, block, net.xm)], full.at[0:2, :, lanes])

    def pass_on(self):
        net = self.net
        arrive(self.copy)
        left = self.full.at[mod(net.x - 1, NX), 0 : BLK // 2, self.lanes]
        right = self.full.at[mod(net.x + 1, NX), BLK // 2 : BLK, self.lanes]
        self.copy = net.group([(left, left, net.xp), (right, right, net.xm)], self.full.at[0, :, self.lanes])

    def done(self):
        arrive(self.copy)


def chain(net, pos, block, from_left, from_right, width):
    hops = NZ // 2
    half = width // 2
    far = mod(pos + hops, NZ)
    copy = net.group(
        [
            (block(far, 0, half), from_left.at[0, ..., 0:half], net.zp),
            (block(far, half, width), from_right.at[0, ..., half:width], net.zm),
        ],
        from_left.at[0],
    )
    yield
    for step in range(1, hops):
        right, left = mod(pos + hops - step, NZ), mod(pos - hops + step, NZ)
        arrive(copy)
        for at, landed, (lo, hi) in ((right, from_left, (0, half)), (left, from_right, (half, width))):
            if step > 1:
                lo, hi = 0, width
            target = block(at, lo, hi)
            target[...] = (target[...].astype(F32) + landed[step - 1, ..., lo:hi].astype(F32)).astype(BF16)
        copy = net.group(
            [
                (block(right, 0, width), from_left.at[step], net.zp),
                (block(left, 0, width), from_right.at[step], net.zm),
            ],
            from_left.at[0:2],
        )
        yield
    arrive(copy)


class SeqSum:
    def __init__(self, net, bufs, out, product, order):
        self.net, self.bufs, self.out, self.product, self.order = net, bufs, out, product, order
        self.by_copies, self.by_all = [], []
        self.steps = [self.along_z_first(0), self.along_z_first(1)]

    def multiply(self, eager):
        net, part, other = self.net, self.bufs[0], self.bufs[1]
        self.copies = []
        for k, pair in enumerate(self.order):
            rows = self.product(pair)
            for owner in range(NX):
                for place in range(2):
                    z = 2 * pair + place
                    y = lax.rem(owner - z + 2 * NZ, NY)
                    for core in range(2):
                        at = ((owner * 2 + place) * 2 + core) * CAP
                        part[core, z, y] = rows[at : at + CAP].astype(BF16)
            both = pl.ds(2 * pair, 2)
            self.copies.append(net.send(part.at[net.o, both], other.at[both], net.twin))
            if k:
                self.merge(k - 1)
            if k == 3 and eager:
                self.turn()
        self.merge(len(self.order) - 1)
        self.steps.append(self.along_y_first())

    def merge(self, k):
        net, part, other, byl = self.net, self.bufs[0], self.bufs[1], self.bufs[9]
        arrive(self.copies[k])
        pair = self.order[k]
        for place in range(2):
            z = 2 * pair + place
            part[net.c, z] = (part[net.c, z].astype(F32) + other[z].astype(F32)).astype(BF16)
        if k == 0:
            for step in self.steps:
                next(step)
        both = pl.ds(2 * pair, 2)
        for d in range(1, NY):
            source = part.at[net.c, both, mod(net.y + d, NY), :, AW:QD]
            self.by_copies.append((source, byl.at[d - 1, both], net.along_y[d - 1]))
        self.by = net.group(self.by_copies, byl.at[:, 0:2])
        self.by_copies = []
        self.by_all.append(self.by)

    def turn(self):
        left = []
        for step in self.steps:
            try:
                next(step)
                left.append(step)
            except StopIteration:
                pass
        self.steps = left
        return bool(left)

    def along_z_first(self, which):
        net, part, qa, ayl = self.net, self.bufs[0], self.bufs[2], self.bufs[8]
        first, width = Z_FIRST[which]
        left, right = self.bufs[4 + 2 * which], self.bufs[5 + 2 * which]
        block = lambda t, lo, hi: part.at[net.c, t, :, :, first + lo : first + hi]
        yield from chain(net, net.z, block, left, right, width)
        last = NZ // 2 - 1
        lanes = slice(first, first + width)
        qa[:, :, lanes] = (
            part[net.c, net.z, :, :, lanes].astype(F32) + left[last].astype(F32) + right[last].astype(F32)
        ).astype(BF16)
        copy = net.group(
            [
                (qa.at[mod(net.y + d, NY), :, lanes], ayl.at[d - 1, :, lanes], net.along_y[d - 1])
                for d in range(1, NY)
            ],
            ayl.at[:, :, lanes],
        )
        yield
        arrive(copy)
        total = qa[net.y, :, lanes].astype(F32)
        for d in range(NY - 1):
            total = total + ayl[d, :, lanes].astype(F32)
        self.out[:, lanes] = total

    def along_y_first(self):
        net, part, qb, byl, bzl = self.net, self.bufs[0], self.bufs[3], self.bufs[9], self.bufs[10]
        arrive(*self.by_all)
        total = part[net.c, :, net.y, :, AW:QD].astype(F32)
        for d in range(NY - 1):
            total = total + byl[d].astype(F32)
        qb[...] = total.astype(BF16)
        copy = net.group(
            [(qb.at[mod(net.z + d, NZ)], bzl.at[d - 1], net.along_z[d - 1]) for d in range(1, NZ)], bzl
        )
        yield
        arrive(copy)
        total = qb[net.z].astype(F32)
        for d in range(NZ - 1):
            total = total + bzl[d].astype(F32)
        self.out[:, AW:QD] = total


def row_sums(tile, columns):
    small = lax.broadcasted_iota(jnp.int32, tile, 1)
    result = jnp.zeros(tile, F32)
    for at, product in enumerate(columns):
        result = jnp.where(small == at, jnp.sum(product, axis=-1, keepdims=True), result)
    return result


def kernel(
    count_ref, pos_ref, res_ref, cot_ref, rw_ref, win_ref, wout_ref,
    fin_out, sel_out,
    send_sem, recv_sem, load_sem, winp, woutp, counts, contrib, from_twin, from_mate, g0, g1,
    pr, prl, pd, pdl, proj, dj, kv, joined, dproj, kg, kgl,
    delta, dnormed, stats, fin, *bufs,
):
    net = Net(send_sem, recv_sem)
    x, y, z, c = net.x, net.y, net.z, net.c
    loads = (
        pltpu.make_async_copy(win_ref, winp.at[0:WIN], load_sem.at[0]),
        pltpu.make_async_copy(wout_ref, woutp.at[0:WOUT], load_sem.at[1]),
    )
    for load in loads:
        load.start()
    net.enter()

    counts[0] = jnp.zeros((8, 128), jnp.int32) + count_ref[...]
    arrive(net.send(counts.at[0], counts.at[1], net.twin))
    n_slots = pos_ref.shape[1]
    mine, twins = counts[0, 0:1, 0:n_slots], counts[1, 0:1, 0:n_slots]
    before = twins * c + (4 * CAP - mine - twins) * net.upper
    row = lax.broadcasted_iota(jnp.int32, (4 * CAP, n_slots), 0)
    slot = lax.broadcasted_iota(jnp.int32, (4 * CAP, n_slots), 1)
    place_of = jnp.where(row - slot == before, F32(1.0), F32(0.0)).astype(BF16)
    token = lax.broadcasted_iota(jnp.int32, (128, n_slots), 0)
    slot = lax.broadcasted_iota(jnp.int32, (128, n_slots), 1)
    token_of = jnp.where((token == pos_ref[...]) & (slot < mine), F32(1.0), F32(0.0)).astype(BF16)
    sel = dot_nt(place_of, token_of).astype(BF16)
    sel_out[...] = sel

    copies = []
    for which, source in enumerate((res_ref, cot_ref)):
        rows = dot_nn(sel, source[...]).astype(BF16)
        for chip in range(2):
            for core in range(2):
                at = (chip * 2 + core) * CAP
                contrib[which, core, chip] = rows[at : at + CAP]
        copies.append(net.send(contrib.at[which, net.o], from_twin.at[which], net.twin))
    for which in range(2):
        arrive(copies[which])
        contrib[which, c] = (contrib[which, c].astype(F32) + from_twin[which].astype(F32)).astype(BF16)
        if which == 0:
            r_copy = net.send(contrib.at[0, c], from_mate.at[0:2], net.mate)
        else:
            d_copy = net.send(contrib.at[1, c, 1 - net.upper], from_mate.at[2], net.mate)
    mine_q = lax.div(y, 2)
    arrive(r_copy)
    for place in range(2):
        g0[z, 2 * mine_q + place, c] = (
            contrib[0, c, place].astype(F32) + from_mate[place].astype(F32)
        ).astype(BF16)

    def both_ways(step, g, ys, few):
        near, far = mod(z - step + 1, NZ), mod(z + step - 1, NZ)
        if step < 4:
            right, left = g.at[near, ys, c], g.at[far, ys, c]
            whole = g.at[0:2, few, 0]
        else:
            right, left = g.at[near, ys, c, :, 0:HALF], g.at[far, ys, c, :, HALF:QD]
            whole = g.at[0, few, 0]
        return net.group([(right, right, net.zp), (left, left, net.zm)], whole)

    def r_ring(step, q):
        return both_ways(step, g0, pl.ds(2 * q, 2), slice(0, 2))

    def d_ring(step):
        return both_ways(step, g1, y, 0)

    def d_out(*ds):
        result = []
        for d in ds:
            block = g1.at[mod(z + d, NZ), y, c]
            result.append((d, net.group([(block, block, device) for device in net.along_y], g1.at[0, 0:3, 0])))
        return result

    def d_twin(items):
        result = []
        for d, copy in items:
            arrive(copy)
            result.append(net.same(g1.at[mod(z + d, NZ), :, c], net.twin))
        return result

    def r_twin(*ds):
        return [net.same(g0.at[mod(z + d, NZ), :, c], net.twin) for d in ds]

    lane = lax.broadcasted_iota(jnp.int32, (BLK, 128), 1)

    def rows_at(g, ds):
        rows = [g[mod(z + d, NZ)].reshape(BLK // 2, QD) for d in ds]
        return rows[0] if len(ds) == 1 else jnp.concatenate(rows, axis=0)

    def hand_out(part, ds, result, columns):
        for i, d in enumerate(ds):
            at = mod(z + d, NZ)
            for row in range(NY):
                owner = lax.rem(at + row, NX)
                part[at, owner, :, columns] = result[(i * NY + row) * 32 : (i * NY + row) * 32 + 32]

    def in_stage(*ds):
        rows = rows_at(g0, ds)
        result = dot_nt(rows, winp[...])
        rows_f = rows.astype(F32)
        tail = result[:, 768:896]
        at = WIN - 768
        for value in (
            jnp.sum(rows_f * rows_f, axis=-1, keepdims=True),
            jnp.sum(rows_f * rw_ref[...], axis=-1, keepdims=True),
        ):
            for _ in range(3):
                rounded = value.astype(BF16).astype(F32)
                tail = jnp.where(lane[0 : rows.shape[0]] == at, rounded, tail)
                value = value - rounded
                at += 1
        hand_out(pr, ds, result[:, 0:768].astype(BF16), slice(0, 768))
        hand_out(pr, ds, tail.astype(BF16), slice(768, WINP))
        return [(mod(z + d, NZ), MpSum(net, pr.at[mod(z + d, NZ)], prl.at[mod(z + d, NZ)])) for d in ds]

    def back_stage(*ds):
        hand_out(pd, ds, dot_nt(rows_at(g1, ds), woutp[...]).astype(BF16), slice(0, WOUTP))
        return [(mod(z + d, NZ), MpSum(net, pd.at[mod(z + d, NZ)], pdl.at[mod(z + d, NZ)])) for d in ds]

    def collect(target, items):
        for at, part in items:
            target[at] = part.total()

    other_q = 1 - mine_q
    p_ring = r_ring(1, mine_q)
    r_copy = net.same(g0.at[z, pl.ds(2 * mine_q, 2), c], net.beyond)
    arrive(d_copy)
    g1[z, y, c] = (contrib[1, c, net.upper].astype(F32) + from_mate[2].astype(F32)).astype(BF16)
    g_ring = d_ring(1)
    d_0 = d_out(0)
    rows = g0[z, y, c].astype(F32)
    stats[0, 3] = row_sums((CAP, 128), (rows * rows, rows * rw_ref[...]))

    def stats_out(which):
        return net.group(
            [(stats.at[which, 3], stats.at[which, d], net.along_x[d]) for d in range(3)], stats.at[which, 0:3]
        )

    first_stats = stats_out(0)
    winp[WIN:WINP] = jnp.zeros((WINP - WIN, QD), BF16)
    woutp[WOUT:WOUTP] = jnp.zeros((WOUTP - WOUT, QD), BF16)
    for load in loads:
        load.wait()
    arrive(r_copy)
    q_ring = r_ring(1, other_q)
    r_0 = r_twin(0)
    arrive(g_ring)
    g_ring = d_ring(2)
    d_1 = d_out(1, -1)
    arrive(p_ring)
    p_ring = r_ring(2, mine_q)
    arrive(*r_0)
    in_0 = in_stage(0)
    arrive(q_ring)
    q_ring = r_ring(2, other_q)
    r_1 = r_twin(1, -1)
    arrive(g_ring)
    g_ring = d_ring(3)
    d_2 = d_out(2, -2)
    d_0 = d_twin(d_0)
    arrive(p_ring)
    p_ring = r_ring(3, mine_q)
    arrive(*r_1)
    in_1 = in_stage(1, -1)
    arrive(q_ring)
    q_ring = r_ring(3, other_q)
    r_2 = r_twin(2, -2)
    d_1 = d_twin(d_1)
    arrive(g_ring)
    g_ring = d_ring(4)
    d_3 = d_out(3, -3)
    arrive(p_ring)
    p_ring = r_ring(4, mine_q)
    arrive(*r_2)
    in_2 = in_stage(2, -2)
    arrive(q_ring)
    q_ring = r_ring(4, other_q)
    r_3 = r_twin(3, -3)
    d_2 = d_twin(d_2)
    arrive(*d_0)
    back_0 = back_stage(0)
    arrive(g_ring)
    d_4 = d_out(4)
    arrive(*r_3)
    in_3 = in_stage(3, -3)
    arrive(p_ring, q_ring)
    r_4 = r_twin(4)
    collect(proj, in_0)
    collect(proj, in_1)
    arrive(*r_4)
    in_4 = in_stage(4)
    arrive(*d_1)
    back_1 = back_stage(1, -1)
    d_3 = d_twin(d_3)
    collect(proj, in_2)
    collect(proj, in_3)
    d_4 = d_twin(d_4)
    collect(proj, in_4)

    tail = proj[:, :, 768:896].reshape(BLK, 128)
    at = WIN - 768
    square = jnp.sum(jnp.where((lane >= at) & (lane < at + 3), tail, 0.0), axis=-1, keepdims=True)
    logit = jnp.sum(jnp.where((lane >= at + 3) & (lane < at + 6), tail, 0.0), axis=-1, keepdims=True)
    in_scale = lax.rsqrt(square / D + 1e-05)
    gate = jax.nn.sigmoid(logit)
    keyraw = proj[:, :, HS : 2 * HS].reshape(BLK, HS) * in_scale
    key_scale = lax.rsqrt(jnp.mean(keyraw * keyraw, axis=-1, keepdims=True) + 1e-06)
    kv[x, :, 0:HS] = (keyraw * key_scale).astype(BF16)
    kv[x, :, HS : 2 * HS] = (proj[:, :, 2 * HS : 3 * HS].reshape(BLK, HS) * in_scale).astype(BF16)
    kv_gather = MpGather(net, kv, slice(0, 2 * HS))

    gate_up = proj[:, :, 384:896].reshape(BLK, 512) * in_scale
    gate_in = gate_up[:, 0:FFD]
    up_in = gate_up[:, FFD : 2 * FFD]
    sigma = jax.nn.sigmoid(gate_in)
    joined[x, :, 256:384] = jnp.zeros((BLK, 128), BF16)
    joined[x, :, HS : HS + FFD] = (gate_in * sigma * up_in).astype(BF16)
    hid_ring = MpRing(net, joined, slice(HS, WOUTP))

    arrive(*d_2)
    back_2 = back_stage(2, -2)
    arrive(*d_3)
    back_3 = back_stage(3, -3)
    arrive(*d_4)
    back_4 = back_stage(4)
    query = proj[:, :, 0:HS].reshape(BLK, HS) * in_scale
    query_scale = lax.rsqrt(jnp.mean(query * query, axis=-1, keepdims=True) + 1e-06)
    query_b = (query * query_scale).astype(BF16)
    row = lax.broadcasted_iota(jnp.int32, (BLK, 1), 0)
    row_z = row >> 5
    query_order = row_z * 128 + ((x + 8 - row_z) & 3) * 32 + (row & 31)
    col = lax.broadcasted_iota(jnp.int32, (1, ROWS), 1)
    col_z = (col >> 5) & 7
    key_order = col_z * 128 + (((col >> 8) + 8 - col_z) & 3) * 32 + (col & 31)
    visible = key_order <= query_order
    kv_gather.done()

    keys = kv[:, :, 0:HS].reshape(ROWS, HS)
    vals = kv[:, :, HS : 2 * HS].reshape(ROWS, HS)
    expo = jnp.where(visible, jnp.exp(dot_nt(query_b, keys) * FACTOR), 0.0)
    inverse = 1.0 / jnp.sum(expo, axis=-1, keepdims=True)
    joined[x, :, 0:HS] = (dot_nn(expo.astype(BF16), vals) * inverse).astype(BF16)
    att_gather = MpGather(net, joined, slice(0, HS))

    for items in (back_0, back_1, back_2, back_3, back_4):
        collect(dj, items)
    dattended = (dj[:, :, 0:HS].reshape(BLK, HS) * gate).astype(BF16)
    dhidden = dj[:, :, HS:WOUTP].reshape(BLK, 256)[:, 0:FFD] * gate
    dup = (dhidden * gate_in * sigma).astype(BF16)
    dgate_in = (dhidden * up_in * sigma * (1.0 + gate_in * (1.0 - sigma))).astype(BF16)
    dproj[x, :, 384:896] = jnp.concatenate([dgate_in, dup, jnp.zeros((BLK, 64), BF16)], axis=-1)

    prob = expo * inverse
    dprob = dot_nt(dattended, vals)
    inner = jnp.sum(prob * dprob, axis=-1, keepdims=True)
    dscore = (prob * (dprob - inner)).astype(BF16)
    prob_b = prob.astype(BF16)
    dkey_part = (dot_tn(dscore, query_b) * FACTOR).astype(BF16)
    dvalue_part = dot_tn(prob_b, dattended).astype(BF16)
    for owner in range(NX):
        kg[owner, :, 0:HS] = dkey_part[owner * BLK : owner * BLK + BLK]
        kg[owner, :, HS : 2 * HS] = dvalue_part[owner * BLK : owner * BLK + BLK]
    kg_sum = MpSum(net, kg, kgl)
    hid_ring.pass_on()
    ff_ring = MpRing(net, dproj, slice(384, WINP))
    dquery_n = dot_nn(dscore, keys) * FACTOR

    def norm_back(values, scale, grads):
        return scale * grads - values * scale**3 * jnp.mean(grads * values, axis=-1, keepdims=True)

    dproj[x, :, 0:HS] = norm_back(query, query_scale, dquery_n).astype(BF16)
    key_grad = kg_sum.total()
    dproj[x, :, HS : 2 * HS] = norm_back(keyraw, key_scale, key_grad[:, 0:HS]).astype(BF16)
    dproj[x, :, 2 * HS : 3 * HS] = key_grad[:, HS : 2 * HS].astype(BF16)
    qkv_gather = MpGather(net, dproj, slice(0, 3 * HS))
    att_gather.done()
    hid_ring.done()

    def rows_of(full, pair, columns):
        return full[:, pl.ds(pl.multiple_of(pair * 64, 64), 64)].reshape(BLK, columns)

    pair = lax.div(z, 2)
    turned = 1 - 2 * lax.rem(z, 2)
    far_first = (mod(pair + 2, 4), mod(pair + turned, 4), mod(pair - turned, 4), pair)
    n_bufs = len(bufs) // 2
    delta_sum = SeqSum(
        net, bufs[:n_bufs], delta, lambda pair: dot_nn(rows_of(joined, pair, WOUTP), woutp[...]), far_first
    )
    dnormed_sum = SeqSum(
        net, bufs[n_bufs:], dnormed, lambda pair: dot_nn(rows_of(dproj, pair, WINP), winp[...]), far_first
    )
    ff_ring.pass_on()
    delta_sum.multiply(False)
    delta_sum.turn()
    ff_ring.done()
    qkv_gather.done()
    delta_sum.turn()
    dnormed_sum.multiply(True)
    while delta_sum.turn():
        dnormed_sum.turn()

    rows = g0[z, y, c].astype(F32)
    grads = g1[z, y, c].astype(F32)
    delta_b = delta[...].astype(BF16).astype(F32)
    small = lax.broadcasted_iota(jnp.int32, (CAP, 128), 1)

    def summed(which):
        return stats[which, 0] + stats[which, 1] + stats[which, 2] + stats[which, 3]

    def pick(tile, at):
        return jnp.sum(jnp.where(small == at, tile, 0.0), axis=-1, keepdims=True)

    def spread(which):
        own = fin.at[which, net.w]
        return net.group([(own, own, device) for device in (net.mate, net.cross, net.twin)], fin.at[which, 0:3])

    stats[1, 3] = row_sums((CAP, 128), (grads * delta_b,))
    arrive(first_stats)
    tile = summed(0)
    in_scale = lax.rsqrt(pick(tile, 0) / D + 1e-05)
    gate = jax.nn.sigmoid(pick(tile, 1))
    fin[0, net.w] = (rows + gate * delta_b).astype(BF16)
    gate_stats = stats_out(1)
    first_rows = spread(0)
    while dnormed_sum.turn():
        pass
    dn = dnormed[...]
    stats[2, 3] = row_sums((CAP, 128), (dn * rows,))
    last_stats = stats_out(2)
    arrive(gate_stats)
    dlogit = pick(summed(1), 0) * gate * (1.0 - gate)
    base = grads + dlogit * rw_ref[...]
    dn = in_scale * dn
    arrive(first_rows, last_stats)
    dinput = (dn - rows * in_scale**3 * (pick(summed(2), 0) / D)).astype(BF16).astype(F32)
    fin[1, net.w] = (base + dinput).astype(BF16)
    last_rows = spread(1)
    fin_out[0] = fin[0]
    arrive(last_rows)
    fin_out[1] = fin[1]
    net.finish()


def place_kernel(sel_ref, fin_ref, res_ref, cot_ref, output_ref, grad_ref):
    sel = sel_ref[...]
    chosen = dot_tn(sel, jnp.ones((4 * CAP, 128), BF16))[:, 0:1] > 0.5
    for which, (source, target) in enumerate(((res_ref, output_ref), (cot_ref, grad_ref))):
        back = dot_tn(sel, fin_ref[which]).astype(BF16)
        target[...] = jnp.where(chosen, back, source[...])


def sum_scratch():
    return [
        pltpu.VMEM((2, NZ, NY, CAP, QD), BF16),
        pltpu.VMEM((NZ, NY, CAP, QD), BF16),
        pltpu.VMEM((NY, CAP, AW), BF16),
        pltpu.VMEM((NZ, CAP, QD - AW), BF16),
        pltpu.VMEM((NZ // 2, NY, CAP, Z_FIRST[0][1]), BF16),
        pltpu.VMEM((NZ // 2, NY, CAP, Z_FIRST[0][1]), BF16),
        pltpu.VMEM((NZ // 2, NY, CAP, Z_FIRST[1][1]), BF16),
        pltpu.VMEM((NZ // 2, NY, CAP, Z_FIRST[1][1]), BF16),
        pltpu.VMEM((NY - 1, CAP, AW), BF16),
        pltpu.VMEM((NY - 1, NZ, CAP, QD - AW), BF16),
        pltpu.VMEM((NZ - 1, CAP, QD - AW), BF16),
    ]


def local(residual, chosen_pos, chosen_count, router_weight, weight_in, weight_out, cotangent):
    n_sem = 109
    scratch = [
        pltpu.SemaphoreType.DMA((n_sem,)),
        pltpu.SemaphoreType.DMA((n_sem,)),
        pltpu.SemaphoreType.DMA((2,)),
        pltpu.VMEM((WINP, QD), BF16),
        pltpu.VMEM((WOUTP, QD), BF16),
        pltpu.VMEM((2, 8, 128), jnp.int32),
        pltpu.VMEM((2, 2, 2, CAP, QD), BF16),
        pltpu.VMEM((2, 2, CAP, QD), BF16),
        pltpu.VMEM((3, CAP, QD), BF16),
        pltpu.VMEM((NZ, NY, 2, CAP, QD), BF16),
        pltpu.VMEM((NZ, NY, 2, CAP, QD), BF16),
        pltpu.VMEM((NZ, NX, 32, WINP), BF16),
        pltpu.VMEM((NZ, NX - 1, 32, WINP), BF16),
        pltpu.VMEM((NZ, NX, 32, WOUTP), BF16),
        pltpu.VMEM((NZ, NX - 1, 32, WOUTP), BF16),
        pltpu.VMEM((NZ, 32, WINP), F32),
        pltpu.VMEM((NZ, 32, WOUTP), F32),
        pltpu.VMEM((NX, BLK, 2 * HS), BF16),
        pltpu.VMEM((NX, BLK, WOUTP), BF16),
        pltpu.VMEM((NX, BLK, WINP), BF16),
        pltpu.VMEM((NX, BLK, 2 * HS), BF16),
        pltpu.VMEM((NX - 1, BLK, 2 * HS), BF16),
        pltpu.VMEM((CAP, QD), F32),
        pltpu.VMEM((CAP, QD), F32),
        pltpu.VMEM((3, 4, CAP, 128), F32),
        pltpu.VMEM((2, 4, CAP, QD), BF16),
    ] + sum_scratch() + sum_scratch()
    vmem = pl.BlockSpec(memory_space=pltpu.VMEM)
    anywhere = pl.BlockSpec(memory_space=pl.ANY)
    fin, sel = pl.pallas_call(
        kernel,
        out_shape=[
            jax.ShapeDtypeStruct((2, 4, CAP, QD), BF16),
            jax.ShapeDtypeStruct((4 * CAP, residual.shape[0]), BF16),
        ],
        in_specs=[vmem] * 5 + [anywhere] * 2,
        out_specs=[vmem] * 2,
        scratch_shapes=scratch,
        compiler_params=pltpu.CompilerParams(
            collective_id=0, has_side_effects=True, vmem_limit_bytes=62 * 1024 * 1024
        ),
        cost_estimate=pl.CostEstimate(flops=10**10, bytes_accessed=10**7, transcendentals=10**6),
    )(
        chosen_count[None, :], chosen_pos[None, :], residual, cotangent, router_weight[None, :],
        weight_in.T, weight_out,
    )
    fin = fin.reshape(2, 4 * CAP, QD)
    n_steps = 1
    tokens = residual.shape[0]
    columns = QD // n_steps
    block = pl.BlockSpec((tokens, columns), lambda i: (0, i))
    return pl.pallas_call(
        place_kernel,
        grid=(n_steps,),
        out_shape=[jax.ShapeDtypeStruct(residual.shape, BF16)] * 2,
        in_specs=[
            pl.BlockSpec((4 * CAP, tokens), lambda i: (0, 0)),
            pl.BlockSpec((2, 4 * CAP, columns), lambda i: (0, 0, i)),
            block,
            block,
        ],
        out_specs=[block, block],
    )(sel, fin, residual, cotangent)


def solution(mesh):
    spec = P("seq", "mp")
    return jax.shard_map(
        local,
        mesh=mesh,
        in_specs=(spec, P("seq"), P("seq"), P("mp"), P("mp", "seq"), spec, spec),
        out_specs=(spec, spec),
        check_vma=False,
    )
```

```python
import jax
import jax.numpy as jnp
from jax import lax
from jax.experimental import pallas as pl
from jax.experimental.pallas import tpu as pltpu
from jax.sharding import PartitionSpec as P

MESH = pl.DeviceIdType.MESH
D = 8192
HS = 128
NZ, NY, NX = 8, 4, 4
CAP = 16
QD = D // NX
FFD = 224
WIN = 3 * HS + 2 * FFD
WINP = 896
WOUT = HS + FFD
WOUTP = 384
ROWS = 1024
BLK = 256
HALF = QD // 2
Z_FIRST = ((0, 512), (512, 256))
AW = 768
F32 = jnp.float32
BF16 = jnp.bfloat16
FACTOR = HS ** (-0.5)


def mod(value, n):
    return lax.rem(value + n, n)


def dot_nn(a, b):
    return jnp.dot(a, b, preferred_element_type=F32)


def dot_nt(a, b):
    return lax.dot_general(a, b, (((1,), (1,)), ((), ())), preferred_element_type=F32)


def dot_tn(a, b):
    return lax.dot_general(a, b, (((0,), (0,)), ((), ())), preferred_element_type=F32)


class Net:
    def __init__(self, send_sem, recv_sem):
        self.send_sem, self.recv_sem = send_sem, recv_sem
        self.used = 0
        self.sent = []
        seq = lax.axis_index("seq")
        x = self.x = lax.axis_index("mp")
        z = self.z = lax.div(seq, NY * 2)
        y = self.y = lax.rem(lax.div(seq, 2), NY)
        c = self.c = lax.rem(seq, 2)
        self.o = 1 - c
        self.upper = lax.rem(y, 2)
        self.w = self.upper * 2 + c
        yw = y + 1 - 2 * self.upper
        yo = mod(y - 1 + 2 * self.upper, NY)
        self.twin = self.at(z, y, self.o, x)
        self.mate = self.at(z, yw, c, x)
        self.cross = self.at(z, yw, self.o, x)
        self.beyond = self.at(z, yo, c, x)
        self.along_x = [self.at(z, y, c, mod(x + d, NX)) for d in range(1, NX)]
        self.along_y = [self.at(z, mod(y + d, NY), c, x) for d in range(1, NY)]
        self.along_z = [self.at(mod(z + d, NZ), y, c, x) for d in range(1, NZ)]
        self.xp, self.xm = self.along_x[0], self.along_x[-1]
        self.yp, self.ym = self.along_y[0], self.along_y[-1]
        self.zp, self.zm = self.along_z[0], self.along_z[-1]

    def at(self, z, y, c, x):
        return ((z * NY + y) * 2 + c, x)

    def enter(self):
        barrier = pltpu.get_barrier_semaphore()
        partners = [self.twin, self.cross] + self.along_x + self.along_y + self.along_z
        for partner in partners:
            pl.semaphore_signal(barrier, inc=1, device_id=partner, device_id_type=MESH)
        pl.semaphore_wait(barrier, len(partners))

    def group(self, copies, whole):
        send_sem, recv_sem = self.send_sem.at[self.used], self.recv_sem.at[self.used]
        self.used += 1
        for src, dst, device in copies:
            pltpu.make_async_remote_copy(
                src_ref=src, dst_ref=dst, send_sem=send_sem, recv_sem=recv_sem, device_id=device, device_id_type=MESH
            ).start()
        self.sent.append(pltpu.make_async_copy(whole, whole, send_sem))
        return pltpu.make_async_copy(whole, whole, recv_sem)

    def send(self, src, dst, device):
        return self.group([(src, dst, device)], dst)

    def same(self, ref, device):
        return self.send(ref, ref, device)

    def finish(self):
        assert self.used == self.send_sem.shape[0], self.used
        for copy in self.sent:
            copy.wait()


def arrive(*copies):
    for copy in copies:
        copy.wait()


class MpSum:
    def __init__(self, net, part, landed):
        self.net, self.part, self.landed = net, part, landed
        self.copy = net.group(
            [(part.at[mod(net.x + d, NX)], landed.at[d - 1], net.along_x[d - 1]) for d in range(1, NX)], landed
        )

    def total(self):
        arrive(self.copy)
        total = self.part[self.net.x].astype(F32)
        for d in range(NX - 1):
            total = total + self.landed[d].astype(F32)
        return total


def rows_of_owner(full, owner, lanes, first=0, last=NZ):
    return [full.at[at, lax.rem(owner - at + NZ, NX), :, lanes] for at in range(first, last)]


def give(net, full, lanes, rows):
    for at in range(NZ):
        full[at, lax.rem(net.x - at + NZ, NX), :, lanes] = rows[at * 32 : at * 32 + 32]


class MpGather:
    def __init__(self, net, full, lanes):
        blocks = rows_of_owner(full, net.x, lanes)
        self.copy = net.group(
            [(block, block, device) for device in net.along_x for block in blocks],
            full.at[0 : NZ // NX * (NX - 1), :, :, lanes],
        )

    def done(self):
        arrive(self.copy)


class MpRing:
    def __init__(self, net, full, lanes):
        self.net, self.full, self.lanes = net, full, lanes
        blocks = rows_of_owner(full, net.x, lanes)
        self.copy = net.group(
            [(block, block, device) for device in (net.xp, net.xm) for block in blocks],
            full.at[0 : NZ // 2, :, :, lanes],
        )

    def pass_on(self):
        net = self.net
        arrive(self.copy)
        left = rows_of_owner(self.full, mod(net.x - 1, NX), self.lanes, 0, NZ // 2)
        right = rows_of_owner(self.full, mod(net.x + 1, NX), self.lanes, NZ // 2, NZ)
        self.copy = net.group(
            [(block, block, net.xp) for block in left] + [(block, block, net.xm) for block in right],
            self.full.at[0 : NZ // NX, :, :, self.lanes],
        )

    def done(self):
        arrive(self.copy)


def chain(net, pos, block, from_left, from_right, width):
    hops = NZ // 2
    half = width // 2
    far = mod(pos + hops, NZ)
    copy = net.group(
        [
            (block(far, 0, half), from_left.at[0, ..., 0:half], net.zp),
            (block(far, half, width), from_right.at[0, ..., half:width], net.zm),
        ],
        from_left.at[0],
    )
    yield
    for step in range(1, hops):
        right, left = mod(pos + hops - step, NZ), mod(pos - hops + step, NZ)
        arrive(copy)
        for at, landed, (lo, hi) in ((right, from_left, (0, half)), (left, from_right, (half, width))):
            if step > 1:
                lo, hi = 0, width
            target = block(at, lo, hi)
            target[...] = (target[...].astype(F32) + landed[step - 1, ..., lo:hi].astype(F32)).astype(BF16)
        copy = net.group(
            [
                (block(right, 0, width), from_left.at[step], net.zp),
                (block(left, 0, width), from_right.at[step], net.zm),
            ],
            from_left.at[0:2],
        )
        yield
    arrive(copy)


class SeqSum:
    def __init__(self, net, bufs, out, product, order):
        self.net, self.bufs, self.out, self.product, self.order = net, bufs, out, product, order
        self.by_copies, self.by_all = [], []
        self.steps = [self.along_z_first(0), self.along_z_first(1)]

    def multiply(self, eager):
        net, part, other = self.net, self.bufs[0], self.bufs[1]
        self.copies = []
        for k, pair in enumerate(self.order):
            rows = self.product(pair)
            for place in range(2):
                for y in range(NY):
                    for core in range(2):
                        at = ((place * NY + y) * 2 + core) * CAP
                        part[core, 2 * pair + place, y] = rows[at : at + CAP].astype(BF16)
            both = pl.ds(2 * pair, 2)
            self.copies.append(net.send(part.at[net.o, both], other.at[both], net.twin))
            if k:
                self.merge(k - 1)
            if k == 3 and eager:
                self.turn()
        self.merge(len(self.order) - 1)
        self.steps.append(self.along_y_first())

    def merge(self, k):
        net, part, other, byl = self.net, self.bufs[0], self.bufs[1], self.bufs[9]
        arrive(self.copies[k])
        pair = self.order[k]
        for place in range(2):
            z = 2 * pair + place
            part[net.c, z] = (part[net.c, z].astype(F32) + other[z].astype(F32)).astype(BF16)
        if k == 0:
            for step in self.steps:
                next(step)
        both = pl.ds(2 * pair, 2)
        for d in range(1, NY):
            source = part.at[net.c, both, mod(net.y + d, NY), :, AW:QD]
            self.by_copies.append((source, byl.at[d - 1, both], net.along_y[d - 1]))
        self.by = net.group(self.by_copies, byl.at[:, 0:2])
        self.by_copies = []
        self.by_all.append(self.by)

    def turn(self):
        left = []
        for step in self.steps:
            try:
                next(step)
                left.append(step)
            except StopIteration:
                pass
        self.steps = left
        return bool(left)

    def along_z_first(self, which):
        net, part, qa, ayl = self.net, self.bufs[0], self.bufs[2], self.bufs[8]
        first, width = Z_FIRST[which]
        left, right = self.bufs[4 + 2 * which], self.bufs[5 + 2 * which]
        block = lambda t, lo, hi: part.at[net.c, t, :, :, first + lo : first + hi]
        yield from chain(net, net.z, block, left, right, width)
        last = NZ // 2 - 1
        lanes = slice(first, first + width)
        qa[:, :, lanes] = (
            part[net.c, net.z, :, :, lanes].astype(F32) + left[last].astype(F32) + right[last].astype(F32)
        ).astype(BF16)
        copy = net.group(
            [
                (qa.at[mod(net.y + d, NY), :, lanes], ayl.at[d - 1, :, lanes], net.along_y[d - 1])
                for d in range(1, NY)
            ],
            ayl.at[:, :, lanes],
        )
        yield
        arrive(copy)
        total = qa[net.y, :, lanes].astype(F32)
        for d in range(NY - 1):
            total = total + ayl[d, :, lanes].astype(F32)
        self.out[:, lanes] = total

    def along_y_first(self):
        net, part, qb, byl, bzl = self.net, self.bufs[0], self.bufs[3], self.bufs[9], self.bufs[10]
        arrive(*self.by_all)
        total = part[net.c, :, net.y, :, AW:QD].astype(F32)
        for d in range(NY - 1):
            total = total + byl[d].astype(F32)
        qb[...] = total.astype(BF16)
        copy = net.group(
            [(qb.at[mod(net.z + d, NZ)], bzl.at[d - 1], net.along_z[d - 1]) for d in range(1, NZ)], bzl
        )
        yield
        arrive(copy)
        total = qb[net.z].astype(F32)
        for d in range(NZ - 1):
            total = total + bzl[d].astype(F32)
        self.out[:, AW:QD] = total


def row_sums(tile, columns):
    small = lax.broadcasted_iota(jnp.int32, tile, 1)
    result = jnp.zeros(tile, F32)
    for at, product in enumerate(columns):
        result = jnp.where(small == at, jnp.sum(product, axis=-1, keepdims=True), result)
    return result


def kernel(
    count_ref, pos_ref, res_ref, cot_ref, rw_ref, win_ref, wout_ref,
    fin_out, sel_out,
    send_sem, recv_sem, load_sem, winp, woutp, counts, contrib, from_twin, from_mate, g0, g1,
    pr, prl, pd, pdl, proj, dj, qkv, joined, datt, dproj, qn, kn, dkey_n, dvalues,
    delta, dnormed, stats, fin, *bufs,
):
    net = Net(send_sem, recv_sem)
    x, y, z, c = net.x, net.y, net.z, net.c
    loads = (
        pltpu.make_async_copy(win_ref, winp.at[0:WIN], load_sem.at[0]),
        pltpu.make_async_copy(wout_ref, woutp.at[0:WOUT], load_sem.at[1]),
    )
    for load in loads:
        load.start()
    net.enter()

    counts[0] = jnp.zeros((8, 128), jnp.int32) + count_ref[...]
    arrive(net.send(counts.at[0], counts.at[1], net.twin))
    n_slots = pos_ref.shape[1]
    mine, twins = counts[0, 0:1, 0:n_slots], counts[1, 0:1, 0:n_slots]
    before = twins * c + (4 * CAP - mine - twins) * net.upper
    row = lax.broadcasted_iota(jnp.int32, (4 * CAP, n_slots), 0)
    slot = lax.broadcasted_iota(jnp.int32, (4 * CAP, n_slots), 1)
    place_of = jnp.where(row - slot == before, F32(1.0), F32(0.0)).astype(BF16)
    token = lax.broadcasted_iota(jnp.int32, (128, n_slots), 0)
    slot = lax.broadcasted_iota(jnp.int32, (128, n_slots), 1)
    token_of = jnp.where((token == pos_ref[...]) & (slot < mine), F32(1.0), F32(0.0)).astype(BF16)
    sel = dot_nt(place_of, token_of).astype(BF16)
    sel_out[...] = sel

    copies = []
    for which, source in enumerate((res_ref, cot_ref)):
        rows = dot_nn(sel, source[...]).astype(BF16)
        for chip in range(2):
            for core in range(2):
                at = (chip * 2 + core) * CAP
                contrib[which, core, chip] = rows[at : at + CAP]
        copies.append(net.send(contrib.at[which, net.o], from_twin.at[which], net.twin))
    for which in range(2):
        arrive(copies[which])
        contrib[which, c] = (contrib[which, c].astype(F32) + from_twin[which].astype(F32)).astype(BF16)
        if which == 0:
            r_copy = net.send(contrib.at[0, c], from_mate.at[0:2], net.mate)
        else:
            d_copy = net.send(contrib.at[1, c, 1 - net.upper], from_mate.at[2], net.mate)
    mine_q = lax.div(y, 2)
    arrive(r_copy)
    for place in range(2):
        g0[z, 2 * mine_q + place, c] = (
            contrib[0, c, place].astype(F32) + from_mate[place].astype(F32)
        ).astype(BF16)

    def both_ways(step, g, ys, few):
        near, far = mod(z - step + 1, NZ), mod(z + step - 1, NZ)
        if step < 4:
            right, left = g.at[near, ys, c], g.at[far, ys, c]
            whole = g.at[0:2, few, 0]
        else:
            right, left = g.at[near, ys, c, :, 0:HALF], g.at[far, ys, c, :, HALF:QD]
            whole = g.at[0, few, 0]
        return net.group([(right, right, net.zp), (left, left, net.zm)], whole)

    def r_ring(step, q):
        return both_ways(step, g0, pl.ds(2 * q, 2), slice(0, 2))

    def d_ring(step):
        return both_ways(step, g1, y, 0)

    def d_out(*ds):
        result = []
        for d in ds:
            block = g1.at[mod(z + d, NZ), y, c]
            result.append((d, net.group([(block, block, device) for device in net.along_y], g1.at[0, 0:3, 0])))
        return result

    def d_twin(items):
        result = []
        for d, copy in items:
            arrive(copy)
            result.append(net.same(g1.at[mod(z + d, NZ), :, c], net.twin))
        return result

    def r_twin(*ds):
        return [net.same(g0.at[mod(z + d, NZ), :, c], net.twin) for d in ds]

    lane = lax.broadcasted_iota(jnp.int32, (BLK, 128), 1)

    def rows_at(g, ds):
        rows = [g[mod(z + d, NZ)].reshape(BLK // 2, QD) for d in ds]
        return rows[0] if len(ds) == 1 else jnp.concatenate(rows, axis=0)

    def hand_out(part, ds, result, columns):
        for i, d in enumerate(ds):
            at = mod(z + d, NZ)
            for row in range(NY):
                owner = lax.rem(at + row, NX)
                part[at, owner, :, columns] = result[(i * NY + row) * 32 : (i * NY + row) * 32 + 32]

    def in_stage(*ds):
        rows = rows_at(g0, ds)
        result = dot_nt(rows, winp[...])
        rows_f = rows.astype(F32)
        tail = result[:, 768:896]
        at = WIN - 768
        for value in (
            jnp.sum(rows_f * rows_f, axis=-1, keepdims=True),
            jnp.sum(rows_f * rw_ref[...], axis=-1, keepdims=True),
        ):
            for _ in range(3):
                rounded = value.astype(BF16).astype(F32)
                tail = jnp.where(lane[0 : rows.shape[0]] == at, rounded, tail)
                value = value - rounded
                at += 1
        hand_out(pr, ds, result[:, 0:768].astype(BF16), slice(0, 768))
        hand_out(pr, ds, tail.astype(BF16), slice(768, WINP))
        return [(mod(z + d, NZ), MpSum(net, pr.at[mod(z + d, NZ)], prl.at[mod(z + d, NZ)])) for d in ds]

    def back_stage(*ds):
        hand_out(pd, ds, dot_nt(rows_at(g1, ds), woutp[...]).astype(BF16), slice(0, WOUTP))
        return [(mod(z + d, NZ), MpSum(net, pd.at[mod(z + d, NZ)], pdl.at[mod(z + d, NZ)])) for d in ds]

    def collect(target, items):
        for at, part in items:
            target[at] = part.total()

    other_q = 1 - mine_q
    p_ring = r_ring(1, mine_q)
    r_copy = net.same(g0.at[z, pl.ds(2 * mine_q, 2), c], net.beyond)
    arrive(d_copy)
    g1[z, y, c] = (contrib[1, c, net.upper].astype(F32) + from_mate[2].astype(F32)).astype(BF16)
    g_ring = d_ring(1)
    d_0 = d_out(0)
    rows = g0[z, y, c].astype(F32)
    stats[0, 3] = row_sums((CAP, 128), (rows * rows, rows * rw_ref[...]))

    def stats_out(which):
        return net.group(
            [(stats.at[which, 3], stats.at[which, d], net.along_x[d]) for d in range(3)], stats.at[which, 0:3]
        )

    first_stats = stats_out(0)
    winp[WIN:WINP] = jnp.zeros((WINP - WIN, QD), BF16)
    woutp[WOUT:WOUTP] = jnp.zeros((WOUTP - WOUT, QD), BF16)
    for load in loads:
        load.wait()
    arrive(r_copy)
    q_ring = r_ring(1, other_q)
    r_0 = r_twin(0)
    arrive(g_ring)
    g_ring = d_ring(2)
    d_1 = d_out(1, -1)
    arrive(p_ring)
    p_ring = r_ring(2, mine_q)
    arrive(*r_0)
    in_0 = in_stage(0)
    arrive(q_ring)
    q_ring = r_ring(2, other_q)
    r_1 = r_twin(1, -1)
    arrive(g_ring)
    g_ring = d_ring(3)
    d_2 = d_out(2, -2)
    d_0 = d_twin(d_0)
    arrive(p_ring)
    p_ring = r_ring(3, mine_q)
    arrive(*r_1)
    in_1 = in_stage(1, -1)
    arrive(q_ring)
    q_ring = r_ring(3, other_q)
    r_2 = r_twin(2, -2)
    d_1 = d_twin(d_1)
    arrive(g_ring)
    g_ring = d_ring(4)
    d_3 = d_out(3, -3)
    arrive(p_ring)
    p_ring = r_ring(4, mine_q)
    arrive(*r_2)
    in_2 = in_stage(2, -2)
    arrive(q_ring)
    q_ring = r_ring(4, other_q)
    r_3 = r_twin(3, -3)
    d_2 = d_twin(d_2)
    arrive(*d_0)
    back_0 = back_stage(0)
    arrive(g_ring)
    d_4 = d_out(4)
    arrive(*r_3)
    in_3 = in_stage(3, -3)
    arrive(p_ring, q_ring)
    r_4 = r_twin(4)
    collect(proj, in_0)
    collect(proj, in_1)
    arrive(*r_4)
    in_4 = in_stage(4)
    arrive(*d_1)
    back_1 = back_stage(1, -1)
    d_3 = d_twin(d_3)
    collect(proj, in_2)
    collect(proj, in_3)
    d_4 = d_twin(d_4)
    collect(proj, in_4)

    tail = proj[:, :, 768:896].reshape(BLK, 128)
    at = WIN - 768
    square = jnp.sum(jnp.where((lane >= at) & (lane < at + 3), tail, 0.0), axis=-1, keepdims=True)
    logit = jnp.sum(jnp.where((lane >= at + 3) & (lane < at + 6), tail, 0.0), axis=-1, keepdims=True)
    in_scale = lax.rsqrt(square / D + 1e-05)
    gate = jax.nn.sigmoid(logit)
    give(net, qkv, slice(0, 3 * HS), (proj[:, :, 0 : 3 * HS].reshape(BLK, 3 * HS) * in_scale).astype(BF16))
    qkv_gather = MpGather(net, qkv, slice(0, 3 * HS))

    gate_up = proj[:, :, 384:896].reshape(BLK, 512) * in_scale
    gate_in = gate_up[:, 0:FFD]
    up_in = gate_up[:, FFD : 2 * FFD]
    sigma = jax.nn.sigmoid(gate_in)
    hidden = (gate_in * sigma * up_in).astype(BF16)
    give(net, joined, slice(HS, WOUTP), jnp.concatenate([hidden, jnp.zeros((BLK, 32), BF16)], axis=-1))
    hid_ring = MpRing(net, joined, slice(HS, WOUTP))
    arrive(*d_2)
    back_2 = back_stage(2, -2)
    arrive(*d_3)
    back_3 = back_stage(3, -3)
    arrive(*d_4)
    back_4 = back_stage(4)
    qkv_gather.done()

    query = qkv[:, :, :, 0:HS].reshape(ROWS, HS).astype(F32)
    keyraw = qkv[:, :, :, HS : 2 * HS].reshape(ROWS, HS).astype(F32)
    vals = qkv[:, :, :, 2 * HS : 3 * HS].reshape(ROWS, HS)
    query_scale = lax.rsqrt(jnp.mean(query * query, axis=-1, keepdims=True) + 1e-06)
    key_scale = lax.rsqrt(jnp.mean(keyraw * keyraw, axis=-1, keepdims=True) + 1e-06)
    qn[...] = (query * query_scale).astype(BF16)
    kn[...] = (keyraw * key_scale).astype(BF16)

    def exp_scores(block):
        first, last = block * BLK, block * BLK + BLK
        raw = dot_nt(qn[first:last], kn[0:last])
        row = lax.broadcasted_iota(jnp.int32, (BLK, 1), 0) + first
        visible = lax.broadcasted_iota(jnp.int32, (1, last), 1) <= row
        return jnp.where(visible, jnp.exp(raw * FACTOR), 0.0)

    inverse = []
    for block in range(4):
        expo = exp_scores(block)
        inverse.append(1.0 / jnp.sum(expo, axis=-1, keepdims=True))
        attended = dot_nn(expo.astype(BF16), vals[0 : block * BLK + BLK]) * inverse[block]
        joined[2 * block : 2 * block + 2, :, :, 0:HS] = attended.astype(BF16).reshape(2, NY, 32, HS)
    hid_ring.pass_on()

    for items in (back_0, back_1, back_2, back_3, back_4):
        collect(dj, items)
    give(net, datt, slice(0, HS), (dj[:, :, 0:HS].reshape(BLK, HS) * gate).astype(BF16))
    datt_gather = MpGather(net, datt, slice(0, HS))
    dhidden = dj[:, :, HS:WOUTP].reshape(BLK, 256)[:, 0:FFD] * gate
    dup = (dhidden * gate_in * sigma).astype(BF16)
    dgate_in = (dhidden * up_in * sigma * (1.0 + gate_in * (1.0 - sigma))).astype(BF16)
    give(net, dproj, slice(384, 896), jnp.concatenate([dgate_in, dup, jnp.zeros((BLK, 64), BF16)], axis=-1))
    ff_ring = MpRing(net, dproj, slice(384, WINP))
    hid_ring.done()

    def rows_of(full, pair, columns):
        return full[pl.ds(2 * pair, 2)].reshape(BLK, columns)

    pair = lax.div(z, 2)
    turned = 1 - 2 * lax.rem(z, 2)
    far_first = (mod(pair + 2, 4), mod(pair + turned, 4), mod(pair - turned, 4), pair)
    n_bufs = len(bufs) // 2
    delta_sum = SeqSum(
        net, bufs[:n_bufs], delta, lambda pair: dot_nn(rows_of(joined, pair, WOUTP), woutp[...]), far_first
    )
    dnormed_sum = SeqSum(
        net, bufs[n_bufs:], dnormed, lambda pair: dot_nn(rows_of(dproj, pair, WINP), winp[...]), far_first
    )
    delta_sum.multiply(False)
    ff_ring.pass_on()
    datt_gather.done()

    def norm_back(values, scale, grads):
        return scale * grads - values * scale**3 * jnp.mean(grads * values, axis=-1, keepdims=True)

    for block in range(3, -1, -1):
        first, last = block * BLK, block * BLK + BLK
        prob = exp_scores(block) * inverse[block]
        dout = datt[2 * block : 2 * block + 2].reshape(BLK, HS)
        dprob = dot_nt(dout, vals[0:last])
        inner = jnp.sum(prob * dprob, axis=-1, keepdims=True)
        dscore = (prob * (dprob - inner)).astype(BF16)
        dquery_n = dot_nn(dscore, kn[0:last]) * FACTOR
        dquery = norm_back(query[first:last], query_scale[first:last], dquery_n)
        dproj[2 * block : 2 * block + 2, :, :, 0:HS] = dquery.astype(BF16).reshape(2, NY, 32, HS)
        dkey_part = dot_tn(dscore, qn[first:last])
        dvalue_part = dot_tn(prob.astype(BF16), dout)
        if block == 3:
            dkey_n[...] = dkey_part
            dvalues[...] = dvalue_part
        else:
            dkey_n[0:last] = dkey_n[0:last] + dkey_part
            dvalues[0:last] = dvalues[0:last] + dvalue_part
    dkey = norm_back(keyraw, key_scale, dkey_n[...] * FACTOR)
    dproj[:, :, :, HS : 2 * HS] = dkey.astype(BF16).reshape(NZ, NY, 32, HS)
    dproj[:, :, :, 2 * HS : 3 * HS] = dvalues[...].astype(BF16).reshape(NZ, NY, 32, HS)
    delta_sum.turn()
    ff_ring.done()
    dnormed_sum.multiply(True)
    while delta_sum.turn():
        dnormed_sum.turn()

    rows = g0[z, y, c].astype(F32)
    grads = g1[z, y, c].astype(F32)
    delta_b = delta[...].astype(BF16).astype(F32)
    small = lax.broadcasted_iota(jnp.int32, (CAP, 128), 1)

    def summed(which):
        return stats[which, 0] + stats[which, 1] + stats[which, 2] + stats[which, 3]

    def pick(tile, at):
        return jnp.sum(jnp.where(small == at, tile, 0.0), axis=-1, keepdims=True)

    def spread(which):
        own = fin.at[which, net.w]
        return net.group([(own, own, device) for device in (net.mate, net.cross, net.twin)], fin.at[which, 0:3])

    stats[1, 3] = row_sums((CAP, 128), (grads * delta_b,))
    arrive(first_stats)
    tile = summed(0)
    in_scale = lax.rsqrt(pick(tile, 0) / D + 1e-05)
    gate = jax.nn.sigmoid(pick(tile, 1))
    fin[0, net.w] = (rows + gate * delta_b).astype(BF16)
    gate_stats = stats_out(1)
    first_rows = spread(0)
    while dnormed_sum.turn():
        pass
    dn = dnormed[...]
    stats[2, 3] = row_sums((CAP, 128), (dn * rows,))
    last_stats = stats_out(2)
    arrive(gate_stats)
    dlogit = pick(summed(1), 0) * gate * (1.0 - gate)
    base = grads + dlogit * rw_ref[...]
    dn = in_scale * dn
    arrive(first_rows, last_stats)
    dinput = (dn - rows * in_scale**3 * (pick(summed(2), 0) / D)).astype(BF16).astype(F32)
    fin[1, net.w] = (base + dinput).astype(BF16)
    last_rows = spread(1)
    fin_out[0] = fin[0]
    arrive(last_rows)
    fin_out[1] = fin[1]
    net.finish()


def place_kernel(sel_ref, fin_ref, res_ref, cot_ref, output_ref, grad_ref):
    sel = sel_ref[...]
    chosen = dot_tn(sel, jnp.ones((4 * CAP, 128), BF16))[:, 0:1] > 0.5
    for which, (source, target) in enumerate(((res_ref, output_ref), (cot_ref, grad_ref))):
        back = dot_tn(sel, fin_ref[which]).astype(BF16)
        target[...] = jnp.where(chosen, back, source[...])


def sum_scratch():
    return [
        pltpu.VMEM((2, NZ, NY, CAP, QD), BF16),
        pltpu.VMEM((NZ, NY, CAP, QD), BF16),
        pltpu.VMEM((NY, CAP, AW), BF16),
        pltpu.VMEM((NZ, CAP, QD - AW), BF16),
        pltpu.VMEM((NZ // 2, NY, CAP, Z_FIRST[0][1]), BF16),
        pltpu.VMEM((NZ // 2, NY, CAP, Z_FIRST[0][1]), BF16),
        pltpu.VMEM((NZ // 2, NY, CAP, Z_FIRST[1][1]), BF16),
        pltpu.VMEM((NZ // 2, NY, CAP, Z_FIRST[1][1]), BF16),
        pltpu.VMEM((NY - 1, CAP, AW), BF16),
        pltpu.VMEM((NY - 1, NZ, CAP, QD - AW), BF16),
        pltpu.VMEM((NZ - 1, CAP, QD - AW), BF16),
    ]


def local(residual, chosen_pos, chosen_count, router_weight, weight_in, weight_out, cotangent):
    n_sem = 107
    scratch = [
        pltpu.SemaphoreType.DMA((n_sem,)),
        pltpu.SemaphoreType.DMA((n_sem,)),
        pltpu.SemaphoreType.DMA((2,)),
        pltpu.VMEM((WINP, QD), BF16),
        pltpu.VMEM((WOUTP, QD), BF16),
        pltpu.VMEM((2, 8, 128), jnp.int32),
        pltpu.VMEM((2, 2, 2, CAP, QD), BF16),
        pltpu.VMEM((2, 2, CAP, QD), BF16),
        pltpu.VMEM((3, CAP, QD), BF16),
        pltpu.VMEM((NZ, NY, 2, CAP, QD), BF16),
        pltpu.VMEM((NZ, NY, 2, CAP, QD), BF16),
        pltpu.VMEM((NZ, NX, 32, WINP), BF16),
        pltpu.VMEM((NZ, NX - 1, 32, WINP), BF16),
        pltpu.VMEM((NZ, NX, 32, WOUTP), BF16),
        pltpu.VMEM((NZ, NX - 1, 32, WOUTP), BF16),
        pltpu.VMEM((NZ, 32, WINP), F32),
        pltpu.VMEM((NZ, 32, WOUTP), F32),
        pltpu.VMEM((NZ, NY, 32, 3 * HS), BF16),
        pltpu.VMEM((NZ, NY, 32, WOUTP), BF16),
        pltpu.VMEM((NZ, NY, 32, HS), BF16),
        pltpu.VMEM((NZ, NY, 32, WINP), BF16),
        pltpu.VMEM((ROWS, HS), BF16),
        pltpu.VMEM((ROWS, HS), BF16),
        pltpu.VMEM((ROWS, HS), F32),
        pltpu.VMEM((ROWS, HS), F32),
        pltpu.VMEM((CAP, QD), F32),
        pltpu.VMEM((CAP, QD), F32),
        pltpu.VMEM((3, 4, CAP, 128), F32),
        pltpu.VMEM((2, 4, CAP, QD), BF16),
    ] + sum_scratch() + sum_scratch()
    vmem = pl.BlockSpec(memory_space=pltpu.VMEM)
    anywhere = pl.BlockSpec(memory_space=pl.ANY)
    fin, sel = pl.pallas_call(
        kernel,
        out_shape=[
            jax.ShapeDtypeStruct((2, 4, CAP, QD), BF16),
            jax.ShapeDtypeStruct((4 * CAP, residual.shape[0]), BF16),
        ],
        in_specs=[vmem] * 5 + [anywhere] * 2,
        out_specs=[vmem] * 2,
        scratch_shapes=scratch,
        compiler_params=pltpu.CompilerParams(
            collective_id=0, has_side_effects=True, vmem_limit_bytes=62 * 1024 * 1024
        ),
        cost_estimate=pl.CostEstimate(flops=10**10, bytes_accessed=10**7, transcendentals=10**6),
    )(
        chosen_count[None, :], chosen_pos[None, :], residual, cotangent, router_weight[None, :],
        weight_in.T, weight_out,
    )
    fin = fin.reshape(2, 4 * CAP, QD)
    n_steps = 1
    tokens = residual.shape[0]
    columns = QD // n_steps
    block = pl.BlockSpec((tokens, columns), lambda i: (0, i))
    return pl.pallas_call(
        place_kernel,
        grid=(n_steps,),
        out_shape=[jax.ShapeDtypeStruct(residual.shape, BF16)] * 2,
        in_specs=[
            pl.BlockSpec((4 * CAP, tokens), lambda i: (0, 0)),
            pl.BlockSpec((2, 4 * CAP, columns), lambda i: (0, 0, i)),
            block,
            block,
        ],
        out_specs=[block, block],
    )(sel, fin, residual, cotangent)


def solution(mesh):
    spec = P("seq", "mp")
    return jax.shard_map(
        local,
        mesh=mesh,
        in_specs=(spec, P("seq"), P("seq"), P("mp"), P("mp", "seq"), spec, spec),
        out_specs=(spec, spec),
        check_vma=False,
    )
```

```python
import jax
import jax.numpy as jnp
from jax import lax
from jax.experimental import pallas as pl
from jax.experimental.pallas import tpu as pltpu
from jax.sharding import PartitionSpec as P

MESH = pl.DeviceIdType.MESH
D = 8192
HS = 128
NZ, NY, NX = 8, 4, 4
CAP = 16
QD = D // NX
FFD = 224
WIN = 3 * HS + 2 * FFD
WINP = 896
WOUT = HS + FFD
WOUTP = 384
ROWS = 1024
BLK = 256
HALF = QD // 2
AW = 512
BW = QD - AW
MIX = 2 * WOUTP
HID = 3 * HS
ATT = HID + 256
F32 = jnp.float32
BF16 = jnp.bfloat16
FACTOR = HS ** (-0.5)


def mod(value, n):
    return lax.rem(value + n, n)


def dot_nn(a, b):
    return jnp.dot(a, b, preferred_element_type=F32)


def dot_nt(a, b):
    return lax.dot_general(a, b, (((1,), (1,)), ((), ())), preferred_element_type=F32)


def dot_tn(a, b):
    return lax.dot_general(a, b, (((0,), (0,)), ((), ())), preferred_element_type=F32)


class Net:
    def __init__(self, send_sem, recv_sem):
        self.send_sem, self.recv_sem = send_sem, recv_sem
        self.used = 0
        self.sent = []
        seq = lax.axis_index("seq")
        x = self.x = lax.axis_index("mp")
        z = self.z = lax.div(seq, NY * 2)
        y = self.y = lax.rem(lax.div(seq, 2), NY)
        c = self.c = lax.rem(seq, 2)
        self.o = 1 - c
        self.upper = lax.rem(y, 2)
        self.w = self.upper * 2 + c
        yw = y + 1 - 2 * self.upper
        yo = mod(y - 1 + 2 * self.upper, NY)
        self.twin = self.at(z, y, self.o, x)
        self.mate = self.at(z, yw, c, x)
        self.cross = self.at(z, yw, self.o, x)
        self.beyond = self.at(z, yo, c, x)
        self.along_x = [self.at(z, y, c, mod(x + d, NX)) for d in range(1, NX)]
        self.along_y = [self.at(z, mod(y + d, NY), c, x) for d in range(1, NY)]
        self.along_z = [self.at(mod(z + d, NZ), y, c, x) for d in range(1, NZ)]
        self.xp, self.xm = self.along_x[0], self.along_x[-1]
        self.yp, self.ym = self.along_y[0], self.along_y[-1]
        self.zp, self.zm = self.along_z[0], self.along_z[-1]

    def at(self, z, y, c, x):
        return ((z * NY + y) * 2 + c, x)

    def enter(self):
        barrier = pltpu.get_barrier_semaphore()
        partners = [self.twin, self.cross] + self.along_x + self.along_y + self.along_z
        for partner in partners:
            pl.semaphore_signal(barrier, inc=1, device_id=partner, device_id_type=MESH)
        pl.semaphore_wait(barrier, len(partners))

    def group(self, copies, whole):
        send_sem, recv_sem = self.send_sem.at[self.used], self.recv_sem.at[self.used]
        self.used += 1
        for src, dst, device in copies:
            pltpu.make_async_remote_copy(
                src_ref=src, dst_ref=dst, send_sem=send_sem, recv_sem=recv_sem, device_id=device, device_id_type=MESH
            ).start()
        self.sent.append(pltpu.make_async_copy(whole, whole, send_sem))
        return pltpu.make_async_copy(whole, whole, recv_sem)

    def open(self):
        self.used += 1
        return self.used - 1

    def put(self, which, src, dst, device):
        pltpu.make_async_remote_copy(
            src_ref=src,
            dst_ref=dst,
            send_sem=self.send_sem.at[which],
            recv_sem=self.recv_sem.at[which],
            device_id=device,
            device_id_type=MESH,
        ).start()

    def close(self, which, whole):
        self.sent.append(pltpu.make_async_copy(whole, whole, self.send_sem.at[which]))
        return pltpu.make_async_copy(whole, whole, self.recv_sem.at[which])

    def send(self, src, dst, device):
        return self.group([(src, dst, device)], dst)

    def same(self, ref, device):
        return self.send(ref, ref, device)

    def finish(self):
        assert self.used == self.send_sem.shape[0], self.used
        for copy in self.sent:
            copy.wait()


def arrive(*copies):
    for copy in copies:
        copy.wait()


class MpSum:
    def __init__(self, net, part, landed):
        self.net, self.part, self.landed = net, part, landed
        self.copy = net.group(
            [(part.at[mod(net.x + d, NX)], landed.at[d - 1], net.along_x[d - 1]) for d in range(1, NX)], landed
        )

    def total(self):
        arrive(self.copy)
        total = self.part[self.net.x].astype(F32)
        for d in range(NX - 1):
            total = total + self.landed[d].astype(F32)
        return total


def rows_of_owner(full, owner, lanes, first=0, last=NZ):
    return [full.at[at, lax.rem(owner - at + NZ, NX), :, lanes] for at in range(first, last)]


def give(net, full, lanes, rows):
    for at in range(NZ):
        full[at, lax.rem(net.x - at + NZ, NX), :, lanes] = rows[at * 32 : at * 32 + 32]


class MpGather:
    def __init__(self, net, full, lanes):
        blocks = rows_of_owner(full, net.x, lanes)
        self.copy = net.group(
            [(block, block, device) for device in net.along_x for block in blocks],
            full.at[0 : NZ // NX * (NX - 1), :, :, lanes],
        )

    def done(self):
        arrive(self.copy)


class MpRing:
    def __init__(self, net, full, lanes):
        self.net, self.full, self.lanes = net, full, lanes
        blocks = rows_of_owner(full, net.x, lanes)
        self.copy = net.group(
            [(block, block, device) for device in (net.xp, net.xm) for block in blocks],
            full.at[0 : NZ // 2, :, :, lanes],
        )

    def pass_on(self):
        net = self.net
        arrive(self.copy)
        left = rows_of_owner(self.full, mod(net.x - 1, NX), self.lanes, 0, NZ // 2)
        right = rows_of_owner(self.full, mod(net.x + 1, NX), self.lanes, NZ // 2, NZ)
        self.copy = net.group(
            [(block, block, net.xp) for block in left] + [(block, block, net.xm) for block in right],
            self.full.at[0 : NZ // NX, :, :, self.lanes],
        )

    def done(self):
        arrive(self.copy)


class SeqSum:
    def __init__(self, net, bufs, out, product, order):
        self.net, self.out, self.product, self.order = net, out, product, order
        self.part, self.other, self.qa, self.qb, self.azl, self.ayl, self.byl, self.bzl = bufs
        self.along_z_a, self.along_z_b = net.open(), net.open()
        self.along_y_b = []
        self.finished = 0
        self.steps = self.finish()

    def places(self, k):
        pair = self.order[k]
        both = (2 * pair, 2 * pair + 1)
        return both, both if k < 3 else (2 * pair + 1 - lax.rem(self.net.z, 2),)

    def at_z(self, z):
        return self.net.at(z, self.net.y, self.net.c, self.net.x)

    def multiply(self, eager):
        net, copies = self.net, []
        for k, pair in enumerate(self.order):
            rows = self.product(pair)
            for place in range(2):
                for y in range(NY):
                    for core in range(2):
                        at = ((place * NY + y) * 2 + core) * CAP
                        self.part[core, 2 * pair + place, y] = rows[at : at + CAP].astype(BF16)
            both = pl.ds(2 * pair, 2)
            copies.append(net.send(self.part.at[net.o, both], self.other.at[both], net.twin))
            if k:
                self.merge(k - 1, copies[k - 1])
            if k == 3 and eager:
                self.sum_y(0)
        self.merge(3, copies[3])

    def merge(self, k, copy):
        net, part = self.net, self.part
        arrive(copy)
        both, others = self.places(k)
        for z in both:
            part[net.c, z] = (part[net.c, z].astype(F32) + self.other[z].astype(F32)).astype(BF16)
        for z in others:
            net.put(self.along_z_a, part.at[net.c, z, :, :, 0:AW], self.azl.at[net.z], self.at_z(z))
        rows = pl.ds(2 * self.order[k], 2)
        copies = [
            (part.at[net.c, rows, mod(net.y + d, NY), :, AW:QD], self.byl.at[d - 1, rows], net.along_y[d - 1])
            for d in range(1, NY)
        ]
        self.along_y_b.append(net.group(copies, self.byl.at[:, 0:2]))

    def sum_y(self, k):
        net = self.net
        arrive(self.along_y_b[k])
        both, others = self.places(k)
        for z in both:
            total = self.part[net.c, z, net.y, :, AW:QD].astype(F32)
            for d in range(NY - 1):
                total = total + self.byl[d, z].astype(F32)
            self.qb[z] = total.astype(BF16)
        for z in others:
            net.put(self.along_z_b, self.qb.at[z], self.bzl.at[net.z], self.at_z(z))
        self.finished = k + 1

    def turn(self):
        return next(self.steps, None) is not None

    def finish(self):
        net = self.net
        for k in range(self.finished, 4):
            self.sum_y(k)
        arrive(net.close(self.along_z_a, self.azl.at[0 : NZ - 1]))
        total = self.part[net.c, net.z, :, :, 0:AW].astype(F32)
        for d in range(1, NZ):
            total = total + self.azl[mod(net.z + d, NZ)].astype(F32)
        self.qa[...] = total.astype(BF16)
        copy = net.group(
            [(self.qa.at[mod(net.y + d, NY)], self.ayl.at[d - 1], net.along_y[d - 1]) for d in range(1, NY)], self.ayl
        )
        yield True
        arrive(net.close(self.along_z_b, self.bzl.at[0 : NZ - 1]))
        total = self.qb[net.z].astype(F32)
        for d in range(1, NZ):
            total = total + self.bzl[mod(net.z + d, NZ)].astype(F32)
        self.out[:, AW:QD] = total
        arrive(copy)
        total = self.qa[net.y].astype(F32)
        for d in range(NY - 1):
            total = total + self.ayl[d].astype(F32)
        self.out[:, 0:AW] = total


def row_sums(tile, columns):
    small = lax.broadcasted_iota(jnp.int32, tile, 1)
    result = jnp.zeros(tile, F32)
    for at, product in enumerate(columns):
        result = jnp.where(small == at, jnp.sum(product, axis=-1, keepdims=True), result)
    return result


def kernel(
    count_ref, pos_ref, res_ref, cot_ref, rw_ref, win_ref, wout_ref,
    fin_out, sel_out,
    send_sem, recv_sem, load_sem, winp, woutp, counts, contrib, from_twin, from_mate, g0, g1,
    pr, prl, pd, pdl, proj, dj, mixed, datt, dproj, qn, kn, dkey_n, dvalues,
    delta, dnormed, stats, fin, *bufs,
):
    net = Net(send_sem, recv_sem)
    x, y, z, c = net.x, net.y, net.z, net.c
    loads = (
        pltpu.make_async_copy(win_ref, winp.at[0:WIN], load_sem.at[0]),
        pltpu.make_async_copy(wout_ref.at[HS:WOUT], woutp.at[0:FFD], load_sem.at[1]),
        pltpu.make_async_copy(wout_ref.at[0:HS], woutp.at[256:WOUTP], load_sem.at[2]),
    )
    for load in loads:
        load.start()
    net.enter()

    counts[0] = jnp.zeros((8, 128), jnp.int32) + count_ref[...]
    arrive(net.send(counts.at[0], counts.at[1], net.twin))
    n_slots = pos_ref.shape[1]
    mine, twins = counts[0, 0:1, 0:n_slots], counts[1, 0:1, 0:n_slots]
    before = twins * c + (4 * CAP - mine - twins) * net.upper
    row = lax.broadcasted_iota(jnp.int32, (4 * CAP, n_slots), 0)
    slot = lax.broadcasted_iota(jnp.int32, (4 * CAP, n_slots), 1)
    place_of = jnp.where(row - slot == before, F32(1.0), F32(0.0)).astype(BF16)
    token = lax.broadcasted_iota(jnp.int32, (128, n_slots), 0)
    slot = lax.broadcasted_iota(jnp.int32, (128, n_slots), 1)
    token_of = jnp.where((token == pos_ref[...]) & (slot < mine), F32(1.0), F32(0.0)).astype(BF16)
    sel = dot_nt(place_of, token_of).astype(BF16)
    sel_out[...] = sel

    copies = []
    for which, source in enumerate((res_ref, cot_ref)):
        rows = dot_nn(sel, source[...]).astype(BF16)
        for chip in range(2):
            for core in range(2):
                at = (chip * 2 + core) * CAP
                contrib[which, core, chip] = rows[at : at + CAP]
        copies.append(net.send(contrib.at[which, net.o], from_twin.at[which], net.twin))
    for which in range(2):
        arrive(copies[which])
        contrib[which, c] = (contrib[which, c].astype(F32) + from_twin[which].astype(F32)).astype(BF16)
        if which == 0:
            r_copy = net.send(contrib.at[0, c], from_mate.at[0:2], net.mate)
        else:
            d_copy = net.send(contrib.at[1, c, 1 - net.upper], from_mate.at[2], net.mate)
    mine_q = lax.div(y, 2)
    arrive(r_copy)
    for place in range(2):
        g0[z, 2 * mine_q + place, c] = (
            contrib[0, c, place].astype(F32) + from_mate[place].astype(F32)
        ).astype(BF16)

    def both_ways(step, g, ys, few):
        near, far = mod(z - step + 1, NZ), mod(z + step - 1, NZ)
        if step < 4:
            right, left = g.at[near, ys, c], g.at[far, ys, c]
            whole = g.at[0:2, few, 0]
        else:
            right, left = g.at[near, ys, c, :, 0:HALF], g.at[far, ys, c, :, HALF:QD]
            whole = g.at[0, few, 0]
        return net.group([(right, right, net.zp), (left, left, net.zm)], whole)

    def r_ring(step, q):
        return both_ways(step, g0, pl.ds(2 * q, 2), slice(0, 2))

    def d_ring(step):
        return both_ways(step, g1, y, 0)

    def d_out(*ds):
        result = []
        for d in ds:
            block = g1.at[mod(z + d, NZ), y, c]
            result.append((d, net.group([(block, block, device) for device in net.along_y], g1.at[0, 0:3, 0])))
        return result

    def d_twin(items):
        result = []
        for d, copy in items:
            arrive(copy)
            result.append(net.same(g1.at[mod(z + d, NZ), :, c], net.twin))
        return result

    def r_twin(*ds):
        return [net.same(g0.at[mod(z + d, NZ), :, c], net.twin) for d in ds]

    lane = lax.broadcasted_iota(jnp.int32, (BLK, 128), 1)

    def rows_at(g, ds):
        rows = [g[mod(z + d, NZ)].reshape(BLK // 2, QD) for d in ds]
        return rows[0] if len(ds) == 1 else jnp.concatenate(rows, axis=0)

    def hand_out(part, ds, result, columns):
        for i, d in enumerate(ds):
            at = mod(z + d, NZ)
            for row in range(NY):
                owner = lax.rem(at + row, NX)
                part[at, owner, :, columns] = result[(i * NY + row) * 32 : (i * NY + row) * 32 + 32]

    def in_stage(*ds):
        rows = rows_at(g0, ds)
        result = dot_nt(rows, winp[...])
        rows_f = rows.astype(F32)
        tail = result[:, 768:896]
        at = WIN - 768
        for value in (
            jnp.sum(rows_f * rows_f, axis=-1, keepdims=True),
            jnp.sum(rows_f * rw_ref[...], axis=-1, keepdims=True),
        ):
            for _ in range(3):
                rounded = value.astype(BF16).astype(F32)
                tail = jnp.where(lane[0 : rows.shape[0]] == at, rounded, tail)
                value = value - rounded
                at += 1
        hand_out(pr, ds, result[:, 0:768].astype(BF16), slice(0, 768))
        hand_out(pr, ds, tail.astype(BF16), slice(768, WINP))
        return [(mod(z + d, NZ), MpSum(net, pr.at[mod(z + d, NZ)], prl.at[mod(z + d, NZ)])) for d in ds]

    def back_stage(*ds):
        hand_out(pd, ds, dot_nt(rows_at(g1, ds), woutp[...]).astype(BF16), slice(0, WOUTP))
        return [(mod(z + d, NZ), MpSum(net, pd.at[mod(z + d, NZ)], pdl.at[mod(z + d, NZ)])) for d in ds]

    def collect(target, items):
        for at, part in items:
            target[at] = part.total()

    def add_up(value, first, last):
        lanes = lane[0 : value.shape[0]]
        return jnp.sum(jnp.where((lanes >= first) & (lanes < last), value, 0.0), axis=-1, keepdims=True)

    def scale_of(tail):
        at = WIN - 768
        return lax.rsqrt(add_up(tail, at, at + 3) / D + 1e-05)

    def project(items):
        copies = []
        for at, part in items:
            total = part.total()
            proj[at] = total
            scale = scale_of(total[:, 768:896])
            row = lax.rem(x - at + NZ, NX)
            gate_up = total[:, 384:896] * scale
            gate_in = gate_up[:, 0:FFD]
            hidden = (gate_in * jax.nn.sigmoid(gate_in) * gate_up[:, FFD : 2 * FFD]).astype(BF16)
            mixed[at, row, :, 0:HID] = (total[:, 0:HID] * scale).astype(BF16)
            mixed[at, row, :, HID:ATT] = jnp.concatenate([hidden, jnp.zeros((32, 256 - FFD), BF16)], axis=-1)
            block = mixed.at[at, row, :, 0:ATT]
            copies.append(
                net.group([(block, block, device) for device in net.along_x], mixed.at[at, 0 : NX - 1, :, 0:ATT])
            )
        return copies

    other_q = 1 - mine_q
    p_ring = r_ring(1, mine_q)
    r_copy = net.same(g0.at[z, pl.ds(2 * mine_q, 2), c], net.beyond)
    arrive(d_copy)
    g1[z, y, c] = (contrib[1, c, net.upper].astype(F32) + from_mate[2].astype(F32)).astype(BF16)
    g_ring = d_ring(1)
    d_0 = d_out(0)
    rows = g0[z, y, c].astype(F32)
    stats[0, 3] = row_sums((CAP, 128), (rows * rows, rows * rw_ref[...]))

    def stats_out(which):
        return net.group(
            [(stats.at[which, 3], stats.at[which, d], net.along_x[d]) for d in range(3)], stats.at[which, 0:3]
        )

    first_stats = stats_out(0)
    winp[WIN:WINP] = jnp.zeros((WINP - WIN, QD), BF16)
    woutp[FFD:256] = jnp.zeros((256 - FFD, QD), BF16)
    for load in loads:
        load.wait()
    arrive(r_copy)
    q_ring = r_ring(1, other_q)
    r_0 = r_twin(0)
    arrive(g_ring)
    g_ring = d_ring(2)
    d_1 = d_out(1, -1)
    arrive(p_ring)
    p_ring = r_ring(2, mine_q)
    arrive(*r_0)
    in_0 = in_stage(0)
    arrive(q_ring)
    q_ring = r_ring(2, other_q)
    r_1 = r_twin(1, -1)
    arrive(g_ring)
    g_ring = d_ring(3)
    d_2 = d_out(2, -2)
    d_0 = d_twin(d_0)
    arrive(p_ring)
    p_ring = r_ring(3, mine_q)
    arrive(*r_1)
    in_1 = in_stage(1, -1)
    arrive(q_ring)
    q_ring = r_ring(3, other_q)
    r_2 = r_twin(2, -2)
    d_1 = d_twin(d_1)
    arrive(g_ring)
    g_ring = d_ring(4)
    d_3 = d_out(3, -3)
    arrive(p_ring)
    p_ring = r_ring(4, mine_q)
    arrive(*r_2)
    in_2 = in_stage(2, -2)
    arrive(q_ring)
    q_ring = r_ring(4, other_q)
    r_3 = r_twin(3, -3)
    d_2 = d_twin(d_2)
    arrive(*d_0)
    back_0 = back_stage(0)
    arrive(g_ring)
    d_4 = d_out(4)
    arrive(*r_3)
    in_3 = in_stage(3, -3)
    arrive(p_ring, q_ring)
    r_4 = r_twin(4)
    mixed_rows = project(in_0) + project(in_1)
    arrive(*r_4)
    in_4 = in_stage(4)
    arrive(*d_1)
    back_1 = back_stage(1, -1)
    d_3 = d_twin(d_3)
    mixed_rows += project(in_2)
    mixed_rows += project(in_3)
    arrive(*d_2)
    back_2 = back_stage(2, -2)
    d_4 = d_twin(d_4)
    mixed_rows += project(in_4)

    arrive(*d_3)
    back_3 = back_stage(3, -3)
    arrive(*d_4)
    back_4 = back_stage(4)
    tail = proj[:, :, 768:896].reshape(BLK, 128)
    in_scale = scale_of(tail)
    gate = jax.nn.sigmoid(add_up(tail, WIN - 765, WIN - 762))
    gate_up = proj[:, :, 384:896].reshape(BLK, 512) * in_scale
    gate_in = gate_up[:, 0:FFD]
    up_in = gate_up[:, FFD : 2 * FFD]
    sigma = jax.nn.sigmoid(gate_in)
    arrive(*mixed_rows)

    query = mixed[:, :, :, 0:HS].reshape(ROWS, HS).astype(F32)
    keyraw = mixed[:, :, :, HS : 2 * HS].reshape(ROWS, HS).astype(F32)
    vals = mixed[:, :, :, 2 * HS : 3 * HS].reshape(ROWS, HS)
    query_scale = lax.rsqrt(jnp.mean(query * query, axis=-1, keepdims=True) + 1e-06)
    key_scale = lax.rsqrt(jnp.mean(keyraw * keyraw, axis=-1, keepdims=True) + 1e-06)
    qn[...] = (query * query_scale).astype(BF16)
    kn[...] = (keyraw * key_scale).astype(BF16)

    def exp_scores(block):
        first, last = block * BLK, block * BLK + BLK
        raw = dot_nt(qn[first:last], kn[0:last])
        row = lax.broadcasted_iota(jnp.int32, (BLK, 1), 0) + first
        visible = lax.broadcasted_iota(jnp.int32, (1, last), 1) <= row
        return jnp.where(visible, jnp.exp(raw * FACTOR), 0.0)

    inverse = []
    for block in range(4):
        expo = exp_scores(block)
        inverse.append(1.0 / jnp.sum(expo, axis=-1, keepdims=True))
        attended = dot_nn(expo.astype(BF16), vals[0 : block * BLK + BLK]) * inverse[block]
        mixed[2 * block : 2 * block + 2, :, :, ATT:MIX] = attended.astype(BF16).reshape(2, NY, 32, HS)

    for items in (back_0, back_1, back_2, back_3, back_4):
        collect(dj, items)
    give(net, datt, slice(0, HS), (dj[:, :, 256:WOUTP].reshape(BLK, HS) * gate).astype(BF16))
    datt_gather = MpGather(net, datt, slice(0, HS))
    dhidden = dj[:, :, 0:256].reshape(BLK, 256)[:, 0:FFD] * gate
    dup = (dhidden * gate_in * sigma).astype(BF16)
    dgate_in = (dhidden * up_in * sigma * (1.0 + gate_in * (1.0 - sigma))).astype(BF16)
    give(net, dproj, slice(384, 896), jnp.concatenate([dgate_in, dup, jnp.zeros((BLK, 64), BF16)], axis=-1))
    ff_ring = MpRing(net, dproj, slice(384, WINP))

    def rows_of(full, pair, lanes):
        rows = full[pl.ds(2 * pair, 2), :, :, lanes]
        return rows.reshape(BLK, rows.shape[-1])

    pair = lax.div(z, 2)
    turned = 1 - 2 * lax.rem(z, 2)
    far_first = (mod(pair + 2, 4), mod(pair + turned, 4), mod(pair - turned, 4), pair)
    n_bufs = len(bufs) // 2
    delta_sum = SeqSum(
        net, bufs[:n_bufs], delta, lambda pair: dot_nn(rows_of(mixed, pair, slice(HID, MIX)), woutp[...]), far_first
    )
    dnormed_sum = SeqSum(
        net, bufs[n_bufs:], dnormed, lambda pair: dot_nn(rows_of(dproj, pair, slice(0, WINP)), winp[...]), far_first
    )
    delta_sum.multiply(False)
    ff_ring.pass_on()
    datt_gather.done()

    def norm_back(values, scale, grads):
        return scale * grads - values * scale**3 * jnp.mean(grads * values, axis=-1, keepdims=True)

    for block in range(3, -1, -1):
        first, last = block * BLK, block * BLK + BLK
        prob = exp_scores(block) * inverse[block]
        dout = datt[2 * block : 2 * block + 2].reshape(BLK, HS)
        dprob = dot_nt(dout, vals[0:last])
        inner = jnp.sum(prob * dprob, axis=-1, keepdims=True)
        dscore = (prob * (dprob - inner)).astype(BF16)
        dquery_n = dot_nn(dscore, kn[0:last]) * FACTOR
        dquery = norm_back(query[first:last], query_scale[first:last], dquery_n)
        dproj[2 * block : 2 * block + 2, :, :, 0:HS] = dquery.astype(BF16).reshape(2, NY, 32, HS)
        dkey_part = dot_tn(dscore, qn[first:last])
        dvalue_part = dot_tn(prob.astype(BF16), dout)
        if block == 3:
            dkey_n[...] = dkey_part
            dvalues[...] = dvalue_part
        else:
            dkey_n[0:last] = dkey_n[0:last] + dkey_part
            dvalues[0:last] = dvalues[0:last] + dvalue_part
    dkey = norm_back(keyraw, key_scale, dkey_n[...] * FACTOR)
    dproj[:, :, :, HS : 2 * HS] = dkey.astype(BF16).reshape(NZ, NY, 32, HS)
    dproj[:, :, :, 2 * HS : 3 * HS] = dvalues[...].astype(BF16).reshape(NZ, NY, 32, HS)
    delta_sum.turn()
    ff_ring.done()
    dnormed_sum.multiply(True)
    while delta_sum.turn():
        dnormed_sum.turn()

    rows = g0[z, y, c].astype(F32)
    grads = g1[z, y, c].astype(F32)
    delta_b = delta[...].astype(BF16).astype(F32)
    small = lax.broadcasted_iota(jnp.int32, (CAP, 128), 1)

    def summed(which):
        return stats[which, 0] + stats[which, 1] + stats[which, 2] + stats[which, 3]

    def pick(tile, at):
        return jnp.sum(jnp.where(small == at, tile, 0.0), axis=-1, keepdims=True)

    def spread(which):
        own = fin.at[which, net.w]
        return net.group([(own, own, device) for device in (net.mate, net.cross, net.twin)], fin.at[which, 0:3])

    stats[1, 3] = row_sums((CAP, 128), (grads * delta_b,))
    arrive(first_stats)
    tile = summed(0)
    in_scale = lax.rsqrt(pick(tile, 0) / D + 1e-05)
    gate = jax.nn.sigmoid(pick(tile, 1))
    fin[0, net.w] = (rows + gate * delta_b).astype(BF16)
    gate_stats = stats_out(1)
    first_rows = spread(0)
    while dnormed_sum.turn():
        pass
    dn = dnormed[...]
    stats[2, 3] = row_sums((CAP, 128), (dn * rows,))
    last_stats = stats_out(2)
    arrive(gate_stats)
    dlogit = pick(summed(1), 0) * gate * (1.0 - gate)
    base = grads + dlogit * rw_ref[...]
    dn = in_scale * dn
    arrive(first_rows, last_stats)
    dinput = (dn - rows * in_scale**3 * (pick(summed(2), 0) / D)).astype(BF16).astype(F32)
    fin[1, net.w] = (base + dinput).astype(BF16)
    last_rows = spread(1)
    fin_out[0] = fin[0]
    arrive(last_rows)
    fin_out[1] = fin[1]
    net.finish()


def place_kernel(sel_ref, fin_ref, res_ref, cot_ref, output_ref, grad_ref):
    sel = sel_ref[...]
    chosen = dot_tn(sel, jnp.ones((4 * CAP, 128), BF16))[:, 0:1] > 0.5
    for which, (source, target) in enumerate(((res_ref, output_ref), (cot_ref, grad_ref))):
        back = dot_tn(sel, fin_ref[which]).astype(BF16)
        target[...] = jnp.where(chosen, back, source[...])


def sum_scratch():
    return [
        pltpu.VMEM((2, NZ, NY, CAP, QD), BF16),
        pltpu.VMEM((NZ, NY, CAP, QD), BF16),
        pltpu.VMEM((NY, CAP, AW), BF16),
        pltpu.VMEM((NZ, CAP, BW), BF16),
        pltpu.VMEM((NZ, NY, CAP, AW), BF16),
        pltpu.VMEM((NY - 1, CAP, AW), BF16),
        pltpu.VMEM((NY - 1, NZ, CAP, BW), BF16),
        pltpu.VMEM((NZ, CAP, BW), BF16),
    ]


def local(residual, chosen_pos, chosen_count, router_weight, weight_in, weight_out, cotangent):
    n_sem = 96
    scratch = [
        pltpu.SemaphoreType.DMA((n_sem,)),
        pltpu.SemaphoreType.DMA((n_sem,)),
        pltpu.SemaphoreType.DMA((3,)),
        pltpu.VMEM((WINP, QD), BF16),
        pltpu.VMEM((WOUTP, QD), BF16),
        pltpu.VMEM((2, 8, 128), jnp.int32),
        pltpu.VMEM((2, 2, 2, CAP, QD), BF16),
        pltpu.VMEM((2, 2, CAP, QD), BF16),
        pltpu.VMEM((3, CAP, QD), BF16),
        pltpu.VMEM((NZ, NY, 2, CAP, QD), BF16),
        pltpu.VMEM((NZ, NY, 2, CAP, QD), BF16),
        pltpu.VMEM((NZ, NX, 32, WINP), BF16),
        pltpu.VMEM((NZ, NX - 1, 32, WINP), BF16),
        pltpu.VMEM((NZ, NX, 32, WOUTP), BF16),
        pltpu.VMEM((NZ, NX - 1, 32, WOUTP), BF16),
        pltpu.VMEM((NZ, 32, WINP), F32),
        pltpu.VMEM((NZ, 32, WOUTP), F32),
        pltpu.VMEM((NZ, NY, 32, MIX), BF16),
        pltpu.VMEM((NZ, NY, 32, HS), BF16),
        pltpu.VMEM((NZ, NY, 32, WINP), BF16),
        pltpu.VMEM((ROWS, HS), BF16),
        pltpu.VMEM((ROWS, HS), BF16),
        pltpu.VMEM((ROWS, HS), F32),
        pltpu.VMEM((ROWS, HS), F32),
        pltpu.VMEM((CAP, QD), F32),
        pltpu.VMEM((CAP, QD), F32),
        pltpu.VMEM((3, 4, CAP, 128), F32),
        pltpu.VMEM((2, 4, CAP, QD), BF16),
    ] + sum_scratch() + sum_scratch()
    vmem = pl.BlockSpec(memory_space=pltpu.VMEM)
    anywhere = pl.BlockSpec(memory_space=pl.ANY)
    fin, sel = pl.pallas_call(
        kernel,
        out_shape=[
            jax.ShapeDtypeStruct((2, 4, CAP, QD), BF16),
            jax.ShapeDtypeStruct((4 * CAP, residual.shape[0]), BF16),
        ],
        in_specs=[vmem] * 5 + [anywhere] * 2,
        out_specs=[vmem] * 2,
        scratch_shapes=scratch,
        compiler_params=pltpu.CompilerParams(
            collective_id=0, has_side_effects=True, vmem_limit_bytes=62 * 1024 * 1024
        ),
        cost_estimate=pl.CostEstimate(flops=10**10, bytes_accessed=10**7, transcendentals=10**6),
    )(
        chosen_count[None, :], chosen_pos[None, :], residual, cotangent, router_weight[None, :],
        weight_in.T, weight_out,
    )
    fin = fin.reshape(2, 4 * CAP, QD)
    n_steps = 1
    tokens = residual.shape[0]
    columns = QD // n_steps
    block = pl.BlockSpec((tokens, columns), lambda i: (0, i))
    return pl.pallas_call(
        place_kernel,
        grid=(n_steps,),
        out_shape=[jax.ShapeDtypeStruct(residual.shape, BF16)] * 2,
        in_specs=[
            pl.BlockSpec((4 * CAP, tokens), lambda i: (0, 0)),
            pl.BlockSpec((2, 4 * CAP, columns), lambda i: (0, 0, i)),
            block,
            block,
        ],
        out_specs=[block, block],
    )(sel, fin, residual, cotangent)


def solution(mesh):
    spec = P("seq", "mp")
    return jax.shard_map(
        local,
        mesh=mesh,
        in_specs=(spec, P("seq"), P("seq"), P("mp"), P("mp", "seq"), spec, spec),
        out_specs=(spec, spec),
        check_vma=False,
    )
```

```python
import jax
import jax.numpy as jnp
from jax import lax
from jax.experimental import pallas as pl
from jax.experimental.pallas import tpu as pltpu
from jax.sharding import PartitionSpec as P

MESH = pl.DeviceIdType.MESH
D = 8192
HS = 128
NZ, NY, NX = 8, 4, 4
CAP = 16
QD = D // NX
FFD = 224
WIN = 3 * HS + 2 * FFD
WINP = 896
WOUT = HS + FFD
WOUTP = 384
ROWS = 1024
BLK = 256
HALF = QD // 2
AW = 512
BW = QD - AW
MIX = 2 * WOUTP
HID = 3 * HS
ATT = HID + 256
F32 = jnp.float32
BF16 = jnp.bfloat16
FACTOR = HS ** (-0.5)


def mod(value, n):
    return lax.rem(value + n, n)


def dot_nn(a, b):
    return jnp.dot(a, b, preferred_element_type=F32)


def dot_nt(a, b):
    return lax.dot_general(a, b, (((1,), (1,)), ((), ())), preferred_element_type=F32)


def dot_tn(a, b):
    return lax.dot_general(a, b, (((0,), (0,)), ((), ())), preferred_element_type=F32)


class Net:
    def __init__(self, send_sem, recv_sem):
        self.send_sem, self.recv_sem = send_sem, recv_sem
        self.used = 0
        self.sent = []
        seq = lax.axis_index("seq")
        x = self.x = lax.axis_index("mp")
        z = self.z = lax.div(seq, NY * 2)
        y = self.y = lax.rem(lax.div(seq, 2), NY)
        c = self.c = lax.rem(seq, 2)
        self.o = 1 - c
        self.upper = lax.rem(y, 2)
        self.w = self.upper * 2 + c
        yw = y + 1 - 2 * self.upper
        yo = mod(y - 1 + 2 * self.upper, NY)
        self.twin = self.at(z, y, self.o, x)
        self.mate = self.at(z, yw, c, x)
        self.cross = self.at(z, yw, self.o, x)
        self.beyond = self.at(z, yo, c, x)
        self.along_x = [self.at(z, y, c, mod(x + d, NX)) for d in range(1, NX)]
        self.along_y = [self.at(z, mod(y + d, NY), c, x) for d in range(1, NY)]
        self.along_z = [self.at(mod(z + d, NZ), y, c, x) for d in range(1, NZ)]
        self.xp, self.xm = self.along_x[0], self.along_x[-1]
        self.yp, self.ym = self.along_y[0], self.along_y[-1]
        self.zp, self.zm = self.along_z[0], self.along_z[-1]

    def at(self, z, y, c, x):
        return ((z * NY + y) * 2 + c, x)

    def enter(self):
        barrier = pltpu.get_barrier_semaphore()
        partners = [self.twin, self.cross] + self.along_x + self.along_y + self.along_z
        for partner in partners:
            pl.semaphore_signal(barrier, inc=1, device_id=partner, device_id_type=MESH)
        pl.semaphore_wait(barrier, len(partners))

    def group(self, copies, whole):
        send_sem, recv_sem = self.send_sem.at[self.used], self.recv_sem.at[self.used]
        self.used += 1
        for src, dst, device in copies:
            pltpu.make_async_remote_copy(
                src_ref=src, dst_ref=dst, send_sem=send_sem, recv_sem=recv_sem, device_id=device, device_id_type=MESH
            ).start()
        self.sent.append(pltpu.make_async_copy(whole, whole, send_sem))
        return pltpu.make_async_copy(whole, whole, recv_sem)

    def open(self):
        self.used += 1
        return self.used - 1

    def put(self, which, src, dst, device):
        pltpu.make_async_remote_copy(
            src_ref=src,
            dst_ref=dst,
            send_sem=self.send_sem.at[which],
            recv_sem=self.recv_sem.at[which],
            device_id=device,
            device_id_type=MESH,
        ).start()

    def close(self, which, whole):
        self.sent.append(pltpu.make_async_copy(whole, whole, self.send_sem.at[which]))
        return pltpu.make_async_copy(whole, whole, self.recv_sem.at[which])

    def send(self, src, dst, device):
        return self.group([(src, dst, device)], dst)

    def same(self, ref, device):
        return self.send(ref, ref, device)

    def finish(self):
        assert self.used == self.send_sem.shape[0], self.used
        for copy in self.sent:
            copy.wait()


def arrive(*copies):
    for copy in copies:
        copy.wait()


class MpSum:
    def __init__(self, net, part, landed):
        self.net, self.part, self.landed = net, part, landed
        self.copy = net.group(
            [(part.at[mod(net.x + d, NX)], landed.at[d - 1], net.along_x[d - 1]) for d in range(1, NX)], landed
        )

    def total(self):
        arrive(self.copy)
        total = self.part[self.net.x].astype(F32)
        for d in range(NX - 1):
            total = total + self.landed[d].astype(F32)
        return total


def rows_of_owner(full, owner, lanes, first=0, last=NZ):
    return [full.at[at, lax.rem(owner - at + NZ, NX), :, lanes] for at in range(first, last)]


def give(net, full, lanes, rows):
    for at in range(NZ):
        full[at, lax.rem(net.x - at + NZ, NX), :, lanes] = rows[at * 32 : at * 32 + 32]


class MpGather:
    def __init__(self, net, full, lanes):
        blocks = rows_of_owner(full, net.x, lanes)
        self.copy = net.group(
            [(block, block, device) for device in net.along_x for block in blocks],
            full.at[0 : NZ // NX * (NX - 1), :, :, lanes],
        )

    def done(self):
        arrive(self.copy)


class MpRing:
    def __init__(self, net, full, lanes):
        self.net, self.full, self.lanes = net, full, lanes
        blocks = rows_of_owner(full, net.x, lanes)
        self.copy = net.group(
            [(block, block, device) for device in (net.xp, net.xm) for block in blocks],
            full.at[0 : NZ // 2, :, :, lanes],
        )

    def pass_on(self):
        net = self.net
        arrive(self.copy)
        left = rows_of_owner(self.full, mod(net.x - 1, NX), self.lanes, 0, NZ // 2)
        right = rows_of_owner(self.full, mod(net.x + 1, NX), self.lanes, NZ // 2, NZ)
        self.copy = net.group(
            [(block, block, net.xp) for block in left] + [(block, block, net.xm) for block in right],
            self.full.at[0 : NZ // NX, :, :, self.lanes],
        )

    def done(self):
        arrive(self.copy)


class SeqSum:
    def __init__(self, net, bufs, out, product, order):
        self.net, self.out, self.product, self.order = net, out, product, order
        self.part, self.qa, self.qb, self.azl, self.ayl, self.byl, self.bzl = bufs
        self.along_z_a, self.along_z_b = net.open(), net.open()
        self.along_y_b = []
        self.steps = self.finish()

    def places(self, k):
        pair = self.order[k]
        both = (2 * pair, 2 * pair + 1)
        return both, both if k < 3 else (2 * pair + 1 - lax.rem(self.net.z, 2),)

    def at_z(self, z):
        return self.net.at(z, self.net.y, self.net.c, self.net.x)

    def multiply(self):
        for half in range(2):
            pairs = self.order[2 * half : 2 * half + 2]
            rows = self.product(pairs)
            for i, pair in enumerate(pairs):
                for place in range(2):
                    for y in range(NY):
                        at = ((i * 2 + place) * NY + y) * CAP
                        self.part[2 * pair + place, y] = rows[at : at + CAP].astype(BF16)
                self.send(2 * half + i)

    def send(self, k):
        net, part = self.net, self.part
        for z in self.places(k)[1]:
            net.put(self.along_z_a, part.at[z, :, :, 0:AW], self.azl.at[net.z], self.at_z(z))
        rows = pl.ds(2 * self.order[k], 2)
        copies = [
            (part.at[rows, mod(net.y + d, NY), :, AW:QD], self.byl.at[d - 1, rows], net.along_y[d - 1])
            for d in range(1, NY)
        ]
        self.along_y_b.append(net.group(copies, self.byl.at[:, 0:2]))

    def sum_y(self, k):
        net = self.net
        arrive(self.along_y_b[k])
        both, others = self.places(k)
        for z in both:
            total = self.part[z, net.y, :, AW:QD].astype(F32)
            for d in range(NY - 1):
                total = total + self.byl[d, z].astype(F32)
            self.qb[z] = total.astype(BF16)
        for z in others:
            net.put(self.along_z_b, self.qb.at[z], self.bzl.at[net.z], self.at_z(z))

    def turn(self):
        return next(self.steps, None) is not None

    def finish(self):
        net = self.net
        for k in range(4):
            self.sum_y(k)
        arrive(net.close(self.along_z_a, self.azl.at[0 : NZ - 1]))
        total = self.part[net.z, :, :, 0:AW].astype(F32)
        for d in range(1, NZ):
            total = total + self.azl[mod(net.z + d, NZ)].astype(F32)
        self.qa[...] = total.astype(BF16)
        copy = net.group(
            [(self.qa.at[mod(net.y + d, NY)], self.ayl.at[d - 1], net.along_y[d - 1]) for d in range(1, NY)], self.ayl
        )
        yield True
        arrive(net.close(self.along_z_b, self.bzl.at[0 : NZ - 1]))
        total = self.qb[net.z].astype(F32)
        for d in range(1, NZ):
            total = total + self.bzl[mod(net.z + d, NZ)].astype(F32)
        self.out[:, AW:QD] = total
        arrive(copy)
        total = self.qa[net.y].astype(F32)
        for d in range(NY - 1):
            total = total + self.ayl[d].astype(F32)
        self.out[:, 0:AW] = total


def row_sums(tile, columns):
    small = lax.broadcasted_iota(jnp.int32, tile, 1)
    result = jnp.zeros(tile, F32)
    for at, product in enumerate(columns):
        result = jnp.where(small == at, jnp.sum(product, axis=-1, keepdims=True), result)
    return result


def kernel(
    count_ref, pos_ref, res_ref, cot_ref, rw_ref, win_ref, wout_ref,
    fin_out, sel_out,
    send_sem, recv_sem, load_sem, winp, woutp, counts, contrib, from_twin, from_mate, g0, g1,
    pr, prl, pd, pdl, proj, dj, mixed, datt, dproj, winp2, woutp2, mixed2, dproj2, qn, kn, dkey_n, dvalues,
    delta, dnormed, stats, fin, *bufs,
):
    net = Net(send_sem, recv_sem)
    x, y, z, c = net.x, net.y, net.z, net.c
    loads = (
        pltpu.make_async_copy(win_ref, winp.at[0:WIN], load_sem.at[0]),
        pltpu.make_async_copy(wout_ref.at[HS:WOUT], woutp.at[0:FFD], load_sem.at[1]),
        pltpu.make_async_copy(wout_ref.at[0:HS], woutp.at[256:WOUTP], load_sem.at[2]),
    )
    for load in loads:
        load.start()
    net.enter()

    counts[0] = jnp.zeros((8, 128), jnp.int32) + count_ref[...]
    arrive(net.send(counts.at[0], counts.at[1], net.twin))
    n_slots = pos_ref.shape[1]
    mine, twins = counts[0, 0:1, 0:n_slots], counts[1, 0:1, 0:n_slots]
    before = twins * c + (4 * CAP - mine - twins) * net.upper
    row = lax.broadcasted_iota(jnp.int32, (4 * CAP, n_slots), 0)
    slot = lax.broadcasted_iota(jnp.int32, (4 * CAP, n_slots), 1)
    place_of = jnp.where(row - slot == before, F32(1.0), F32(0.0)).astype(BF16)
    token = lax.broadcasted_iota(jnp.int32, (128, n_slots), 0)
    slot = lax.broadcasted_iota(jnp.int32, (128, n_slots), 1)
    token_of = jnp.where((token == pos_ref[...]) & (slot < mine), F32(1.0), F32(0.0)).astype(BF16)
    sel = dot_nt(place_of, token_of).astype(BF16)
    sel_out[...] = sel

    copies = []
    for which, source in enumerate((res_ref, cot_ref)):
        rows = dot_nn(sel, source[...]).astype(BF16)
        for chip in range(2):
            for core in range(2):
                at = (chip * 2 + core) * CAP
                contrib[which, core, chip] = rows[at : at + CAP]
        copies.append(net.send(contrib.at[which, net.o], from_twin.at[which], net.twin))
    for which in range(2):
        arrive(copies[which])
        contrib[which, c] = (contrib[which, c].astype(F32) + from_twin[which].astype(F32)).astype(BF16)
        if which == 0:
            r_copy = net.send(contrib.at[0, c], from_mate.at[0:2], net.mate)
        else:
            d_copy = net.send(contrib.at[1, c, 1 - net.upper], from_mate.at[2], net.mate)
    mine_q = lax.div(y, 2)
    arrive(r_copy)
    for place in range(2):
        g0[z, 2 * mine_q + place, c] = (
            contrib[0, c, place].astype(F32) + from_mate[place].astype(F32)
        ).astype(BF16)

    def both_ways(step, g, ys, few):
        near, far = mod(z - step + 1, NZ), mod(z + step - 1, NZ)
        if step < 4:
            right, left = g.at[near, ys, c], g.at[far, ys, c]
            whole = g.at[0:2, few, 0]
        else:
            right, left = g.at[near, ys, c, :, 0:HALF], g.at[far, ys, c, :, HALF:QD]
            whole = g.at[0, few, 0]
        return net.group([(right, right, net.zp), (left, left, net.zm)], whole)

    def r_ring(step, q):
        return both_ways(step, g0, pl.ds(2 * q, 2), slice(0, 2))

    def d_ring(step):
        return both_ways(step, g1, y, 0)

    def d_out(*ds):
        result = []
        for d in ds:
            block = g1.at[mod(z + d, NZ), y, c]
            result.append((d, net.group([(block, block, device) for device in net.along_y], g1.at[0, 0:3, 0])))
        return result

    def d_twin(items):
        result = []
        for d, copy in items:
            arrive(copy)
            result.append(net.same(g1.at[mod(z + d, NZ), :, c], net.twin))
        return result

    def r_twin(*ds):
        return [net.same(g0.at[mod(z + d, NZ), :, c], net.twin) for d in ds]

    lane = lax.broadcasted_iota(jnp.int32, (BLK, 128), 1)

    def rows_at(g, ds):
        rows = [g[mod(z + d, NZ)].reshape(BLK // 2, QD) for d in ds]
        return rows[0] if len(ds) == 1 else jnp.concatenate(rows, axis=0)

    def hand_out(part, ds, result, columns):
        for i, d in enumerate(ds):
            at = mod(z + d, NZ)
            for row in range(NY):
                owner = lax.rem(at + row, NX)
                part[at, owner, :, columns] = result[(i * NY + row) * 32 : (i * NY + row) * 32 + 32]

    def in_stage(*ds):
        rows = rows_at(g0, ds)
        result = dot_nt(rows, winp[...])
        rows_f = rows.astype(F32)
        tail = result[:, 768:896]
        at = WIN - 768
        for value in (
            jnp.sum(rows_f * rows_f, axis=-1, keepdims=True),
            jnp.sum(rows_f * rw_ref[...], axis=-1, keepdims=True),
        ):
            for _ in range(3):
                rounded = value.astype(BF16).astype(F32)
                tail = jnp.where(lane[0 : rows.shape[0]] == at, rounded, tail)
                value = value - rounded
                at += 1
        hand_out(pr, ds, result[:, 0:768].astype(BF16), slice(0, 768))
        hand_out(pr, ds, tail.astype(BF16), slice(768, WINP))
        return [(mod(z + d, NZ), MpSum(net, pr.at[mod(z + d, NZ)], prl.at[mod(z + d, NZ)])) for d in ds]

    def back_stage(*ds):
        hand_out(pd, ds, dot_nt(rows_at(g1, ds), woutp[...]).astype(BF16), slice(0, WOUTP))
        return [(mod(z + d, NZ), MpSum(net, pd.at[mod(z + d, NZ)], pdl.at[mod(z + d, NZ)])) for d in ds]

    def collect(target, items):
        for at, part in items:
            target[at] = part.total()

    def add_up(value, first, last):
        lanes = lane[0 : value.shape[0]]
        return jnp.sum(jnp.where((lanes >= first) & (lanes < last), value, 0.0), axis=-1, keepdims=True)

    def scale_of(tail):
        at = WIN - 768
        return lax.rsqrt(add_up(tail, at, at + 3) / D + 1e-05)

    def project(items):
        copies = []
        for at, part in items:
            total = part.total()
            proj[at] = total
            scale = scale_of(total[:, 768:896])
            row = lax.rem(x - at + NZ, NX)
            gate_up = total[:, 384:896] * scale
            gate_in = gate_up[:, 0:FFD]
            hidden = (gate_in * jax.nn.sigmoid(gate_in) * gate_up[:, FFD : 2 * FFD]).astype(BF16)
            mixed[at, row, :, 0:HID] = (total[:, 0:HID] * scale).astype(BF16)
            mixed[at, row, :, HID:ATT] = jnp.concatenate([hidden, jnp.zeros((32, 256 - FFD), BF16)], axis=-1)
            block = mixed.at[at, row, :, 0:ATT]
            copies.append(
                net.group([(block, block, device) for device in net.along_x], mixed.at[at, 0 : NX - 1, :, 0:ATT])
            )
        return copies

    def weights_out(quarter):
        rows = slice(quarter * WINP // 4, (quarter + 1) * WINP // 4)
        return net.send(winp.at[rows], winp2.at[rows], net.twin)

    other_q = 1 - mine_q
    p_ring = r_ring(1, mine_q)
    r_copy = net.same(g0.at[z, pl.ds(2 * mine_q, 2), c], net.beyond)
    arrive(d_copy)
    g1[z, y, c] = (contrib[1, c, net.upper].astype(F32) + from_mate[2].astype(F32)).astype(BF16)
    g_ring = d_ring(1)
    d_0 = d_out(0)
    rows = g0[z, y, c].astype(F32)
    stats[0, 3] = row_sums((CAP, 128), (rows * rows, rows * rw_ref[...]))

    def stats_out(which):
        return net.group(
            [(stats.at[which, 3], stats.at[which, d], net.along_x[d]) for d in range(3)], stats.at[which, 0:3]
        )

    first_stats = stats_out(0)
    winp[WIN:WINP] = jnp.zeros((WINP - WIN, QD), BF16)
    woutp[FFD:256] = jnp.zeros((256 - FFD, QD), BF16)
    for load in loads:
        load.wait()
    arrive(r_copy)
    q_ring = r_ring(1, other_q)
    r_0 = r_twin(0)
    arrive(g_ring)
    g_ring = d_ring(2)
    d_1 = d_out(1, -1)
    arrive(p_ring)
    p_ring = r_ring(2, mine_q)
    arrive(*r_0)
    in_0 = in_stage(0)
    twin_weights = [net.send(woutp, woutp2, net.twin)]
    arrive(q_ring)
    q_ring = r_ring(2, other_q)
    r_1 = r_twin(1, -1)
    arrive(g_ring)
    g_ring = d_ring(3)
    d_2 = d_out(2, -2)
    d_0 = d_twin(d_0)
    arrive(p_ring)
    p_ring = r_ring(3, mine_q)
    arrive(*r_1)
    in_1 = in_stage(1, -1)
    twin_weights.append(weights_out(0))
    arrive(q_ring)
    q_ring = r_ring(3, other_q)
    r_2 = r_twin(2, -2)
    d_1 = d_twin(d_1)
    arrive(g_ring)
    g_ring = d_ring(4)
    d_3 = d_out(3, -3)
    arrive(p_ring)
    p_ring = r_ring(4, mine_q)
    arrive(*r_2)
    in_2 = in_stage(2, -2)
    twin_weights.append(weights_out(1))
    arrive(q_ring)
    q_ring = r_ring(4, other_q)
    r_3 = r_twin(3, -3)
    d_2 = d_twin(d_2)
    arrive(*d_0)
    back_0 = back_stage(0)
    arrive(g_ring)
    d_4 = d_out(4)
    arrive(*r_3)
    in_3 = in_stage(3, -3)
    twin_weights.append(weights_out(2))
    arrive(p_ring, q_ring)
    r_4 = r_twin(4)
    mixed_rows = project(in_0) + project(in_1)
    arrive(*r_4)
    in_4 = in_stage(4)
    twin_weights.append(weights_out(3))
    arrive(*d_1)
    back_1 = back_stage(1, -1)
    d_3 = d_twin(d_3)
    mixed_rows += project(in_2)
    mixed_rows += project(in_3)
    arrive(*d_2)
    back_2 = back_stage(2, -2)
    d_4 = d_twin(d_4)
    mixed_rows += project(in_4)

    arrive(*d_3)
    back_3 = back_stage(3, -3)
    arrive(*d_4)
    back_4 = back_stage(4)
    tail = proj[:, :, 768:896].reshape(BLK, 128)
    in_scale = scale_of(tail)
    gate = jax.nn.sigmoid(add_up(tail, WIN - 765, WIN - 762))
    gate_up = proj[:, :, 384:896].reshape(BLK, 512) * in_scale
    gate_in = gate_up[:, 0:FFD]
    up_in = gate_up[:, FFD : 2 * FFD]
    sigma = jax.nn.sigmoid(gate_in)
    arrive(*mixed_rows)

    query = mixed[:, :, :, 0:HS].reshape(ROWS, HS).astype(F32)
    keyraw = mixed[:, :, :, HS : 2 * HS].reshape(ROWS, HS).astype(F32)
    vals = mixed[:, :, :, 2 * HS : 3 * HS].reshape(ROWS, HS)
    query_scale = lax.rsqrt(jnp.mean(query * query, axis=-1, keepdims=True) + 1e-06)
    key_scale = lax.rsqrt(jnp.mean(keyraw * keyraw, axis=-1, keepdims=True) + 1e-06)
    qn[...] = (query * query_scale).astype(BF16)
    kn[...] = (keyraw * key_scale).astype(BF16)

    def exp_scores(block):
        first, last = block * BLK, block * BLK + BLK
        raw = dot_nt(qn[first:last], kn[0:last])
        row = lax.broadcasted_iota(jnp.int32, (BLK, 1), 0) + first
        visible = lax.broadcasted_iota(jnp.int32, (1, last), 1) <= row
        return jnp.where(visible, jnp.exp(raw * FACTOR), 0.0)

    inverse = []
    for block in range(4):
        expo = exp_scores(block)
        inverse.append(1.0 / jnp.sum(expo, axis=-1, keepdims=True))
        attended = dot_nn(expo.astype(BF16), vals[0 : block * BLK + BLK]) * inverse[block]
        mixed[2 * block : 2 * block + 2, :, :, ATT:MIX] = attended.astype(BF16).reshape(2, NY, 32, HS)
    own_rows, twin_half = pl.multiple_of(c * CAP, CAP), pl.multiple_of(net.o * CAP, CAP)
    mixed_copy = net.send(mixed.at[:, :, pl.ds(twin_half, CAP), HID:MIX], mixed2, net.twin)

    for items in (back_0, back_1, back_2, back_3, back_4):
        collect(dj, items)
    give(net, datt, slice(0, HS), (dj[:, :, 256:WOUTP].reshape(BLK, HS) * gate).astype(BF16))
    datt_gather = MpGather(net, datt, slice(0, HS))
    dhidden = dj[:, :, 0:256].reshape(BLK, 256)[:, 0:FFD] * gate
    dup = (dhidden * gate_in * sigma).astype(BF16)
    dgate_in = (dhidden * up_in * sigma * (1.0 + gate_in * (1.0 - sigma))).astype(BF16)
    give(net, dproj, slice(384, 896), jnp.concatenate([dgate_in, dup, jnp.zeros((BLK, 64), BF16)], axis=-1))
    ff_ring = MpRing(net, dproj, slice(384, WINP))

    def rows_of(full, pairs, lanes, first):
        rows = [full[pl.ds(2 * pair, 2), :, pl.ds(first, CAP), lanes] for pair in pairs]
        return jnp.concatenate([part.reshape(BLK // 2, part.shape[-1]) for part in rows], axis=0)

    def both_cores(full, lanes, weights, twin_rows, twin_weights, copies):
        def product(pairs):
            own = dot_nn(rows_of(full, pairs, lanes, own_rows), weights[...])
            while copies:
                arrive(copies.pop())
            return own + dot_nn(rows_of(twin_rows, pairs, slice(0, twin_rows.shape[-1]), 0), twin_weights[...])

        return product

    pair = lax.div(z, 2)
    turned = 1 - 2 * lax.rem(z, 2)
    far_first = (mod(pair + 2, 4), mod(pair + turned, 4), mod(pair - turned, 4), pair)
    n_bufs = len(bufs) // 2
    dproj_copies = twin_weights[1:]
    delta_sum = SeqSum(
        net, bufs[:n_bufs], delta,
        both_cores(mixed, slice(HID, MIX), woutp, mixed2, woutp2, [twin_weights[0], mixed_copy]), far_first,
    )
    dnormed_sum = SeqSum(
        net, bufs[n_bufs:], dnormed,
        both_cores(dproj, slice(0, WINP), winp, dproj2, winp2, dproj_copies), far_first,
    )
    delta_sum.multiply()
    ff_ring.pass_on()
    datt_gather.done()

    def norm_back(values, scale, grads):
        return scale * grads - values * scale**3 * jnp.mean(grads * values, axis=-1, keepdims=True)

    for block in range(3, -1, -1):
        first, last = block * BLK, block * BLK + BLK
        prob = exp_scores(block) * inverse[block]
        dout = datt[2 * block : 2 * block + 2].reshape(BLK, HS)
        dprob = dot_nt(dout, vals[0:last])
        inner = jnp.sum(prob * dprob, axis=-1, keepdims=True)
        dscore = (prob * (dprob - inner)).astype(BF16)
        dquery_n = dot_nn(dscore, kn[0:last]) * FACTOR
        dquery = norm_back(query[first:last], query_scale[first:last], dquery_n)
        dproj[2 * block : 2 * block + 2, :, :, 0:HS] = dquery.astype(BF16).reshape(2, NY, 32, HS)
        dkey_part = dot_tn(dscore, qn[first:last])
        dvalue_part = dot_tn(prob.astype(BF16), dout)
        if block == 3:
            dkey_n[...] = dkey_part
            dvalues[...] = dvalue_part
        else:
            dkey_n[0:last] = dkey_n[0:last] + dkey_part
            dvalues[0:last] = dvalues[0:last] + dvalue_part
    dkey = norm_back(keyraw, key_scale, dkey_n[...] * FACTOR)
    dproj[:, :, :, HS : 2 * HS] = dkey.astype(BF16).reshape(NZ, NY, 32, HS)
    dproj[:, :, :, 2 * HS : 3 * HS] = dvalues[...].astype(BF16).reshape(NZ, NY, 32, HS)
    ff_ring.done()
    dproj_copies.append(net.send(dproj.at[:, :, pl.ds(twin_half, CAP)], dproj2, net.twin))
    dnormed_sum.multiply()
    while delta_sum.turn():
        pass

    rows = g0[z, y, c].astype(F32)
    grads = g1[z, y, c].astype(F32)
    delta_b = delta[...].astype(BF16).astype(F32)
    small = lax.broadcasted_iota(jnp.int32, (CAP, 128), 1)

    def summed(which):
        return stats[which, 0] + stats[which, 1] + stats[which, 2] + stats[which, 3]

    def pick(tile, at):
        return jnp.sum(jnp.where(small == at, tile, 0.0), axis=-1, keepdims=True)

    def spread(which):
        own = fin.at[which, net.w]
        return net.group([(own, own, device) for device in (net.mate, net.cross, net.twin)], fin.at[which, 0:3])

    stats[1, 3] = row_sums((CAP, 128), (grads * delta_b,))
    arrive(first_stats)
    tile = summed(0)
    in_scale = lax.rsqrt(pick(tile, 0) / D + 1e-05)
    gate = jax.nn.sigmoid(pick(tile, 1))
    fin[0, net.w] = (rows + gate * delta_b).astype(BF16)
    gate_stats = stats_out(1)
    first_rows = spread(0)
    while dnormed_sum.turn():
        pass
    dn = dnormed[...]
    stats[2, 3] = row_sums((CAP, 128), (dn * rows,))
    last_stats = stats_out(2)
    arrive(gate_stats)
    dlogit = pick(summed(1), 0) * gate * (1.0 - gate)
    base = grads + dlogit * rw_ref[...]
    dn = in_scale * dn
    arrive(first_rows, last_stats)
    dinput = (dn - rows * in_scale**3 * (pick(summed(2), 0) / D)).astype(BF16).astype(F32)
    fin[1, net.w] = (base + dinput).astype(BF16)
    last_rows = spread(1)
    fin_out[0] = fin[0]
    arrive(last_rows)
    fin_out[1] = fin[1]
    net.finish()


def place_kernel(sel_ref, fin_ref, res_ref, cot_ref, output_ref, grad_ref):
    sel = sel_ref[...]
    chosen = dot_tn(sel, jnp.ones((4 * CAP, 128), BF16))[:, 0:1] > 0.5
    for which, (source, target) in enumerate(((res_ref, output_ref), (cot_ref, grad_ref))):
        back = dot_tn(sel, fin_ref[which]).astype(BF16)
        target[...] = jnp.where(chosen, back, source[...])


def sum_scratch():
    return [
        pltpu.VMEM((NZ, NY, CAP, QD), BF16),
        pltpu.VMEM((NY, CAP, AW), BF16),
        pltpu.VMEM((NZ, CAP, BW), BF16),
        pltpu.VMEM((NZ, NY, CAP, AW), BF16),
        pltpu.VMEM((NY - 1, CAP, AW), BF16),
        pltpu.VMEM((NY - 1, NZ, CAP, BW), BF16),
        pltpu.VMEM((NZ, CAP, BW), BF16),
    ]


def local(residual, chosen_pos, chosen_count, router_weight, weight_in, weight_out, cotangent):
    n_sem = 95
    scratch = [
        pltpu.SemaphoreType.DMA((n_sem,)),
        pltpu.SemaphoreType.DMA((n_sem,)),
        pltpu.SemaphoreType.DMA((3,)),
        pltpu.VMEM((WINP, QD), BF16),
        pltpu.VMEM((WOUTP, QD), BF16),
        pltpu.VMEM((2, 8, 128), jnp.int32),
        pltpu.VMEM((2, 2, 2, CAP, QD), BF16),
        pltpu.VMEM((2, 2, CAP, QD), BF16),
        pltpu.VMEM((3, CAP, QD), BF16),
        pltpu.VMEM((NZ, NY, 2, CAP, QD), BF16),
        pltpu.VMEM((NZ, NY, 2, CAP, QD), BF16),
        pltpu.VMEM((NZ, NX, 32, WINP), BF16),
        pltpu.VMEM((NZ, NX - 1, 32, WINP), BF16),
        pltpu.VMEM((NZ, NX, 32, WOUTP), BF16),
        pltpu.VMEM((NZ, NX - 1, 32, WOUTP), BF16),
        pltpu.VMEM((NZ, 32, WINP), F32),
        pltpu.VMEM((NZ, 32, WOUTP), F32),
        pltpu.VMEM((NZ, NY, 32, MIX), BF16),
        pltpu.VMEM((NZ, NY, 32, HS), BF16),
        pltpu.VMEM((NZ, NY, 32, WINP), BF16),
        pltpu.VMEM((WINP, QD), BF16),
        pltpu.VMEM((WOUTP, QD), BF16),
        pltpu.VMEM((NZ, NY, CAP, WOUTP), BF16),
        pltpu.VMEM((NZ, NY, CAP, WINP), BF16),
        pltpu.VMEM((ROWS, HS), BF16),
        pltpu.VMEM((ROWS, HS), BF16),
        pltpu.VMEM((ROWS, HS), F32),
        pltpu.VMEM((ROWS, HS), F32),
        pltpu.VMEM((CAP, QD), F32),
        pltpu.VMEM((CAP, QD), F32),
        pltpu.VMEM((3, 4, CAP, 128), F32),
        pltpu.VMEM((2, 4, CAP, QD), BF16),
    ] + sum_scratch() + sum_scratch()
    vmem = pl.BlockSpec(memory_space=pltpu.VMEM)
    anywhere = pl.BlockSpec(memory_space=pl.ANY)
    fin, sel = pl.pallas_call(
        kernel,
        out_shape=[
            jax.ShapeDtypeStruct((2, 4, CAP, QD), BF16),
            jax.ShapeDtypeStruct((4 * CAP, residual.shape[0]), BF16),
        ],
        in_specs=[vmem] * 5 + [anywhere] * 2,
        out_specs=[vmem] * 2,
        scratch_shapes=scratch,
        compiler_params=pltpu.CompilerParams(
            collective_id=0, has_side_effects=True, vmem_limit_bytes=62 * 1024 * 1024
        ),
        cost_estimate=pl.CostEstimate(flops=10**10, bytes_accessed=10**7, transcendentals=10**6),
    )(
        chosen_count[None, :], chosen_pos[None, :], residual, cotangent, router_weight[None, :],
        weight_in.T, weight_out,
    )
    fin = fin.reshape(2, 4 * CAP, QD)
    n_steps = 1
    tokens = residual.shape[0]
    columns = QD // n_steps
    block = pl.BlockSpec((tokens, columns), lambda i: (0, i))
    return pl.pallas_call(
        place_kernel,
        grid=(n_steps,),
        out_shape=[jax.ShapeDtypeStruct(residual.shape, BF16)] * 2,
        in_specs=[
            pl.BlockSpec((4 * CAP, tokens), lambda i: (0, 0)),
            pl.BlockSpec((2, 4 * CAP, columns), lambda i: (0, 0, i)),
            block,
            block,
        ],
        out_specs=[block, block],
    )(sel, fin, residual, cotangent)


def solution(mesh):
    spec = P("seq", "mp")
    return jax.shard_map(
        local,
        mesh=mesh,
        in_specs=(spec, P("seq"), P("seq"), P("mp"), P("mp", "seq"), spec, spec),
        out_specs=(spec, spec),
        check_vma=False,
    )
```

```python
import jax
import jax.numpy as jnp
from jax import lax
from jax.experimental import pallas as pl
from jax.experimental.pallas import tpu as pltpu
from jax.sharding import PartitionSpec as P

MESH = pl.DeviceIdType.MESH
D = 8192
HS = 128
NZ, NY, NX = 8, 4, 4
CAP = 16
QD = D // NX
FFD = 224
WIN = 3 * HS + 2 * FFD
WINP = 896
WOUT = HS + FFD
WOUTP = 384
ROWS = 1024
BLK = 256
HALF = QD // 2
AW = 512
BW = QD - AW
MIX = 2 * WOUTP
HID = 3 * HS
ATT = HID + 256
F32 = jnp.float32
BF16 = jnp.bfloat16
FACTOR = HS ** (-0.5)


def mod(value, n):
    return lax.rem(value + n, n)


def dot_nn(a, b):
    return jnp.dot(a, b, preferred_element_type=F32)


def dot_nt(a, b):
    return lax.dot_general(a, b, (((1,), (1,)), ((), ())), preferred_element_type=F32)


def dot_tn(a, b):
    return lax.dot_general(a, b, (((0,), (0,)), ((), ())), preferred_element_type=F32)


class Net:
    def __init__(self, send_sem, recv_sem):
        self.send_sem, self.recv_sem = send_sem, recv_sem
        self.used = 0
        self.sent = []
        seq = lax.axis_index("seq")
        x = self.x = lax.axis_index("mp")
        z = self.z = lax.div(seq, NY * 2)
        y = self.y = lax.rem(lax.div(seq, 2), NY)
        c = self.c = lax.rem(seq, 2)
        self.o = 1 - c
        self.upper = lax.rem(y, 2)
        self.w = self.upper * 2 + c
        yw = y + 1 - 2 * self.upper
        yo = mod(y - 1 + 2 * self.upper, NY)
        self.twin = self.at(z, y, self.o, x)
        self.mate = self.at(z, yw, c, x)
        self.cross = self.at(z, yw, self.o, x)
        self.beyond = self.at(z, yo, c, x)
        self.along_x = [self.at(z, y, c, mod(x + d, NX)) for d in range(1, NX)]
        self.along_y = [self.at(z, mod(y + d, NY), c, x) for d in range(1, NY)]
        self.along_z = [self.at(mod(z + d, NZ), y, c, x) for d in range(1, NZ)]
        self.xp, self.xm = self.along_x[0], self.along_x[-1]
        self.yp, self.ym = self.along_y[0], self.along_y[-1]
        self.zp, self.zm = self.along_z[0], self.along_z[-1]

    def at(self, z, y, c, x):
        return ((z * NY + y) * 2 + c, x)

    def enter(self):
        barrier = pltpu.get_barrier_semaphore()
        partners = [self.twin, self.cross] + self.along_x + self.along_y + self.along_z
        for partner in partners:
            pl.semaphore_signal(barrier, inc=1, device_id=partner, device_id_type=MESH)
        pl.semaphore_wait(barrier, len(partners))

    def group(self, copies, whole):
        send_sem, recv_sem = self.send_sem.at[self.used], self.recv_sem.at[self.used]
        self.used += 1
        for src, dst, device in copies:
            pltpu.make_async_remote_copy(
                src_ref=src, dst_ref=dst, send_sem=send_sem, recv_sem=recv_sem, device_id=device, device_id_type=MESH
            ).start()
        self.sent.append(pltpu.make_async_copy(whole, whole, send_sem))
        return pltpu.make_async_copy(whole, whole, recv_sem)

    def open(self):
        self.used += 1
        return self.used - 1

    def put(self, which, src, dst, device):
        pltpu.make_async_remote_copy(
            src_ref=src,
            dst_ref=dst,
            send_sem=self.send_sem.at[which],
            recv_sem=self.recv_sem.at[which],
            device_id=device,
            device_id_type=MESH,
        ).start()

    def close(self, which, whole):
        self.sent.append(pltpu.make_async_copy(whole, whole, self.send_sem.at[which]))
        return pltpu.make_async_copy(whole, whole, self.recv_sem.at[which])

    def send(self, src, dst, device):
        return self.group([(src, dst, device)], dst)

    def same(self, ref, device):
        return self.send(ref, ref, device)

    def finish(self):
        assert self.used == self.send_sem.shape[0], self.used
        for copy in self.sent:
            copy.wait()


def arrive(*copies):
    for copy in copies:
        copy.wait()


class MpSum:
    def __init__(self, net, part, landed):
        self.net, self.part, self.landed = net, part, landed
        self.copy = net.group(
            [(part.at[mod(net.x + d, NX)], landed.at[d - 1], net.along_x[d - 1]) for d in range(1, NX)], landed
        )

    def total(self):
        arrive(self.copy)
        total = self.part[self.net.x].astype(F32)
        for d in range(NX - 1):
            total = total + self.landed[d].astype(F32)
        return total


def rows_of_owner(full, owner, lanes, first=0, last=NZ):
    return [full.at[at, lax.rem(owner - at + NZ, NX), :, lanes] for at in range(first, last)]


def give(net, full, lanes, rows):
    for at in range(NZ):
        full[at, lax.rem(net.x - at + NZ, NX), :, lanes] = rows[at * 32 : at * 32 + 32]


class MpGather:
    def __init__(self, net, full, lanes):
        blocks = rows_of_owner(full, net.x, lanes)
        self.copy = net.group(
            [(block, block, device) for device in net.along_x for block in blocks],
            full.at[0 : NZ // NX * (NX - 1), :, :, lanes],
        )

    def done(self):
        arrive(self.copy)


class MpRing:
    def __init__(self, net, full, lanes):
        self.net, self.full, self.lanes = net, full, lanes
        blocks = rows_of_owner(full, net.x, lanes)
        self.copy = net.group(
            [(block, block, device) for device in (net.xp, net.xm) for block in blocks],
            full.at[0 : NZ // 2, :, :, lanes],
        )

    def pass_on(self):
        net = self.net
        arrive(self.copy)
        left = rows_of_owner(self.full, mod(net.x - 1, NX), self.lanes, 0, NZ // 2)
        right = rows_of_owner(self.full, mod(net.x + 1, NX), self.lanes, NZ // 2, NZ)
        self.copy = net.group(
            [(block, block, net.xp) for block in left] + [(block, block, net.xm) for block in right],
            self.full.at[0 : NZ // NX, :, :, self.lanes],
        )

    def done(self):
        arrive(self.copy)


class SeqSum:
    def __init__(self, net, bufs, out, product, order):
        self.net, self.out, self.product, self.order = net, out, product, order
        self.part, self.qa, self.qb, self.azl, self.ayl, self.byl, self.bzl = bufs
        self.along_z_a, self.along_z_b = net.open(), net.open()
        self.along_y_b = []
        self.steps = self.finish()

    def places(self, k):
        pair = self.order[k]
        both = (2 * pair, 2 * pair + 1)
        return both, both if k < 3 else (2 * pair + 1 - lax.rem(self.net.z, 2),)

    def at_z(self, z):
        return self.net.at(z, self.net.y, self.net.c, self.net.x)

    def multiply(self):
        for half in range(2):
            pairs = self.order[2 * half : 2 * half + 2]
            rows = self.product(pairs)
            for i, pair in enumerate(pairs):
                for place in range(2):
                    for y in range(NY):
                        at = ((i * 2 + place) * NY + y) * CAP
                        self.part[2 * pair + place, y] = rows[at : at + CAP].astype(BF16)
                self.send(2 * half + i)

    def send(self, k):
        net, part = self.net, self.part
        for z in self.places(k)[1]:
            net.put(self.along_z_a, part.at[z, :, :, 0:AW], self.azl.at[net.z], self.at_z(z))
        rows = pl.ds(2 * self.order[k], 2)
        copies = [
            (part.at[rows, mod(net.y + d, NY), :, AW:QD], self.byl.at[d - 1, rows], net.along_y[d - 1])
            for d in range(1, NY)
        ]
        self.along_y_b.append(net.group(copies, self.byl.at[:, 0:2]))

    def sum_y(self, k):
        net = self.net
        arrive(self.along_y_b[k])
        both, others = self.places(k)
        for z in both:
            total = self.part[z, net.y, :, AW:QD].astype(F32)
            for d in range(NY - 1):
                total = total + self.byl[d, z].astype(F32)
            self.qb[z] = total.astype(BF16)
        for z in others:
            net.put(self.along_z_b, self.qb.at[z], self.bzl.at[net.z], self.at_z(z))

    def turn(self):
        return next(self.steps, None) is not None

    def finish(self):
        net = self.net
        for k in range(4):
            self.sum_y(k)
        arrive(net.close(self.along_z_a, self.azl.at[0 : NZ - 1]))
        total = self.part[net.z, :, :, 0:AW].astype(F32)
        for d in range(1, NZ):
            total = total + self.azl[mod(net.z + d, NZ)].astype(F32)
        self.qa[...] = total.astype(BF16)
        copy = net.group(
            [(self.qa.at[mod(net.y + d, NY)], self.ayl.at[d - 1], net.along_y[d - 1]) for d in range(1, NY)], self.ayl
        )
        yield True
        arrive(net.close(self.along_z_b, self.bzl.at[0 : NZ - 1]))
        total = self.qb[net.z].astype(F32)
        for d in range(1, NZ):
            total = total + self.bzl[mod(net.z + d, NZ)].astype(F32)
        self.out[:, AW:QD] = total
        arrive(copy)
        total = self.qa[net.y].astype(F32)
        for d in range(NY - 1):
            total = total + self.ayl[d].astype(F32)
        self.out[:, 0:AW] = total


def row_sums(tile, columns):
    small = lax.broadcasted_iota(jnp.int32, tile, 1)
    result = jnp.zeros(tile, F32)
    for at, product in enumerate(columns):
        result = jnp.where(small == at, jnp.sum(product, axis=-1, keepdims=True), result)
    return result


def kernel(
    count_ref, pos_ref, res_ref, cot_ref, rw_ref, win_ref, wout_ref,
    fin_out, sel_out,
    send_sem, recv_sem, load_sem, winp, woutp, counts, contrib, from_twin, from_mate, g0, g1,
    pr, prl, pd, pdl, proj, dj, mixed, datt, dproj, winp2, woutp2, mixed2, dproj2, qn, kn, dkey_n, dvalues,
    delta, dnormed, stats, fin, *bufs,
):
    net = Net(send_sem, recv_sem)
    x, y, z, c = net.x, net.y, net.z, net.c
    loads = (
        pltpu.make_async_copy(win_ref, winp.at[0:WIN], load_sem.at[0]),
        pltpu.make_async_copy(wout_ref.at[HS:WOUT], woutp.at[0:FFD], load_sem.at[1]),
        pltpu.make_async_copy(wout_ref.at[0:HS], woutp.at[256:WOUTP], load_sem.at[2]),
    )
    for load in loads:
        load.start()
    net.enter()

    counts[0] = jnp.zeros((8, 128), jnp.int32) + count_ref[...]
    arrive(net.send(counts.at[0], counts.at[1], net.twin))
    n_slots = pos_ref.shape[1]
    mine, twins = counts[0, 0:1, 0:n_slots], counts[1, 0:1, 0:n_slots]
    before = twins * c + (4 * CAP - mine - twins) * net.upper
    row = lax.broadcasted_iota(jnp.int32, (4 * CAP, n_slots), 0)
    slot = lax.broadcasted_iota(jnp.int32, (4 * CAP, n_slots), 1)
    place_of = jnp.where(row - slot == before, F32(1.0), F32(0.0)).astype(BF16)
    token = lax.broadcasted_iota(jnp.int32, (128, n_slots), 0)
    slot = lax.broadcasted_iota(jnp.int32, (128, n_slots), 1)
    token_of = jnp.where((token == pos_ref[...]) & (slot < mine), F32(1.0), F32(0.0)).astype(BF16)
    sel = dot_nt(place_of, token_of).astype(BF16)
    sel_out[...] = sel

    copies = []
    for which, source in enumerate((res_ref, cot_ref)):
        rows = dot_nn(sel, source[...]).astype(BF16)
        for chip in range(2):
            for core in range(2):
                at = (chip * 2 + core) * CAP
                contrib[which, core, chip] = rows[at : at + CAP]
        copies.append(net.send(contrib.at[which, net.o], from_twin.at[which], net.twin))
    for which in range(2):
        arrive(copies[which])
        contrib[which, c] = (contrib[which, c].astype(F32) + from_twin[which].astype(F32)).astype(BF16)
        if which == 0:
            r_copy = net.send(contrib.at[0, c], from_mate.at[0:2], net.mate)
        else:
            d_copy = net.send(contrib.at[1, c, 1 - net.upper], from_mate.at[2], net.mate)
    mine_q = lax.div(y, 2)
    arrive(r_copy)
    for place in range(2):
        g0[z, 2 * mine_q + place, c] = (
            contrib[0, c, place].astype(F32) + from_mate[place].astype(F32)
        ).astype(BF16)

    def both_ways(step, g, ys, few):
        near, far = mod(z - step + 1, NZ), mod(z + step - 1, NZ)
        if step < 4:
            right, left = g.at[near, ys, c], g.at[far, ys, c]
            whole = g.at[0:2, few, 0]
        else:
            right, left = g.at[near, ys, c, :, 0:HALF], g.at[far, ys, c, :, HALF:QD]
            whole = g.at[0, few, 0]
        return net.group([(right, right, net.zp), (left, left, net.zm)], whole)

    def r_ring(step, q):
        return both_ways(step, g0, pl.ds(2 * q, 2), slice(0, 2))

    def d_ring(step):
        return both_ways(step, g1, y, 0)

    def d_out(*ds):
        result = []
        for d in ds:
            block = g1.at[mod(z + d, NZ), y, c]
            result.append((d, net.group([(block, block, device) for device in net.along_y], g1.at[0, 0:3, 0])))
        return result

    def d_twin(items):
        result = []
        for d, copy in items:
            arrive(copy)
            result.append(net.same(g1.at[mod(z + d, NZ), :, c], net.twin))
        return result

    def r_twin(*ds):
        return [net.same(g0.at[mod(z + d, NZ), :, c], net.twin) for d in ds]

    lane = lax.broadcasted_iota(jnp.int32, (BLK, 128), 1)

    def rows_at(g, ds):
        rows = [g[mod(z + d, NZ)].reshape(BLK // 2, QD) for d in ds]
        return rows[0] if len(ds) == 1 else jnp.concatenate(rows, axis=0)

    def hand_out(part, ds, result, columns):
        for i, d in enumerate(ds):
            at = mod(z + d, NZ)
            for row in range(NY):
                owner = lax.rem(at + row, NX)
                part[at, owner, :, columns] = result[(i * NY + row) * 32 : (i * NY + row) * 32 + 32]

    def in_stage(*ds):
        rows = rows_at(g0, ds)
        result = dot_nt(rows, winp[...])
        rows_f = rows.astype(F32)
        tail = result[:, 768:896]
        at = WIN - 768
        for value in (
            jnp.sum(rows_f * rows_f, axis=-1, keepdims=True),
            jnp.sum(rows_f * rw_ref[...], axis=-1, keepdims=True),
        ):
            for _ in range(3):
                rounded = value.astype(BF16).astype(F32)
                tail = jnp.where(lane[0 : rows.shape[0]] == at, rounded, tail)
                value = value - rounded
                at += 1
        hand_out(pr, ds, result[:, 0:768].astype(BF16), slice(0, 768))
        hand_out(pr, ds, tail.astype(BF16), slice(768, WINP))
        return [(mod(z + d, NZ), MpSum(net, pr.at[mod(z + d, NZ)], prl.at[mod(z + d, NZ)])) for d in ds]

    def back_stage(*ds):
        hand_out(pd, ds, dot_nt(rows_at(g1, ds), woutp[...]).astype(BF16), slice(0, WOUTP))
        return [(mod(z + d, NZ), MpSum(net, pd.at[mod(z + d, NZ)], pdl.at[mod(z + d, NZ)])) for d in ds]

    def collect(target, items):
        for at, part in items:
            target[at] = part.total()

    def add_up(value, first, last):
        lanes = lane[0 : value.shape[0]]
        return jnp.sum(jnp.where((lanes >= first) & (lanes < last), value, 0.0), axis=-1, keepdims=True)

    def scale_of(tail):
        at = WIN - 768
        return lax.rsqrt(add_up(tail, at, at + 3) / D + 1e-05)

    def project(items):
        copies = []
        for at, part in items:
            total = part.total()
            proj[at] = total
            scale = scale_of(total[:, 768:896])
            row = lax.rem(x - at + NZ, NX)
            gate_up = total[:, 384:896] * scale
            gate_in = gate_up[:, 0:FFD]
            hidden = (gate_in * jax.nn.sigmoid(gate_in) * gate_up[:, FFD : 2 * FFD]).astype(BF16)
            mixed[at, row, :, 0:HID] = (total[:, 0:HID] * scale).astype(BF16)
            mixed[at, row, :, HID:ATT] = jnp.concatenate([hidden, jnp.zeros((32, 256 - FFD), BF16)], axis=-1)
            block = mixed.at[at, row, :, 0:ATT]
            copies.append(
                net.group([(block, block, device) for device in net.along_x], mixed.at[at, 0 : NX - 1, :, 0:ATT])
            )
        return copies

    def weights_out(quarter):
        rows = slice(quarter * WINP // 4, (quarter + 1) * WINP // 4)
        return net.send(winp.at[rows], winp2.at[rows], net.twin)

    other_q = 1 - mine_q
    p_ring = r_ring(1, mine_q)
    r_copy = net.same(g0.at[z, pl.ds(2 * mine_q, 2), c], net.beyond)
    arrive(d_copy)
    g1[z, y, c] = (contrib[1, c, net.upper].astype(F32) + from_mate[2].astype(F32)).astype(BF16)
    g_ring = d_ring(1)
    d_0 = d_out(0)
    rows = g0[z, y, c].astype(F32)
    stats[0, 3] = row_sums((CAP, 128), (rows * rows, rows * rw_ref[...]))

    def stats_out(which):
        return net.group(
            [(stats.at[which, 3], stats.at[which, d], net.along_x[d]) for d in range(3)], stats.at[which, 0:3]
        )

    first_stats = stats_out(0)
    winp[WIN:WINP] = jnp.zeros((WINP - WIN, QD), BF16)
    woutp[FFD:256] = jnp.zeros((256 - FFD, QD), BF16)
    for load in loads:
        load.wait()
    arrive(r_copy)
    q_ring = r_ring(1, other_q)
    r_0 = r_twin(0)
    arrive(g_ring)
    g_ring = d_ring(2)
    d_1 = d_out(1, -1)
    arrive(p_ring)
    p_ring = r_ring(2, mine_q)
    arrive(*r_0)
    in_0 = in_stage(0)
    twin_weights = [net.send(woutp, woutp2, net.twin)]
    arrive(q_ring)
    q_ring = r_ring(2, other_q)
    r_1 = r_twin(1, -1)
    arrive(g_ring)
    g_ring = d_ring(3)
    d_2 = d_out(2, -2)
    d_0 = d_twin(d_0)
    arrive(p_ring)
    p_ring = r_ring(3, mine_q)
    arrive(*r_1)
    in_1 = in_stage(1, -1)
    twin_weights.append(weights_out(0))
    arrive(q_ring)
    q_ring = r_ring(3, other_q)
    r_2 = r_twin(2, -2)
    d_1 = d_twin(d_1)
    arrive(g_ring)
    g_ring = d_ring(4)
    d_3 = d_out(3, -3)
    arrive(p_ring)
    p_ring = r_ring(4, mine_q)
    arrive(*r_2)
    in_2 = in_stage(2, -2)
    twin_weights.append(weights_out(1))
    arrive(q_ring)
    q_ring = r_ring(4, other_q)
    r_3 = r_twin(3, -3)
    d_2 = d_twin(d_2)
    arrive(*d_0)
    back_0 = back_stage(0)
    arrive(g_ring)
    d_4 = d_out(4)
    arrive(*r_3)
    in_3 = in_stage(3, -3)
    twin_weights.append(weights_out(2))
    arrive(p_ring, q_ring)
    r_4 = r_twin(4)
    mixed_rows = project(in_0) + project(in_1)
    arrive(*r_4)
    in_4 = in_stage(4)
    twin_weights.append(weights_out(3))
    arrive(*d_1)
    back_1 = back_stage(1, -1)
    d_3 = d_twin(d_3)
    mixed_rows += project(in_2)
    mixed_rows += project(in_3)
    arrive(*d_2)
    back_2 = back_stage(2, -2)
    d_4 = d_twin(d_4)
    mixed_rows += project(in_4)

    arrive(*d_3)
    back_3 = back_stage(3, -3)
    arrive(*d_4)
    back_4 = back_stage(4)
    tail = proj[:, :, 768:896].reshape(BLK, 128)
    in_scale = scale_of(tail)
    gate = jax.nn.sigmoid(add_up(tail, WIN - 765, WIN - 762))
    gate_up = proj[:, :, 384:896].reshape(BLK, 512) * in_scale
    gate_in = gate_up[:, 0:FFD]
    up_in = gate_up[:, FFD : 2 * FFD]
    sigma = jax.nn.sigmoid(gate_in)
    arrive(*mixed_rows)

    query = mixed[:, :, :, 0:HS].reshape(ROWS, HS).astype(F32)
    keyraw = mixed[:, :, :, HS : 2 * HS].reshape(ROWS, HS).astype(F32)
    vals = mixed[:, :, :, 2 * HS : 3 * HS].reshape(ROWS, HS)
    query_scale = lax.rsqrt(jnp.mean(query * query, axis=-1, keepdims=True) + 1e-06)
    key_scale = lax.rsqrt(jnp.mean(keyraw * keyraw, axis=-1, keepdims=True) + 1e-06)
    qn[...] = (query * query_scale).astype(BF16)
    kn[...] = (keyraw * key_scale).astype(BF16)

    def exp_scores(block):
        first, last = block * BLK, block * BLK + BLK
        raw = dot_nt(qn[first:last], kn[0:last])
        row = lax.broadcasted_iota(jnp.int32, (BLK, 1), 0) + first
        visible = lax.broadcasted_iota(jnp.int32, (1, last), 1) <= row
        return jnp.where(visible, jnp.exp(raw * FACTOR), 0.0)

    inverse = []
    for block in range(4):
        expo = exp_scores(block)
        inverse.append(1.0 / jnp.sum(expo, axis=-1, keepdims=True))
        attended = dot_nn(expo.astype(BF16), vals[0 : block * BLK + BLK]) * inverse[block]
        mixed[2 * block : 2 * block + 2, :, :, ATT:MIX] = attended.astype(BF16).reshape(2, NY, 32, HS)
    own_rows, twin_half = pl.multiple_of(c * CAP, CAP), pl.multiple_of(net.o * CAP, CAP)
    mixed_copy = net.send(mixed.at[:, :, pl.ds(twin_half, CAP), HID:MIX], mixed2, net.twin)

    for items in (back_0, back_1, back_2, back_3, back_4):
        collect(dj, items)
    give(net, datt, slice(0, HS), (dj[:, :, 256:WOUTP].reshape(BLK, HS) * gate).astype(BF16))
    datt_gather = MpGather(net, datt, slice(0, HS))
    dhidden = dj[:, :, 0:256].reshape(BLK, 256)[:, 0:FFD] * gate
    dup = (dhidden * gate_in * sigma).astype(BF16)
    dgate_in = (dhidden * up_in * sigma * (1.0 + gate_in * (1.0 - sigma))).astype(BF16)
    give(net, dproj, slice(384, 896), jnp.concatenate([dgate_in, dup, jnp.zeros((BLK, 64), BF16)], axis=-1))
    ff_ring = MpRing(net, dproj, slice(384, WINP))

    def rows_of(full, pairs, lanes, first):
        rows = [full[pl.ds(2 * pair, 2), :, pl.ds(first, CAP), lanes] for pair in pairs]
        return jnp.concatenate([part.reshape(BLK // 2, part.shape[-1]) for part in rows], axis=0)

    def both_cores(full, lanes, weights, twin_rows, twin_weights, copies):
        def product(pairs):
            own = dot_nn(rows_of(full, pairs, lanes, own_rows), weights[...])
            while copies:
                arrive(copies.pop())
            return own + dot_nn(rows_of(twin_rows, pairs, slice(0, twin_rows.shape[-1]), 0), twin_weights[...])

        return product

    pair = lax.div(z, 2)
    turned = 1 - 2 * lax.rem(z, 2)
    far_first = (mod(pair + 2, 4), mod(pair + turned, 4), mod(pair - turned, 4), pair)
    n_bufs = len(bufs) // 2
    dproj_copies = twin_weights[1:]
    delta_sum = SeqSum(
        net, bufs[:n_bufs], delta,
        both_cores(mixed, slice(HID, MIX), woutp, mixed2, woutp2, [twin_weights[0], mixed_copy]), far_first,
    )
    dnormed_sum = SeqSum(
        net, bufs[n_bufs:], dnormed,
        both_cores(dproj, slice(0, WINP), winp, dproj2, winp2, dproj_copies), far_first,
    )
    delta_sum.multiply()
    ff_ring.pass_on()
    datt_gather.done()

    def norm_back(values, scale, grads):
        return scale * grads - values * scale**3 * jnp.mean(grads * values, axis=-1, keepdims=True)

    for block in range(3, -1, -1):
        first, last = block * BLK, block * BLK + BLK
        prob = exp_scores(block) * inverse[block]
        dout = datt[2 * block : 2 * block + 2].reshape(BLK, HS)
        dprob = dot_nt(dout, vals[0:last])
        inner = jnp.sum(prob * dprob, axis=-1, keepdims=True)
        dscore = (prob * (dprob - inner)).astype(BF16)
        dquery_n = dot_nn(dscore, kn[0:last]) * FACTOR
        dquery = norm_back(query[first:last], query_scale[first:last], dquery_n)
        dproj[2 * block : 2 * block + 2, :, :, 0:HS] = dquery.astype(BF16).reshape(2, NY, 32, HS)
        dkey_part = dot_tn(dscore, qn[first:last])
        dvalue_part = dot_tn(prob.astype(BF16), dout)
        if block == 3:
            dkey_n[...] = dkey_part
            dvalues[...] = dvalue_part
        else:
            dkey_n[0:last] = dkey_n[0:last] + dkey_part
            dvalues[0:last] = dvalues[0:last] + dvalue_part
    dkey = norm_back(keyraw, key_scale, dkey_n[...] * FACTOR)
    dproj[:, :, :, HS : 2 * HS] = dkey.astype(BF16).reshape(NZ, NY, 32, HS)
    dproj[:, :, :, 2 * HS : 3 * HS] = dvalues[...].astype(BF16).reshape(NZ, NY, 32, HS)
    delta_sum.turn()
    ff_ring.done()
    dproj_copies.append(net.send(dproj.at[:, :, pl.ds(twin_half, CAP)], dproj2, net.twin))
    dnormed_sum.multiply()
    while delta_sum.turn():
        pass

    rows = g0[z, y, c].astype(F32)
    grads = g1[z, y, c].astype(F32)
    delta_b = delta[...].astype(BF16).astype(F32)
    small = lax.broadcasted_iota(jnp.int32, (CAP, 128), 1)

    def summed(which):
        return stats[which, 0] + stats[which, 1] + stats[which, 2] + stats[which, 3]

    def pick(tile, at):
        return jnp.sum(jnp.where(small == at, tile, 0.0), axis=-1, keepdims=True)

    def spread(which):
        own = fin.at[which, net.w]
        return net.group([(own, own, device) for device in (net.mate, net.cross, net.twin)], fin.at[which, 0:3])

    stats[1, 3] = row_sums((CAP, 128), (grads * delta_b,))
    arrive(first_stats)
    tile = summed(0)
    in_scale = lax.rsqrt(pick(tile, 0) / D + 1e-05)
    gate = jax.nn.sigmoid(pick(tile, 1))
    fin[0, net.w] = (rows + gate * delta_b).astype(BF16)
    gate_stats = stats_out(1)
    first_rows = spread(0)
    while dnormed_sum.turn():
        pass
    dn = dnormed[...]
    stats[2, 3] = row_sums((CAP, 128), (dn * rows,))
    last_stats = stats_out(2)
    arrive(gate_stats)
    dlogit = pick(summed(1), 0) * gate * (1.0 - gate)
    base = grads + dlogit * rw_ref[...]
    dn = in_scale * dn
    arrive(first_rows, last_stats)
    dinput = (dn - rows * in_scale**3 * (pick(summed(2), 0) / D)).astype(BF16).astype(F32)
    fin[1, net.w] = (base + dinput).astype(BF16)
    last_rows = spread(1)
    fin_out[0] = fin[0]
    arrive(last_rows)
    fin_out[1] = fin[1]
    net.finish()


def place_kernel(sel_ref, fin_ref, res_ref, cot_ref, output_ref, grad_ref):
    sel = sel_ref[...]
    chosen = dot_tn(sel, jnp.ones((4 * CAP, 128), BF16))[:, 0:1] > 0.5
    for which, (source, target) in enumerate(((res_ref, output_ref), (cot_ref, grad_ref))):
        back = dot_tn(sel, fin_ref[which]).astype(BF16)
        target[...] = jnp.where(chosen, back, source[...])


def sum_scratch():
    return [
        pltpu.VMEM((NZ, NY, CAP, QD), BF16),
        pltpu.VMEM((NY, CAP, AW), BF16),
        pltpu.VMEM((NZ, CAP, BW), BF16),
        pltpu.VMEM((NZ, NY, CAP, AW), BF16),
        pltpu.VMEM((NY - 1, CAP, AW), BF16),
        pltpu.VMEM((NY - 1, NZ, CAP, BW), BF16),
        pltpu.VMEM((NZ, CAP, BW), BF16),
    ]


def local(residual, chosen_pos, chosen_count, router_weight, weight_in, weight_out, cotangent):
    n_sem = 95
    scratch = [
        pltpu.SemaphoreType.DMA((n_sem,)),
        pltpu.SemaphoreType.DMA((n_sem,)),
        pltpu.SemaphoreType.DMA((3,)),
        pltpu.VMEM((WINP, QD), BF16),
        pltpu.VMEM((WOUTP, QD), BF16),
        pltpu.VMEM((2, 8, 128), jnp.int32),
        pltpu.VMEM((2, 2, 2, CAP, QD), BF16),
        pltpu.VMEM((2, 2, CAP, QD), BF16),
        pltpu.VMEM((3, CAP, QD), BF16),
        pltpu.VMEM((NZ, NY, 2, CAP, QD), BF16),
        pltpu.VMEM((NZ, NY, 2, CAP, QD), BF16),
        pltpu.VMEM((NZ, NX, 32, WINP), BF16),
        pltpu.VMEM((NZ, NX - 1, 32, WINP), BF16),
        pltpu.VMEM((NZ, NX, 32, WOUTP), BF16),
        pltpu.VMEM((NZ, NX - 1, 32, WOUTP), BF16),
        pltpu.VMEM((NZ, 32, WINP), F32),
        pltpu.VMEM((NZ, 32, WOUTP), F32),
        pltpu.VMEM((NZ, NY, 32, MIX), BF16),
        pltpu.VMEM((NZ, NY, 32, HS), BF16),
        pltpu.VMEM((NZ, NY, 32, WINP), BF16),
        pltpu.VMEM((WINP, QD), BF16),
        pltpu.VMEM((WOUTP, QD), BF16),
        pltpu.VMEM((NZ, NY, CAP, WOUTP), BF16),
        pltpu.VMEM((NZ, NY, CAP, WINP), BF16),
        pltpu.VMEM((ROWS, HS), BF16),
        pltpu.VMEM((ROWS, HS), BF16),
        pltpu.VMEM((ROWS, HS), F32),
        pltpu.VMEM((ROWS, HS), F32),
        pltpu.VMEM((CAP, QD), F32),
        pltpu.VMEM((CAP, QD), F32),
        pltpu.VMEM((3, 4, CAP, 128), F32),
        pltpu.VMEM((2, 4, CAP, QD), BF16),
    ] + sum_scratch() + sum_scratch()
    vmem = pl.BlockSpec(memory_space=pltpu.VMEM)
    anywhere = pl.BlockSpec(memory_space=pl.ANY)
    fin, sel = pl.pallas_call(
        kernel,
        out_shape=[
            jax.ShapeDtypeStruct((2, 4, CAP, QD), BF16),
            jax.ShapeDtypeStruct((4 * CAP, residual.shape[0]), BF16),
        ],
        in_specs=[vmem] * 5 + [anywhere] * 2,
        out_specs=[vmem] * 2,
        scratch_shapes=scratch,
        compiler_params=pltpu.CompilerParams(
            collective_id=0, has_side_effects=True, vmem_limit_bytes=62 * 1024 * 1024
        ),
        cost_estimate=pl.CostEstimate(flops=10**10, bytes_accessed=10**7, transcendentals=10**6),
    )(
        chosen_count[None, :], chosen_pos[None, :], residual, cotangent, router_weight[None, :],
        weight_in.T, weight_out,
    )
    fin = fin.reshape(2, 4 * CAP, QD)
    n_steps = 1
    tokens = residual.shape[0]
    columns = QD // n_steps
    block = pl.BlockSpec((tokens, columns), lambda i: (0, i))
    return pl.pallas_call(
        place_kernel,
        grid=(n_steps,),
        out_shape=[jax.ShapeDtypeStruct(residual.shape, BF16)] * 2,
        in_specs=[
            pl.BlockSpec((4 * CAP, tokens), lambda i: (0, 0)),
            pl.BlockSpec((2, 4 * CAP, columns), lambda i: (0, 0, i)),
            block,
            block,
        ],
        out_specs=[block, block],
    )(sel, fin, residual, cotangent)


def solution(mesh):
    spec = P("seq", "mp")
    return jax.shard_map(
        local,
        mesh=mesh,
        in_specs=(spec, P("seq"), P("seq"), P("mp"), P("mp", "seq"), spec, spec),
        out_specs=(spec, spec),
        check_vma=False,
    )
```

```python
import jax
import jax.numpy as jnp
from jax import lax
from jax.experimental import pallas as pl
from jax.experimental.pallas import tpu as pltpu
from jax.sharding import PartitionSpec as P

MESH = pl.DeviceIdType.MESH
D = 8192
HS = 128
NZ, NY, NX = 8, 4, 4
CAP = 16
QD = D // NX
FFD = 224
WIN = 3 * HS + 2 * FFD
WINP = 896
WOUT = HS + FFD
WOUTP = 384
ROWS = 1024
BLK = 256
HALF = QD // 2
AW = 768
BW = QD - AW
MIX = 2 * WOUTP
HID = 3 * HS
ATT = HID + 256
F32 = jnp.float32
BF16 = jnp.bfloat16
FACTOR = HS ** (-0.5)


def mod(value, n):
    return lax.rem(value + n, n)


def dot_nn(a, b):
    return jnp.dot(a, b, preferred_element_type=F32)


def dot_nt(a, b):
    return lax.dot_general(a, b, (((1,), (1,)), ((), ())), preferred_element_type=F32)


def dot_tn(a, b):
    return lax.dot_general(a, b, (((0,), (0,)), ((), ())), preferred_element_type=F32)


class Net:
    def __init__(self, send_sem, recv_sem):
        self.send_sem, self.recv_sem = send_sem, recv_sem
        self.used = 0
        self.sent = []
        seq = lax.axis_index("seq")
        x = self.x = lax.axis_index("mp")
        z = self.z = lax.div(seq, NY * 2)
        y = self.y = lax.rem(lax.div(seq, 2), NY)
        c = self.c = lax.rem(seq, 2)
        self.o = 1 - c
        self.upper = lax.rem(y, 2)
        self.w = self.upper * 2 + c
        yw = y + 1 - 2 * self.upper
        yo = mod(y - 1 + 2 * self.upper, NY)
        self.twin = self.at(z, y, self.o, x)
        self.mate = self.at(z, yw, c, x)
        self.cross = self.at(z, yw, self.o, x)
        self.beyond = self.at(z, yo, c, x)
        self.along_x = [self.at(z, y, c, mod(x + d, NX)) for d in range(1, NX)]
        self.along_y = [self.at(z, mod(y + d, NY), c, x) for d in range(1, NY)]
        self.along_z = [self.at(mod(z + d, NZ), y, c, x) for d in range(1, NZ)]
        self.xp, self.xm = self.along_x[0], self.along_x[-1]
        self.yp, self.ym = self.along_y[0], self.along_y[-1]
        self.zp, self.zm = self.along_z[0], self.along_z[-1]

    def at(self, z, y, c, x):
        return ((z * NY + y) * 2 + c, x)

    def enter(self):
        barrier = pltpu.get_barrier_semaphore()
        partners = [self.twin, self.cross] + self.along_x + self.along_y + self.along_z
        for partner in partners:
            pl.semaphore_signal(barrier, inc=1, device_id=partner, device_id_type=MESH)
        pl.semaphore_wait(barrier, len(partners))

    def group(self, copies, whole):
        send_sem, recv_sem = self.send_sem.at[self.used], self.recv_sem.at[self.used]
        self.used += 1
        for src, dst, device in copies:
            pltpu.make_async_remote_copy(
                src_ref=src, dst_ref=dst, send_sem=send_sem, recv_sem=recv_sem, device_id=device, device_id_type=MESH
            ).start()
        self.sent.append(pltpu.make_async_copy(whole, whole, send_sem))
        return pltpu.make_async_copy(whole, whole, recv_sem)

    def open(self):
        self.used += 1
        return self.used - 1

    def put(self, which, src, dst, device):
        pltpu.make_async_remote_copy(
            src_ref=src,
            dst_ref=dst,
            send_sem=self.send_sem.at[which],
            recv_sem=self.recv_sem.at[which],
            device_id=device,
            device_id_type=MESH,
        ).start()

    def close(self, which, whole):
        self.sent.append(pltpu.make_async_copy(whole, whole, self.send_sem.at[which]))
        return pltpu.make_async_copy(whole, whole, self.recv_sem.at[which])

    def send(self, src, dst, device):
        return self.group([(src, dst, device)], dst)

    def same(self, ref, device):
        return self.send(ref, ref, device)

    def finish(self):
        assert self.used == self.send_sem.shape[0], self.used
        for copy in self.sent:
            copy.wait()


def arrive(*copies):
    for copy in copies:
        copy.wait()


class MpSum:
    def __init__(self, net, part, landed):
        self.net, self.part, self.landed = net, part, landed
        self.copy = net.group(
            [(part.at[mod(net.x + d, NX)], landed.at[d - 1], net.along_x[d - 1]) for d in range(1, NX)], landed
        )

    def total(self):
        arrive(self.copy)
        total = self.part[self.net.x].astype(F32)
        for d in range(NX - 1):
            total = total + self.landed[d].astype(F32)
        return total


def rows_of_owner(full, owner, lanes, first=0, last=NZ):
    return [full.at[at, lax.rem(owner - at + NZ, NX), :, lanes] for at in range(first, last)]


def give(net, full, lanes, rows):
    for at in range(NZ):
        full[at, lax.rem(net.x - at + NZ, NX), :, lanes] = rows[at * 32 : at * 32 + 32]


class MpGather:
    def __init__(self, net, full, lanes):
        blocks = rows_of_owner(full, net.x, lanes)
        self.copy = net.group(
            [(block, block, device) for device in net.along_x for block in blocks],
            full.at[0 : NZ // NX * (NX - 1), :, :, lanes],
        )

    def done(self):
        arrive(self.copy)


class MpRing:
    def __init__(self, net, full, lanes):
        self.net, self.full, self.lanes = net, full, lanes
        blocks = rows_of_owner(full, net.x, lanes)
        self.copy = net.group(
            [(block, block, device) for device in (net.xp, net.xm) for block in blocks],
            full.at[0 : NZ // 2, :, :, lanes],
        )

    def pass_on(self):
        net = self.net
        arrive(self.copy)
        left = rows_of_owner(self.full, mod(net.x - 1, NX), self.lanes, 0, NZ // 2)
        right = rows_of_owner(self.full, mod(net.x + 1, NX), self.lanes, NZ // 2, NZ)
        self.copy = net.group(
            [(block, block, net.xp) for block in left] + [(block, block, net.xm) for block in right],
            self.full.at[0 : NZ // NX, :, :, self.lanes],
        )

    def done(self):
        arrive(self.copy)


def chain(net, block, from_left, from_right):
    hops, half = NZ // 2, AW // 2
    far = mod(net.z + hops, NZ)
    copy = net.group(
        [
            (block(far, 0, half), from_left.at[0, ..., 0:half], net.zp),
            (block(far, half, AW), from_right.at[0, ..., half:AW], net.zm),
        ],
        from_left.at[0],
    )
    yield
    for step in range(1, hops):
        right, left = mod(net.z + hops - step, NZ), mod(net.z - hops + step, NZ)
        arrive(copy)
        for at, landed, (lo, hi) in ((right, from_left, (0, half)), (left, from_right, (half, AW))):
            if step > 1:
                lo, hi = 0, AW
            target = block(at, lo, hi)
            target[...] = (target[...].astype(F32) + landed[step - 1, ..., lo:hi].astype(F32)).astype(BF16)
        copy = net.group(
            [
                (block(right, 0, AW), from_left.at[step], net.zp),
                (block(left, 0, AW), from_right.at[step], net.zm),
            ],
            from_left.at[0:2],
        )
        yield
    arrive(copy)


class SeqSum:
    def __init__(self, net, bufs, out, product, order):
        self.net, self.out, self.product, self.order = net, out, product, order
        self.part, self.qa, self.qb, self.azl, self.azr, self.ayl, self.byl, self.bzl = bufs
        self.along_z_b = net.open()
        self.ring = chain(net, lambda t, lo, hi: self.part.at[t, :, :, lo:hi], self.azl, self.azr)
        self.along_y_b = []
        self.steps = self.finish()

    def places(self, k):
        pair = self.order[k]
        both = (2 * pair, 2 * pair + 1)
        return both, both if k < 3 else (2 * pair + 1 - lax.rem(self.net.z, 2),)

    def at_z(self, z):
        return self.net.at(z, self.net.y, self.net.c, self.net.x)

    def multiply(self):
        for half in range(2):
            pairs = self.order[2 * half : 2 * half + 2]
            rows = self.product(pairs)
            for i, pair in enumerate(pairs):
                for place in range(2):
                    for y in range(NY):
                        at = ((i * 2 + place) * NY + y) * CAP
                        self.part[2 * pair + place, y] = rows[at : at + CAP].astype(BF16)
                self.send(2 * half + i)
            if half == 0:
                self.pass_on()

    def send(self, k):
        net, part = self.net, self.part
        rows = pl.ds(2 * self.order[k], 2)
        copies = [
            (part.at[rows, mod(net.y + d, NY), :, AW:QD], self.byl.at[d - 1, rows], net.along_y[d - 1])
            for d in range(1, NY)
        ]
        self.along_y_b.append(net.group(copies, self.byl.at[:, 0:2]))

    def sum_y(self, k):
        net = self.net
        arrive(self.along_y_b[k])
        both, others = self.places(k)
        for z in both:
            total = self.part[z, net.y, :, AW:QD].astype(F32)
            for d in range(NY - 1):
                total = total + self.byl[d, z].astype(F32)
            self.qb[z] = total.astype(BF16)
        for z in others:
            net.put(self.along_z_b, self.qb.at[z], self.bzl.at[net.z], self.at_z(z))

    def pass_on(self):
        next(self.ring, None)

    def turn(self):
        return next(self.steps, None) is not None

    def finish(self):
        net = self.net
        self.pass_on()
        self.sum_y(0)
        self.pass_on()
        self.sum_y(1)
        self.sum_y(2)
        self.pass_on()
        self.sum_y(3)
        for _ in self.ring:
            pass
        last = NZ // 2 - 1
        total = self.part[net.z, :, :, 0:AW].astype(F32) + self.azl[last].astype(F32) + self.azr[last].astype(F32)
        self.qa[...] = total.astype(BF16)
        copy = net.group(
            [(self.qa.at[mod(net.y + d, NY)], self.ayl.at[d - 1], net.along_y[d - 1]) for d in range(1, NY)], self.ayl
        )
        yield True
        arrive(net.close(self.along_z_b, self.bzl.at[0 : NZ - 1]))
        total = self.qb[net.z].astype(F32)
        for d in range(1, NZ):
            total = total + self.bzl[mod(net.z + d, NZ)].astype(F32)
        self.out[:, AW:QD] = total
        arrive(copy)
        total = self.qa[net.y].astype(F32)
        for d in range(NY - 1):
            total = total + self.ayl[d].astype(F32)
        self.out[:, 0:AW] = total


def row_sums(tile, columns):
    small = lax.broadcasted_iota(jnp.int32, tile, 1)
    result = jnp.zeros(tile, F32)
    for at, product in enumerate(columns):
        result = jnp.where(small == at, jnp.sum(product, axis=-1, keepdims=True), result)
    return result


def kernel(
    count_ref, pos_ref, res_ref, cot_ref, rw_ref, win_ref, wout_ref,
    fin_out, sel_out,
    send_sem, recv_sem, load_sem, winp, woutp, counts, contrib, from_twin, from_mate, g0, g1,
    pr, prl, pd, pdl, proj, dj, mixed, datt, dproj, winp2, woutp2, mixed2, dproj2, qn, kn, dkey_n, dvalues,
    delta, dnormed, stats, fin, *bufs,
):
    net = Net(send_sem, recv_sem)
    x, y, z, c = net.x, net.y, net.z, net.c
    loads = (
        pltpu.make_async_copy(win_ref, winp.at[0:WIN], load_sem.at[0]),
        pltpu.make_async_copy(wout_ref.at[HS:WOUT], woutp.at[0:FFD], load_sem.at[1]),
        pltpu.make_async_copy(wout_ref.at[0:HS], woutp.at[256:WOUTP], load_sem.at[2]),
    )
    for load in loads:
        load.start()
    net.enter()

    counts[0] = jnp.zeros((8, 128), jnp.int32) + count_ref[...]
    arrive(net.send(counts.at[0], counts.at[1], net.twin))
    n_slots = pos_ref.shape[1]
    mine, twins = counts[0, 0:1, 0:n_slots], counts[1, 0:1, 0:n_slots]
    before = twins * c + (4 * CAP - mine - twins) * net.upper
    row = lax.broadcasted_iota(jnp.int32, (4 * CAP, n_slots), 0)
    slot = lax.broadcasted_iota(jnp.int32, (4 * CAP, n_slots), 1)
    place_of = jnp.where(row - slot == before, F32(1.0), F32(0.0)).astype(BF16)
    token = lax.broadcasted_iota(jnp.int32, (128, n_slots), 0)
    slot = lax.broadcasted_iota(jnp.int32, (128, n_slots), 1)
    token_of = jnp.where((token == pos_ref[...]) & (slot < mine), F32(1.0), F32(0.0)).astype(BF16)
    sel = dot_nt(place_of, token_of).astype(BF16)
    sel_out[...] = sel

    copies = []
    for which, source in enumerate((res_ref, cot_ref)):
        rows = dot_nn(sel, source[...]).astype(BF16)
        for chip in range(2):
            for core in range(2):
                at = (chip * 2 + core) * CAP
                contrib[which, core, chip] = rows[at : at + CAP]
        copies.append(net.send(contrib.at[which, net.o], from_twin.at[which], net.twin))
    for which in range(2):
        arrive(copies[which])
        contrib[which, c] = (contrib[which, c].astype(F32) + from_twin[which].astype(F32)).astype(BF16)
        if which == 0:
            r_copy = net.send(contrib.at[0, c], from_mate.at[0:2], net.mate)
        else:
            d_copy = net.send(contrib.at[1, c, 1 - net.upper], from_mate.at[2], net.mate)
    mine_q = lax.div(y, 2)
    arrive(r_copy)
    for place in range(2):
        g0[z, 2 * mine_q + place, c] = (
            contrib[0, c, place].astype(F32) + from_mate[place].astype(F32)
        ).astype(BF16)

    def both_ways(step, g, ys, few):
        near, far = mod(z - step + 1, NZ), mod(z + step - 1, NZ)
        if step < 4:
            right, left = g.at[near, ys, c], g.at[far, ys, c]
            whole = g.at[0:2, few, 0]
        else:
            right, left = g.at[near, ys, c, :, 0:HALF], g.at[far, ys, c, :, HALF:QD]
            whole = g.at[0, few, 0]
        return net.group([(right, right, net.zp), (left, left, net.zm)], whole)

    def r_ring(step, q):
        return both_ways(step, g0, pl.ds(2 * q, 2), slice(0, 2))

    def d_ring(step):
        return both_ways(step, g1, y, 0)

    def d_out(*ds):
        result = []
        for d in ds:
            block = g1.at[mod(z + d, NZ), y, c]
            result.append((d, net.group([(block, block, device) for device in net.along_y], g1.at[0, 0:3, 0])))
        return result

    def d_twin(items):
        result = []
        for d, copy in items:
            arrive(copy)
            result.append(net.same(g1.at[mod(z + d, NZ), :, c], net.twin))
        return result

    def r_twin(*ds):
        return [net.same(g0.at[mod(z + d, NZ), :, c], net.twin) for d in ds]

    lane = lax.broadcasted_iota(jnp.int32, (BLK, 128), 1)

    def rows_at(g, ds):
        rows = [g[mod(z + d, NZ)].reshape(BLK // 2, QD) for d in ds]
        return rows[0] if len(ds) == 1 else jnp.concatenate(rows, axis=0)

    def hand_out(part, ds, result, columns):
        for i, d in enumerate(ds):
            at = mod(z + d, NZ)
            for row in range(NY):
                owner = lax.rem(at + row, NX)
                part[at, owner, :, columns] = result[(i * NY + row) * 32 : (i * NY + row) * 32 + 32]

    def in_stage(*ds):
        rows = rows_at(g0, ds)
        result = dot_nt(rows, winp[...])
        rows_f = rows.astype(F32)
        tail = result[:, 768:896]
        at = WIN - 768
        for value in (
            jnp.sum(rows_f * rows_f, axis=-1, keepdims=True),
            jnp.sum(rows_f * rw_ref[...], axis=-1, keepdims=True),
        ):
            for _ in range(3):
                rounded = value.astype(BF16).astype(F32)
                tail = jnp.where(lane[0 : rows.shape[0]] == at, rounded, tail)
                value = value - rounded
                at += 1
        hand_out(pr, ds, result[:, 0:768].astype(BF16), slice(0, 768))
        hand_out(pr, ds, tail.astype(BF16), slice(768, WINP))
        return [(mod(z + d, NZ), MpSum(net, pr.at[mod(z + d, NZ)], prl.at[mod(z + d, NZ)])) for d in ds]

    def back_stage(*ds):
        hand_out(pd, ds, dot_nt(rows_at(g1, ds), woutp[...]).astype(BF16), slice(0, WOUTP))
        return [(mod(z + d, NZ), MpSum(net, pd.at[mod(z + d, NZ)], pdl.at[mod(z + d, NZ)])) for d in ds]

    def collect(target, items):
        for at, part in items:
            target[at] = part.total()

    def add_up(value, first, last):
        lanes = lane[0 : value.shape[0]]
        return jnp.sum(jnp.where((lanes >= first) & (lanes < last), value, 0.0), axis=-1, keepdims=True)

    def scale_of(tail):
        at = WIN - 768
        return lax.rsqrt(add_up(tail, at, at + 3) / D + 1e-05)

    def project(items):
        copies = []
        for at, part in items:
            total = part.total()
            proj[at] = total
            scale = scale_of(total[:, 768:896])
            row = lax.rem(x - at + NZ, NX)
            gate_up = total[:, 384:896] * scale
            gate_in = gate_up[:, 0:FFD]
            hidden = (gate_in * jax.nn.sigmoid(gate_in) * gate_up[:, FFD : 2 * FFD]).astype(BF16)
            mixed[at, row, :, 0:HID] = (total[:, 0:HID] * scale).astype(BF16)
            mixed[at, row, :, HID:ATT] = jnp.concatenate([hidden, jnp.zeros((32, 256 - FFD), BF16)], axis=-1)
            block = mixed.at[at, row, :, 0:ATT]
            copies.append(
                net.group([(block, block, device) for device in net.along_x], mixed.at[at, 0 : NX - 1, :, 0:ATT])
            )
        return copies

    def weights_out(quarter):
        rows = slice(quarter * WINP // 4, (quarter + 1) * WINP // 4)
        return net.send(winp.at[rows], winp2.at[rows], net.twin)

    other_q = 1 - mine_q
    p_ring = r_ring(1, mine_q)
    r_copy = net.same(g0.at[z, pl.ds(2 * mine_q, 2), c], net.beyond)
    arrive(d_copy)
    g1[z, y, c] = (contrib[1, c, net.upper].astype(F32) + from_mate[2].astype(F32)).astype(BF16)
    g_ring = d_ring(1)
    d_0 = d_out(0)
    rows = g0[z, y, c].astype(F32)
    stats[0, 3] = row_sums((CAP, 128), (rows * rows, rows * rw_ref[...]))

    def stats_out(which):
        return net.group(
            [(stats.at[which, 3], stats.at[which, d], net.along_x[d]) for d in range(3)], stats.at[which, 0:3]
        )

    first_stats = stats_out(0)
    winp[WIN:WINP] = jnp.zeros((WINP - WIN, QD), BF16)
    woutp[FFD:256] = jnp.zeros((256 - FFD, QD), BF16)
    for load in loads:
        load.wait()
    arrive(r_copy)
    q_ring = r_ring(1, other_q)
    r_0 = r_twin(0)
    arrive(g_ring)
    g_ring = d_ring(2)
    d_1 = d_out(1, -1)
    arrive(p_ring)
    p_ring = r_ring(2, mine_q)
    arrive(*r_0)
    in_0 = in_stage(0)
    twin_weights = [net.send(woutp, woutp2, net.twin)]
    arrive(q_ring)
    q_ring = r_ring(2, other_q)
    r_1 = r_twin(1, -1)
    arrive(g_ring)
    g_ring = d_ring(3)
    d_2 = d_out(2, -2)
    d_0 = d_twin(d_0)
    arrive(p_ring)
    p_ring = r_ring(3, mine_q)
    arrive(*r_1)
    in_1 = in_stage(1, -1)
    twin_weights.append(weights_out(0))
    arrive(q_ring)
    q_ring = r_ring(3, other_q)
    r_2 = r_twin(2, -2)
    d_1 = d_twin(d_1)
    arrive(g_ring)
    g_ring = d_ring(4)
    d_3 = d_out(3, -3)
    arrive(p_ring)
    p_ring = r_ring(4, mine_q)
    arrive(*r_2)
    in_2 = in_stage(2, -2)
    twin_weights.append(weights_out(1))
    arrive(q_ring)
    q_ring = r_ring(4, other_q)
    r_3 = r_twin(3, -3)
    d_2 = d_twin(d_2)
    arrive(*d_0)
    back_0 = back_stage(0)
    arrive(g_ring)
    d_4 = d_out(4)
    arrive(*r_3)
    in_3 = in_stage(3, -3)
    twin_weights.append(weights_out(2))
    arrive(p_ring, q_ring)
    r_4 = r_twin(4)
    mixed_rows = project(in_0) + project(in_1)
    arrive(*r_4)
    in_4 = in_stage(4)
    twin_weights.append(weights_out(3))
    arrive(*d_1)
    back_1 = back_stage(1, -1)
    d_3 = d_twin(d_3)
    mixed_rows += project(in_2)
    mixed_rows += project(in_3)
    arrive(*d_2)
    back_2 = back_stage(2, -2)
    d_4 = d_twin(d_4)
    mixed_rows += project(in_4)

    arrive(*d_3)
    back_3 = back_stage(3, -3)
    arrive(*d_4)
    back_4 = back_stage(4)
    tail = proj[:, :, 768:896].reshape(BLK, 128)
    in_scale = scale_of(tail)
    gate = jax.nn.sigmoid(add_up(tail, WIN - 765, WIN - 762))
    gate_up = proj[:, :, 384:896].reshape(BLK, 512) * in_scale
    gate_in = gate_up[:, 0:FFD]
    up_in = gate_up[:, FFD : 2 * FFD]
    sigma = jax.nn.sigmoid(gate_in)
    arrive(*mixed_rows)

    query = mixed[:, :, :, 0:HS].reshape(ROWS, HS).astype(F32)
    keyraw = mixed[:, :, :, HS : 2 * HS].reshape(ROWS, HS).astype(F32)
    vals = mixed[:, :, :, 2 * HS : 3 * HS].reshape(ROWS, HS)
    query_scale = lax.rsqrt(jnp.mean(query * query, axis=-1, keepdims=True) + 1e-06)
    key_scale = lax.rsqrt(jnp.mean(keyraw * keyraw, axis=-1, keepdims=True) + 1e-06)
    qn[...] = (query * query_scale).astype(BF16)
    kn[...] = (keyraw * key_scale).astype(BF16)

    def exp_scores(block):
        first, last = block * BLK, block * BLK + BLK
        raw = dot_nt(qn[first:last], kn[0:last])
        row = lax.broadcasted_iota(jnp.int32, (BLK, 1), 0) + first
        visible = lax.broadcasted_iota(jnp.int32, (1, last), 1) <= row
        return jnp.where(visible, jnp.exp(raw * FACTOR), 0.0)

    inverse = []
    for block in range(4):
        expo = exp_scores(block)
        inverse.append(1.0 / jnp.sum(expo, axis=-1, keepdims=True))
        attended = dot_nn(expo.astype(BF16), vals[0 : block * BLK + BLK]) * inverse[block]
        mixed[2 * block : 2 * block + 2, :, :, ATT:MIX] = attended.astype(BF16).reshape(2, NY, 32, HS)
    own_rows, twin_half = pl.multiple_of(c * CAP, CAP), pl.multiple_of(net.o * CAP, CAP)
    mixed_copy = net.send(mixed.at[:, :, pl.ds(twin_half, CAP), HID:MIX], mixed2, net.twin)

    for items in (back_0, back_1, back_2, back_3, back_4):
        collect(dj, items)
    give(net, datt, slice(0, HS), (dj[:, :, 256:WOUTP].reshape(BLK, HS) * gate).astype(BF16))
    datt_gather = MpGather(net, datt, slice(0, HS))
    dhidden = dj[:, :, 0:256].reshape(BLK, 256)[:, 0:FFD] * gate
    dup = (dhidden * gate_in * sigma).astype(BF16)
    dgate_in = (dhidden * up_in * sigma * (1.0 + gate_in * (1.0 - sigma))).astype(BF16)
    give(net, dproj, slice(384, 896), jnp.concatenate([dgate_in, dup, jnp.zeros((BLK, 64), BF16)], axis=-1))
    ff_ring = MpRing(net, dproj, slice(384, WINP))

    def rows_of(full, pairs, lanes, first):
        rows = [full[pl.ds(2 * pair, 2), :, pl.ds(first, CAP), lanes] for pair in pairs]
        return jnp.concatenate([part.reshape(BLK // 2, part.shape[-1]) for part in rows], axis=0)

    def both_cores(full, lanes, weights, twin_rows, twin_weights, copies):
        def product(pairs):
            own = dot_nn(rows_of(full, pairs, lanes, own_rows), weights[...])
            while copies:
                arrive(copies.pop())
            return own + dot_nn(rows_of(twin_rows, pairs, slice(0, twin_rows.shape[-1]), 0), twin_weights[...])

        return product

    pair = lax.div(z, 2)
    turned = 1 - 2 * lax.rem(z, 2)
    far_first = (mod(pair + 2, 4), mod(pair + turned, 4), mod(pair - turned, 4), pair)
    n_bufs = len(bufs) // 2
    dproj_copies = twin_weights[1:]
    delta_sum = SeqSum(
        net, bufs[:n_bufs], delta,
        both_cores(mixed, slice(HID, MIX), woutp, mixed2, woutp2, [twin_weights[0], mixed_copy]), far_first,
    )
    dnormed_sum = SeqSum(
        net, bufs[n_bufs:], dnormed,
        both_cores(dproj, slice(0, WINP), winp, dproj2, winp2, dproj_copies), far_first,
    )
    delta_sum.multiply()
    ff_ring.pass_on()
    datt_gather.done()
    delta_sum.pass_on()

    def norm_back(values, scale, grads):
        return scale * grads - values * scale**3 * jnp.mean(grads * values, axis=-1, keepdims=True)

    for block in range(3, -1, -1):
        first, last = block * BLK, block * BLK + BLK
        prob = exp_scores(block) * inverse[block]
        dout = datt[2 * block : 2 * block + 2].reshape(BLK, HS)
        dprob = dot_nt(dout, vals[0:last])
        inner = jnp.sum(prob * dprob, axis=-1, keepdims=True)
        dscore = (prob * (dprob - inner)).astype(BF16)
        dquery_n = dot_nn(dscore, kn[0:last]) * FACTOR
        dquery = norm_back(query[first:last], query_scale[first:last], dquery_n)
        dproj[2 * block : 2 * block + 2, :, :, 0:HS] = dquery.astype(BF16).reshape(2, NY, 32, HS)
        dkey_part = dot_tn(dscore, qn[first:last])
        dvalue_part = dot_tn(prob.astype(BF16), dout)
        if block == 3:
            dkey_n[...] = dkey_part
            dvalues[...] = dvalue_part
        else:
            dkey_n[0:last] = dkey_n[0:last] + dkey_part
            dvalues[0:last] = dvalues[0:last] + dvalue_part
        if block == 3 or block == 1:
            delta_sum.pass_on()
    dkey = norm_back(keyraw, key_scale, dkey_n[...] * FACTOR)
    dproj[:, :, :, HS : 2 * HS] = dkey.astype(BF16).reshape(NZ, NY, 32, HS)
    dproj[:, :, :, 2 * HS : 3 * HS] = dvalues[...].astype(BF16).reshape(NZ, NY, 32, HS)
    delta_sum.turn()
    ff_ring.done()
    dproj_copies.append(net.send(dproj.at[:, :, pl.ds(twin_half, CAP)], dproj2, net.twin))
    dnormed_sum.multiply()
    while delta_sum.turn():
        pass

    rows = g0[z, y, c].astype(F32)
    grads = g1[z, y, c].astype(F32)
    delta_b = delta[...].astype(BF16).astype(F32)
    small = lax.broadcasted_iota(jnp.int32, (CAP, 128), 1)

    def summed(which):
        return stats[which, 0] + stats[which, 1] + stats[which, 2] + stats[which, 3]

    def pick(tile, at):
        return jnp.sum(jnp.where(small == at, tile, 0.0), axis=-1, keepdims=True)

    def spread(which):
        own = fin.at[which, net.w]
        return net.group([(own, own, device) for device in (net.mate, net.cross, net.twin)], fin.at[which, 0:3])

    stats[1, 3] = row_sums((CAP, 128), (grads * delta_b,))
    arrive(first_stats)
    tile = summed(0)
    in_scale = lax.rsqrt(pick(tile, 0) / D + 1e-05)
    gate = jax.nn.sigmoid(pick(tile, 1))
    fin[0, net.w] = (rows + gate * delta_b).astype(BF16)
    gate_stats = stats_out(1)
    first_rows = spread(0)
    while dnormed_sum.turn():
        pass
    dn = dnormed[...]
    stats[2, 3] = row_sums((CAP, 128), (dn * rows,))
    last_stats = stats_out(2)
    arrive(gate_stats)
    dlogit = pick(summed(1), 0) * gate * (1.0 - gate)
    base = grads + dlogit * rw_ref[...]
    dn = in_scale * dn
    arrive(first_rows, last_stats)
    dinput = (dn - rows * in_scale**3 * (pick(summed(2), 0) / D)).astype(BF16).astype(F32)
    fin[1, net.w] = (base + dinput).astype(BF16)
    last_rows = spread(1)
    fin_out[0] = fin[0]
    arrive(last_rows)
    fin_out[1] = fin[1]
    net.finish()


def place_kernel(sel_ref, fin_ref, res_ref, cot_ref, output_ref, grad_ref):
    sel = sel_ref[...]
    chosen = dot_tn(sel, jnp.ones((4 * CAP, 128), BF16))[:, 0:1] > 0.5
    for which, (source, target) in enumerate(((res_ref, output_ref), (cot_ref, grad_ref))):
        back = dot_tn(sel, fin_ref[which]).astype(BF16)
        target[...] = jnp.where(chosen, back, source[...])


def sum_scratch():
    return [
        pltpu.VMEM((NZ, NY, CAP, QD), BF16),
        pltpu.VMEM((NY, CAP, AW), BF16),
        pltpu.VMEM((NZ, CAP, BW), BF16),
        pltpu.VMEM((NZ // 2, NY, CAP, AW), BF16),
        pltpu.VMEM((NZ // 2, NY, CAP, AW), BF16),
        pltpu.VMEM((NY - 1, CAP, AW), BF16),
        pltpu.VMEM((NY - 1, NZ, CAP, BW), BF16),
        pltpu.VMEM((NZ, CAP, BW), BF16),
    ]


def local(residual, chosen_pos, chosen_count, router_weight, weight_in, weight_out, cotangent):
    n_sem = 101
    scratch = [
        pltpu.SemaphoreType.DMA((n_sem,)),
        pltpu.SemaphoreType.DMA((n_sem,)),
        pltpu.SemaphoreType.DMA((3,)),
        pltpu.VMEM((WINP, QD), BF16),
        pltpu.VMEM((WOUTP, QD), BF16),
        pltpu.VMEM((2, 8, 128), jnp.int32),
        pltpu.VMEM((2, 2, 2, CAP, QD), BF16),
        pltpu.VMEM((2, 2, CAP, QD), BF16),
        pltpu.VMEM((3, CAP, QD), BF16),
        pltpu.VMEM((NZ, NY, 2, CAP, QD), BF16),
        pltpu.VMEM((NZ, NY, 2, CAP, QD), BF16),
        pltpu.VMEM((NZ, NX, 32, WINP), BF16),
        pltpu.VMEM((NZ, NX - 1, 32, WINP), BF16),
        pltpu.VMEM((NZ, NX, 32, WOUTP), BF16),
        pltpu.VMEM((NZ, NX - 1, 32, WOUTP), BF16),
        pltpu.VMEM((NZ, 32, WINP), F32),
        pltpu.VMEM((NZ, 32, WOUTP), F32),
        pltpu.VMEM((NZ, NY, 32, MIX), BF16),
        pltpu.VMEM((NZ, NY, 32, HS), BF16),
        pltpu.VMEM((NZ, NY, 32, WINP), BF16),
        pltpu.VMEM((WINP, QD), BF16),
        pltpu.VMEM((WOUTP, QD), BF16),
        pltpu.VMEM((NZ, NY, CAP, WOUTP), BF16),
        pltpu.VMEM((NZ, NY, CAP, WINP), BF16),
        pltpu.VMEM((ROWS, HS), BF16),
        pltpu.VMEM((ROWS, HS), BF16),
        pltpu.VMEM((ROWS, HS), F32),
        pltpu.VMEM((ROWS, HS), F32),
        pltpu.VMEM((CAP, QD), F32),
        pltpu.VMEM((CAP, QD), F32),
        pltpu.VMEM((3, 4, CAP, 128), F32),
        pltpu.VMEM((2, 4, CAP, QD), BF16),
    ] + sum_scratch() + sum_scratch()
    vmem = pl.BlockSpec(memory_space=pltpu.VMEM)
    anywhere = pl.BlockSpec(memory_space=pl.ANY)
    fin, sel = pl.pallas_call(
        kernel,
        out_shape=[
            jax.ShapeDtypeStruct((2, 4, CAP, QD), BF16),
            jax.ShapeDtypeStruct((4 * CAP, residual.shape[0]), BF16),
        ],
        in_specs=[vmem] * 5 + [anywhere] * 2,
        out_specs=[vmem] * 2,
        scratch_shapes=scratch,
        compiler_params=pltpu.CompilerParams(
            collective_id=0, has_side_effects=True, vmem_limit_bytes=62 * 1024 * 1024
        ),
        cost_estimate=pl.CostEstimate(flops=10**10, bytes_accessed=10**7, transcendentals=10**6),
    )(
        chosen_count[None, :], chosen_pos[None, :], residual, cotangent, router_weight[None, :],
        weight_in.T, weight_out,
    )
    fin = fin.reshape(2, 4 * CAP, QD)
    n_steps = 1
    tokens = residual.shape[0]
    columns = QD // n_steps
    block = pl.BlockSpec((tokens, columns), lambda i: (0, i))
    return pl.pallas_call(
        place_kernel,
        grid=(n_steps,),
        out_shape=[jax.ShapeDtypeStruct(residual.shape, BF16)] * 2,
        in_specs=[
            pl.BlockSpec((4 * CAP, tokens), lambda i: (0, 0)),
            pl.BlockSpec((2, 4 * CAP, columns), lambda i: (0, 0, i)),
            block,
            block,
        ],
        out_specs=[block, block],
    )(sel, fin, residual, cotangent)


def solution(mesh):
    spec = P("seq", "mp")
    return jax.shard_map(
        local,
        mesh=mesh,
        in_specs=(spec, P("seq"), P("seq"), P("mp"), P("mp", "seq"), spec, spec),
        out_specs=(spec, spec),
        check_vma=False,
    )
```

```python
import jax
import jax.numpy as jnp
from jax import lax
from jax.experimental import pallas as pl
from jax.experimental.pallas import tpu as pltpu
from jax.sharding import PartitionSpec as P

MESH = pl.DeviceIdType.MESH
D = 8192
HS = 128
NZ, NY, NX = 8, 4, 4
CAP = 16
QD = D // NX
FFD = 224
WIN = 3 * HS + 2 * FFD
WINP = 896
WOUT = HS + FFD
WOUTP = 384
ROWS = 1024
BLK = 256
HALF = QD // 2
AW = 512
BW = QD - AW
MIX = 2 * WOUTP
HID = 3 * HS
ATT = HID + 256
F32 = jnp.float32
BF16 = jnp.bfloat16
FACTOR = HS ** (-0.5)


def mod(value, n):
    return lax.rem(value + n, n)


def dot_nn(a, b):
    return jnp.dot(a, b, preferred_element_type=F32)


def dot_nt(a, b):
    return lax.dot_general(a, b, (((1,), (1,)), ((), ())), preferred_element_type=F32)


def dot_tn(a, b):
    return lax.dot_general(a, b, (((0,), (0,)), ((), ())), preferred_element_type=F32)


class Net:
    def __init__(self, send_sem, recv_sem):
        self.send_sem, self.recv_sem = send_sem, recv_sem
        self.used = 0
        self.sent = []
        seq = lax.axis_index("seq")
        x = self.x = lax.axis_index("mp")
        z = self.z = lax.div(seq, NY * 2)
        y = self.y = lax.rem(lax.div(seq, 2), NY)
        c = self.c = lax.rem(seq, 2)
        self.o = 1 - c
        self.upper = lax.rem(y, 2)
        self.w = self.upper * 2 + c
        yw = y + 1 - 2 * self.upper
        yo = mod(y - 1 + 2 * self.upper, NY)
        self.twin = self.at(z, y, self.o, x)
        self.mate = self.at(z, yw, c, x)
        self.cross = self.at(z, yw, self.o, x)
        self.beyond = self.at(z, yo, c, x)
        self.along_x = [self.at(z, y, c, mod(x + d, NX)) for d in range(1, NX)]
        self.along_y = [self.at(z, mod(y + d, NY), c, x) for d in range(1, NY)]
        self.along_z = [self.at(mod(z + d, NZ), y, c, x) for d in range(1, NZ)]
        self.xp, self.xm = self.along_x[0], self.along_x[-1]
        self.yp, self.ym = self.along_y[0], self.along_y[-1]
        self.zp, self.zm = self.along_z[0], self.along_z[-1]

    def at(self, z, y, c, x):
        return ((z * NY + y) * 2 + c, x)

    def enter(self):
        barrier = pltpu.get_barrier_semaphore()
        partners = [self.twin, self.cross] + self.along_x + self.along_y + self.along_z
        for partner in partners:
            pl.semaphore_signal(barrier, inc=1, device_id=partner, device_id_type=MESH)
        pl.semaphore_wait(barrier, len(partners))

    def group(self, copies, whole):
        send_sem, recv_sem = self.send_sem.at[self.used], self.recv_sem.at[self.used]
        self.used += 1
        for src, dst, device in copies:
            pltpu.make_async_remote_copy(
                src_ref=src, dst_ref=dst, send_sem=send_sem, recv_sem=recv_sem, device_id=device, device_id_type=MESH
            ).start()
        self.sent.append(pltpu.make_async_copy(whole, whole, send_sem))
        return pltpu.make_async_copy(whole, whole, recv_sem)

    def open(self):
        self.used += 1
        return self.used - 1

    def put(self, which, src, dst, device):
        pltpu.make_async_remote_copy(
            src_ref=src,
            dst_ref=dst,
            send_sem=self.send_sem.at[which],
            recv_sem=self.recv_sem.at[which],
            device_id=device,
            device_id_type=MESH,
        ).start()

    def close(self, which, whole):
        self.sent.append(pltpu.make_async_copy(whole, whole, self.send_sem.at[which]))
        return pltpu.make_async_copy(whole, whole, self.recv_sem.at[which])

    def send(self, src, dst, device):
        return self.group([(src, dst, device)], dst)

    def same(self, ref, device):
        return self.send(ref, ref, device)

    def finish(self):
        assert self.used == self.send_sem.shape[0], self.used
        for copy in self.sent:
            copy.wait()


def arrive(*copies):
    for copy in copies:
        copy.wait()


class MpSum:
    def __init__(self, net, part, landed):
        self.net, self.part, self.landed = net, part, landed
        self.copy = net.group(
            [(part.at[mod(net.x + d, NX)], landed.at[d - 1], net.along_x[d - 1]) for d in range(1, NX)], landed
        )

    def total(self):
        arrive(self.copy)
        total = self.part[self.net.x].astype(F32)
        for d in range(NX - 1):
            total = total + self.landed[d].astype(F32)
        return total


def rows_of_owner(full, owner, lanes, first=0, last=NZ):
    return [full.at[at, lax.rem(owner - at + NZ, NX), :, lanes] for at in range(first, last)]


def give(net, full, lanes, rows):
    for at in range(NZ):
        full[at, lax.rem(net.x - at + NZ, NX), :, lanes] = rows[at * 32 : at * 32 + 32]


class MpGather:
    def __init__(self, net, full, lanes):
        blocks = rows_of_owner(full, net.x, lanes)
        self.copy = net.group(
            [(block, block, device) for device in net.along_x for block in blocks],
            full.at[0 : NZ // NX * (NX - 1), :, :, lanes],
        )

    def done(self):
        arrive(self.copy)


class MpRing:
    def __init__(self, net, full, lanes):
        self.net, self.full, self.lanes = net, full, lanes
        blocks = rows_of_owner(full, net.x, lanes)
        self.copy = net.group(
            [(block, block, device) for device in (net.xp, net.xm) for block in blocks],
            full.at[0 : NZ // 2, :, :, lanes],
        )

    def pass_on(self):
        net = self.net
        arrive(self.copy)
        left = rows_of_owner(self.full, mod(net.x - 1, NX), self.lanes, 0, NZ // 2)
        right = rows_of_owner(self.full, mod(net.x + 1, NX), self.lanes, NZ // 2, NZ)
        self.copy = net.group(
            [(block, block, net.xp) for block in left] + [(block, block, net.xm) for block in right],
            self.full.at[0 : NZ // NX, :, :, self.lanes],
        )

    def done(self):
        arrive(self.copy)


class SeqSum:
    def __init__(self, net, bufs, out, product, order):
        self.net, self.out, self.product, self.order = net, out, product, order
        self.part, self.qa, self.qb, self.azl, self.ayl, self.byl, self.bzl = bufs
        self.along_z_a, self.along_z_b = net.open(), net.open()
        self.along_y_b = []
        self.steps = self.finish()

    def places(self, k):
        pair = self.order[k]
        both = (2 * pair, 2 * pair + 1)
        return both, both if k < 3 else (2 * pair + 1 - lax.rem(self.net.z, 2),)

    def at_z(self, z):
        return self.net.at(z, self.net.y, self.net.c, self.net.x)

    def multiply(self):
        for half in range(2):
            pairs = self.order[2 * half : 2 * half + 2]
            rows = self.product(pairs)
            for i, pair in enumerate(pairs):
                for place in range(2):
                    for y in range(NY):
                        at = ((i * 2 + place) * NY + y) * CAP
                        self.part[2 * pair + place, y] = rows[at : at + CAP].astype(BF16)
                self.send(2 * half + i)

    def send(self, k):
        net, part = self.net, self.part
        for z in self.places(k)[1]:
            net.put(self.along_z_a, part.at[z, :, :, 0:AW], self.azl.at[net.z], self.at_z(z))
        rows = pl.ds(2 * self.order[k], 2)
        copies = [
            (part.at[rows, mod(net.y + d, NY), :, AW:QD], self.byl.at[d - 1, rows], net.along_y[d - 1])
            for d in range(1, NY)
        ]
        self.along_y_b.append(net.group(copies, self.byl.at[:, 0:2]))

    def sum_y(self, k):
        net = self.net
        arrive(self.along_y_b[k])
        both, others = self.places(k)
        for z in both:
            total = self.part[z, net.y, :, AW:QD].astype(F32)
            for d in range(NY - 1):
                total = total + self.byl[d, z].astype(F32)
            self.qb[z] = total.astype(BF16)
        for z in others:
            net.put(self.along_z_b, self.qb.at[z], self.bzl.at[net.z], self.at_z(z))

    def turn(self):
        return next(self.steps, None) is not None

    def finish(self):
        net = self.net
        for k in range(4):
            self.sum_y(k)
        arrive(net.close(self.along_z_a, self.azl.at[0 : NZ - 1]))
        total = self.part[net.z, :, :, 0:AW].astype(F32)
        for d in range(1, NZ):
            total = total + self.azl[mod(net.z + d, NZ)].astype(F32)
        self.qa[...] = total.astype(BF16)
        copy = net.group(
            [(self.qa.at[mod(net.y + d, NY)], self.ayl.at[d - 1], net.along_y[d - 1]) for d in range(1, NY)], self.ayl
        )
        yield True
        arrive(net.close(self.along_z_b, self.bzl.at[0 : NZ - 1]))
        total = self.qb[net.z].astype(F32)
        for d in range(1, NZ):
            total = total + self.bzl[mod(net.z + d, NZ)].astype(F32)
        self.out[:, AW:QD] = total
        arrive(copy)
        total = self.qa[net.y].astype(F32)
        for d in range(NY - 1):
            total = total + self.ayl[d].astype(F32)
        self.out[:, 0:AW] = total


def row_sums(tile, columns):
    small = lax.broadcasted_iota(jnp.int32, tile, 1)
    result = jnp.zeros(tile, F32)
    for at, product in enumerate(columns):
        result = jnp.where(small == at, jnp.sum(product, axis=-1, keepdims=True), result)
    return result


def kernel(
    count_ref, pos_ref, res_ref, cot_ref, rw_ref, win_ref, wout_ref,
    fin_out, sel_out,
    send_sem, recv_sem, load_sem, winp, woutp, counts, contrib, from_twin, from_mate, g0, g1,
    pr, prl, pd, pdl, proj, dj, mixed, datt, dproj, winp2, woutp2, mixed2, dproj2, qn, kn, dkey_n, dvalues,
    delta, dnormed, stats, fin, *bufs,
):
    net = Net(send_sem, recv_sem)
    x, y, z, c = net.x, net.y, net.z, net.c
    loads = (
        pltpu.make_async_copy(win_ref, winp.at[0:WIN], load_sem.at[0]),
        pltpu.make_async_copy(wout_ref.at[HS:WOUT], woutp.at[0:FFD], load_sem.at[1]),
        pltpu.make_async_copy(wout_ref.at[0:HS], woutp.at[256:WOUTP], load_sem.at[2]),
    )
    for load in loads:
        load.start()
    net.enter()

    counts[0] = jnp.zeros((8, 128), jnp.int32) + count_ref[...]
    arrive(net.send(counts.at[0], counts.at[1], net.twin))
    n_slots = pos_ref.shape[1]
    mine, twins = counts[0, 0:1, 0:n_slots], counts[1, 0:1, 0:n_slots]
    before = twins * c + (4 * CAP - mine - twins) * net.upper
    row = lax.broadcasted_iota(jnp.int32, (4 * CAP, n_slots), 0)
    slot = lax.broadcasted_iota(jnp.int32, (4 * CAP, n_slots), 1)
    place_of = jnp.where(row - slot == before, F32(1.0), F32(0.0)).astype(BF16)
    token = lax.broadcasted_iota(jnp.int32, (128, n_slots), 0)
    slot = lax.broadcasted_iota(jnp.int32, (128, n_slots), 1)
    token_of = jnp.where((token == pos_ref[...]) & (slot < mine), F32(1.0), F32(0.0)).astype(BF16)
    sel = dot_nt(place_of, token_of).astype(BF16)
    sel_out[...] = sel

    copies = []
    for which, source in enumerate((res_ref, cot_ref)):
        rows = dot_nn(sel, source[...]).astype(BF16)
        for chip in range(2):
            for core in range(2):
                at = (chip * 2 + core) * CAP
                contrib[which, core, chip] = rows[at : at + CAP]
        copies.append(net.send(contrib.at[which, net.o], from_twin.at[which], net.twin))
    for which in range(2):
        arrive(copies[which])
        contrib[which, c] = (contrib[which, c].astype(F32) + from_twin[which].astype(F32)).astype(BF16)
        if which == 0:
            r_copy = net.send(contrib.at[0, c], from_mate.at[0:2], net.mate)
        else:
            d_copy = net.send(contrib.at[1, c, 1 - net.upper], from_mate.at[2], net.mate)
    mine_q = lax.div(y, 2)
    arrive(r_copy)
    for place in range(2):
        g0[z, 2 * mine_q + place, c] = (
            contrib[0, c, place].astype(F32) + from_mate[place].astype(F32)
        ).astype(BF16)

    def both_ways(step, g, ys, few):
        near, far = mod(z - step + 1, NZ), mod(z + step - 1, NZ)
        if step < 4:
            right, left = g.at[near, ys, c], g.at[far, ys, c]
            whole = g.at[0:2, few, 0]
        else:
            right, left = g.at[near, ys, c, :, 0:HALF], g.at[far, ys, c, :, HALF:QD]
            whole = g.at[0, few, 0]
        return net.group([(right, right, net.zp), (left, left, net.zm)], whole)

    def r_ring(step, q):
        return both_ways(step, g0, pl.ds(2 * q, 2), slice(0, 2))

    def d_ring(step):
        return both_ways(step, g1, y, 0)

    def d_out(*ds):
        result = []
        for d in ds:
            block = g1.at[mod(z + d, NZ), y, c]
            result.append((d, net.group([(block, block, device) for device in net.along_y], g1.at[0, 0:3, 0])))
        return result

    def d_twin(items):
        result = []
        for d, copy in items:
            arrive(copy)
            result.append(net.same(g1.at[mod(z + d, NZ), :, c], net.twin))
        return result

    def r_twin(*ds):
        return [net.same(g0.at[mod(z + d, NZ), :, c], net.twin) for d in ds]

    lane = lax.broadcasted_iota(jnp.int32, (BLK, 128), 1)

    def rows_at(g, ds):
        rows = [g[mod(z + d, NZ)].reshape(BLK // 2, QD) for d in ds]
        return rows[0] if len(ds) == 1 else jnp.concatenate(rows, axis=0)

    def hand_out(part, ds, result, columns):
        for i, d in enumerate(ds):
            at = mod(z + d, NZ)
            for row in range(NY):
                owner = lax.rem(at + row, NX)
                part[at, owner, :, columns] = result[(i * NY + row) * 32 : (i * NY + row) * 32 + 32]

    def in_stage(*ds):
        rows = rows_at(g0, ds)
        result = dot_nt(rows, winp[...])
        rows_f = rows.astype(F32)
        tail = result[:, 768:896]
        at = WIN - 768
        for value in (
            jnp.sum(rows_f * rows_f, axis=-1, keepdims=True),
            jnp.sum(rows_f * rw_ref[...], axis=-1, keepdims=True),
        ):
            for _ in range(3):
                rounded = value.astype(BF16).astype(F32)
                tail = jnp.where(lane[0 : rows.shape[0]] == at, rounded, tail)
                value = value - rounded
                at += 1
        hand_out(pr, ds, result[:, 0:768].astype(BF16), slice(0, 768))
        hand_out(pr, ds, tail.astype(BF16), slice(768, WINP))
        return [(mod(z + d, NZ), MpSum(net, pr.at[mod(z + d, NZ)], prl.at[mod(z + d, NZ)])) for d in ds]

    def back_stage(*ds):
        hand_out(pd, ds, dot_nt(rows_at(g1, ds), woutp[...]).astype(BF16), slice(0, WOUTP))
        return [(mod(z + d, NZ), MpSum(net, pd.at[mod(z + d, NZ)], pdl.at[mod(z + d, NZ)])) for d in ds]

    def collect(target, items):
        for at, part in items:
            target[at] = part.total()

    def add_up(value, first, last):
        lanes = lane[0 : value.shape[0]]
        return jnp.sum(jnp.where((lanes >= first) & (lanes < last), value, 0.0), axis=-1, keepdims=True)

    def scale_of(tail):
        at = WIN - 768
        return lax.rsqrt(add_up(tail, at, at + 3) / D + 1e-05)

    def project(items):
        copies = []
        for at, part in items:
            total = part.total()
            proj[at] = total
            scale = scale_of(total[:, 768:896])
            row = lax.rem(x - at + NZ, NX)
            gate_up = total[:, 384:896] * scale
            gate_in = gate_up[:, 0:FFD]
            hidden = (gate_in * jax.nn.sigmoid(gate_in) * gate_up[:, FFD : 2 * FFD]).astype(BF16)
            mixed[at, row, :, 0:HID] = (total[:, 0:HID] * scale).astype(BF16)
            mixed[at, row, :, HID:ATT] = jnp.concatenate([hidden, jnp.zeros((32, 256 - FFD), BF16)], axis=-1)
            block = mixed.at[at, row, :, 0:ATT]
            copies.append(
                net.group([(block, block, device) for device in net.along_x], mixed.at[at, 0 : NX - 1, :, 0:ATT])
            )
        return copies

    def weights_out(quarter):
        rows = slice(quarter * WINP // 4, (quarter + 1) * WINP // 4)
        return net.send(winp.at[rows], winp2.at[rows], net.twin)

    other_q = 1 - mine_q
    p_ring = r_ring(1, mine_q)
    r_copy = net.same(g0.at[z, pl.ds(2 * mine_q, 2), c], net.beyond)
    arrive(d_copy)
    g1[z, y, c] = (contrib[1, c, net.upper].astype(F32) + from_mate[2].astype(F32)).astype(BF16)
    g_ring = d_ring(1)
    d_0 = d_out(0)
    rows = g0[z, y, c].astype(F32)
    stats[0, 3] = row_sums((CAP, 128), (rows * rows, rows * rw_ref[...]))

    def stats_out(which):
        return net.group(
            [(stats.at[which, 3], stats.at[which, d], net.along_x[d]) for d in range(3)], stats.at[which, 0:3]
        )

    first_stats = stats_out(0)
    winp[WIN:WINP] = jnp.zeros((WINP - WIN, QD), BF16)
    woutp[FFD:256] = jnp.zeros((256 - FFD, QD), BF16)
    for load in loads:
        load.wait()
    arrive(r_copy)
    q_ring = r_ring(1, other_q)
    r_0 = r_twin(0)
    arrive(g_ring)
    g_ring = d_ring(2)
    d_1 = d_out(1, -1)
    arrive(p_ring)
    p_ring = r_ring(2, mine_q)
    arrive(*r_0)
    in_0 = in_stage(0)
    twin_weights = [net.send(woutp, woutp2, net.twin)]
    arrive(q_ring)
    q_ring = r_ring(2, other_q)
    r_1 = r_twin(1, -1)
    arrive(g_ring)
    g_ring = d_ring(3)
    d_2 = d_out(2, -2)
    d_0 = d_twin(d_0)
    arrive(p_ring)
    p_ring = r_ring(3, mine_q)
    arrive(*r_1)
    in_1 = in_stage(1, -1)
    twin_weights.append(weights_out(0))
    arrive(q_ring)
    q_ring = r_ring(3, other_q)
    r_2 = r_twin(2, -2)
    d_1 = d_twin(d_1)
    arrive(g_ring)
    g_ring = d_ring(4)
    d_3 = d_out(3, -3)
    arrive(p_ring)
    p_ring = r_ring(4, mine_q)
    arrive(*r_2)
    in_2 = in_stage(2, -2)
    twin_weights.append(weights_out(1))
    arrive(q_ring)
    q_ring = r_ring(4, other_q)
    r_3 = r_twin(3, -3)
    d_2 = d_twin(d_2)
    arrive(*d_0)
    back_0 = back_stage(0)
    arrive(g_ring)
    d_4 = d_out(4)
    arrive(*r_3)
    in_3 = in_stage(3, -3)
    twin_weights.append(weights_out(2))
    arrive(p_ring, q_ring)
    r_4 = r_twin(4)
    mixed_rows = project(in_0) + project(in_1)
    arrive(*r_4)
    in_4 = in_stage(4)
    twin_weights.append(weights_out(3))
    arrive(*d_1)
    back_1 = back_stage(1, -1)
    d_3 = d_twin(d_3)
    mixed_rows += project(in_2)
    mixed_rows += project(in_3)
    arrive(*d_2)
    back_2 = back_stage(2, -2)
    d_4 = d_twin(d_4)
    mixed_rows += project(in_4)

    arrive(*d_3)
    back_3 = back_stage(3, -3)
    arrive(*d_4)
    back_4 = back_stage(4)
    tail = proj[:, :, 768:896].reshape(BLK, 128)
    in_scale = scale_of(tail)
    gate = jax.nn.sigmoid(add_up(tail, WIN - 765, WIN - 762))
    gate_up = proj[:, :, 384:896].reshape(BLK, 512) * in_scale
    gate_in = gate_up[:, 0:FFD]
    up_in = gate_up[:, FFD : 2 * FFD]
    sigma = jax.nn.sigmoid(gate_in)
    arrive(*mixed_rows)

    query = mixed[:, :, :, 0:HS].reshape(ROWS, HS).astype(F32)
    keyraw = mixed[:, :, :, HS : 2 * HS].reshape(ROWS, HS).astype(F32)
    vals = mixed[:, :, :, 2 * HS : 3 * HS].reshape(ROWS, HS)
    query_scale = lax.rsqrt(jnp.mean(query * query, axis=-1, keepdims=True) + 1e-06)
    key_scale = lax.rsqrt(jnp.mean(keyraw * keyraw, axis=-1, keepdims=True) + 1e-06)
    qn[...] = (query * query_scale).astype(BF16)
    kn[...] = (keyraw * key_scale).astype(BF16)

    def exp_scores(block):
        first, last = block * BLK, block * BLK + BLK
        raw = dot_nt(qn[first:last], kn[0:last])
        row = lax.broadcasted_iota(jnp.int32, (BLK, 1), 0) + first
        visible = lax.broadcasted_iota(jnp.int32, (1, last), 1) <= row
        return jnp.where(visible, jnp.exp(raw * FACTOR), 0.0)

    inverse = []
    for block in range(4):
        expo = exp_scores(block)
        inverse.append(1.0 / jnp.sum(expo, axis=-1, keepdims=True))
        attended = dot_nn(expo.astype(BF16), vals[0 : block * BLK + BLK]) * inverse[block]
        mixed[2 * block : 2 * block + 2, :, :, ATT:MIX] = attended.astype(BF16).reshape(2, NY, 32, HS)
    own_rows, twin_half = pl.multiple_of(c * CAP, CAP), pl.multiple_of(net.o * CAP, CAP)
    mixed_copy = net.send(mixed.at[:, :, pl.ds(twin_half, CAP), HID:MIX], mixed2, net.twin)

    for items in (back_0, back_1, back_2, back_3, back_4):
        collect(dj, items)
    give(net, datt, slice(0, HS), (dj[:, :, 256:WOUTP].reshape(BLK, HS) * gate).astype(BF16))
    datt_gather = MpGather(net, datt, slice(0, HS))
    dhidden = dj[:, :, 0:256].reshape(BLK, 256)[:, 0:FFD] * gate
    dup = (dhidden * gate_in * sigma).astype(BF16)
    dgate_in = (dhidden * up_in * sigma * (1.0 + gate_in * (1.0 - sigma))).astype(BF16)
    give(net, dproj, slice(384, 896), jnp.concatenate([dgate_in, dup, jnp.zeros((BLK, 64), BF16)], axis=-1))
    ff_ring = MpRing(net, dproj, slice(384, WINP))

    def rows_of(full, pairs, lanes, first):
        rows = [full[pl.ds(2 * pair, 2), :, pl.ds(first, CAP), lanes] for pair in pairs]
        return jnp.concatenate([part.reshape(BLK // 2, part.shape[-1]) for part in rows], axis=0)

    def both_cores(full, lanes, weights, twin_rows, twin_weights, copies):
        def product(pairs):
            own = dot_nn(rows_of(full, pairs, lanes, own_rows), weights[...])
            while copies:
                arrive(copies.pop())
            return own + dot_nn(rows_of(twin_rows, pairs, slice(0, twin_rows.shape[-1]), 0), twin_weights[...])

        return product

    pair = lax.div(z, 2)
    turned = 1 - 2 * lax.rem(z, 2)
    far_first = (mod(pair + 2, 4), mod(pair + turned, 4), mod(pair - turned, 4), pair)
    n_bufs = len(bufs) // 2
    dproj_copies = twin_weights[1:]
    delta_sum = SeqSum(
        net, bufs[:n_bufs], delta,
        both_cores(mixed, slice(HID, MIX), woutp, mixed2, woutp2, [twin_weights[0], mixed_copy]), far_first,
    )
    dnormed_sum = SeqSum(
        net, bufs[n_bufs:], dnormed,
        both_cores(dproj, slice(0, WINP), winp, dproj2, winp2, dproj_copies), far_first,
    )
    delta_sum.multiply()
    datt_gather.done()

    def norm_back(values, scale, grads):
        return scale * grads - values * scale**3 * jnp.mean(grads * values, axis=-1, keepdims=True)

    for block in range(3, -1, -1):
        first, last = block * BLK, block * BLK + BLK
        prob = exp_scores(block) * inverse[block]
        dout = datt[2 * block : 2 * block + 2].reshape(BLK, HS)
        dprob = dot_nt(dout, vals[0:last])
        inner = jnp.sum(prob * dprob, axis=-1, keepdims=True)
        dscore = (prob * (dprob - inner)).astype(BF16)
        dquery_n = dot_nn(dscore, kn[0:last]) * FACTOR
        dquery = norm_back(query[first:last], query_scale[first:last], dquery_n)
        dproj[2 * block : 2 * block + 2, :, :, 0:HS] = dquery.astype(BF16).reshape(2, NY, 32, HS)
        dkey_part = dot_tn(dscore, qn[first:last])
        dvalue_part = dot_tn(prob.astype(BF16), dout)
        if block == 3:
            dkey_n[...] = dkey_part
            dvalues[...] = dvalue_part
        else:
            dkey_n[0:last] = dkey_n[0:last] + dkey_part
            dvalues[0:last] = dvalues[0:last] + dvalue_part
        if block == 2:
            ff_ring.pass_on()
    dkey = norm_back(keyraw, key_scale, dkey_n[...] * FACTOR)
    dproj[:, :, :, HS : 2 * HS] = dkey.astype(BF16).reshape(NZ, NY, 32, HS)
    dproj[:, :, :, 2 * HS : 3 * HS] = dvalues[...].astype(BF16).reshape(NZ, NY, 32, HS)
    delta_sum.turn()
    ff_ring.done()
    dproj_copies.append(net.send(dproj.at[:, :, pl.ds(twin_half, CAP)], dproj2, net.twin))
    dnormed_sum.multiply()
    while delta_sum.turn():
        pass

    rows = g0[z, y, c].astype(F32)
    grads = g1[z, y, c].astype(F32)
    delta_b = delta[...].astype(BF16).astype(F32)
    small = lax.broadcasted_iota(jnp.int32, (CAP, 128), 1)

    def summed(which):
        return stats[which, 0] + stats[which, 1] + stats[which, 2] + stats[which, 3]

    def pick(tile, at):
        return jnp.sum(jnp.where(small == at, tile, 0.0), axis=-1, keepdims=True)

    def spread(which):
        own = fin.at[which, net.w]
        return net.group([(own, own, device) for device in (net.mate, net.cross, net.twin)], fin.at[which, 0:3])

    stats[1, 3] = row_sums((CAP, 128), (grads * delta_b,))
    arrive(first_stats)
    tile = summed(0)
    in_scale = lax.rsqrt(pick(tile, 0) / D + 1e-05)
    gate = jax.nn.sigmoid(pick(tile, 1))
    fin[0, net.w] = (rows + gate * delta_b).astype(BF16)
    gate_stats = stats_out(1)
    first_rows = spread(0)
    while dnormed_sum.turn():
        pass
    dn = dnormed[...]
    stats[2, 3] = row_sums((CAP, 128), (dn * rows,))
    last_stats = stats_out(2)
    arrive(gate_stats)
    dlogit = pick(summed(1), 0) * gate * (1.0 - gate)
    base = grads + dlogit * rw_ref[...]
    dn = in_scale * dn
    arrive(first_rows, last_stats)
    dinput = (dn - rows * in_scale**3 * (pick(summed(2), 0) / D)).astype(BF16).astype(F32)
    fin[1, net.w] = (base + dinput).astype(BF16)
    last_rows = spread(1)
    fin_out[0] = fin[0]
    arrive(last_rows)
    fin_out[1] = fin[1]
    net.finish()


def place_kernel(sel_ref, fin_ref, res_ref, cot_ref, output_ref, grad_ref):
    sel = sel_ref[...]
    chosen = dot_tn(sel, jnp.ones((4 * CAP, 128), BF16))[:, 0:1] > 0.5
    for which, (source, target) in enumerate(((res_ref, output_ref), (cot_ref, grad_ref))):
        back = dot_tn(sel, fin_ref[which]).astype(BF16)
        target[...] = jnp.where(chosen, back, source[...])


def sum_scratch():
    return [
        pltpu.VMEM((NZ, NY, CAP, QD), BF16),
        pltpu.VMEM((NY, CAP, AW), BF16),
        pltpu.VMEM((NZ, CAP, BW), BF16),
        pltpu.VMEM((NZ, NY, CAP, AW), BF16),
        pltpu.VMEM((NY - 1, CAP, AW), BF16),
        pltpu.VMEM((NY - 1, NZ, CAP, BW), BF16),
        pltpu.VMEM((NZ, CAP, BW), BF16),
    ]


def local(residual, chosen_pos, chosen_count, router_weight, weight_in, weight_out, cotangent):
    n_sem = 95
    scratch = [
        pltpu.SemaphoreType.DMA((n_sem,)),
        pltpu.SemaphoreType.DMA((n_sem,)),
        pltpu.SemaphoreType.DMA((3,)),
        pltpu.VMEM((WINP, QD), BF16),
        pltpu.VMEM((WOUTP, QD), BF16),
        pltpu.VMEM((2, 8, 128), jnp.int32),
        pltpu.VMEM((2, 2, 2, CAP, QD), BF16),
        pltpu.VMEM((2, 2, CAP, QD), BF16),
        pltpu.VMEM((3, CAP, QD), BF16),
        pltpu.VMEM((NZ, NY, 2, CAP, QD), BF16),
        pltpu.VMEM((NZ, NY, 2, CAP, QD), BF16),
        pltpu.VMEM((NZ, NX, 32, WINP), BF16),
        pltpu.VMEM((NZ, NX - 1, 32, WINP), BF16),
        pltpu.VMEM((NZ, NX, 32, WOUTP), BF16),
        pltpu.VMEM((NZ, NX - 1, 32, WOUTP), BF16),
        pltpu.VMEM((NZ, 32, WINP), F32),
        pltpu.VMEM((NZ, 32, WOUTP), F32),
        pltpu.VMEM((NZ, NY, 32, MIX), BF16),
        pltpu.VMEM((NZ, NY, 32, HS), BF16),
        pltpu.VMEM((NZ, NY, 32, WINP), BF16),
        pltpu.VMEM((WINP, QD), BF16),
        pltpu.VMEM((WOUTP, QD), BF16),
        pltpu.VMEM((NZ, NY, CAP, WOUTP), BF16),
        pltpu.VMEM((NZ, NY, CAP, WINP), BF16),
        pltpu.VMEM((ROWS, HS), BF16),
        pltpu.VMEM((ROWS, HS), BF16),
        pltpu.VMEM((ROWS, HS), F32),
        pltpu.VMEM((ROWS, HS), F32),
        pltpu.VMEM((CAP, QD), F32),
        pltpu.VMEM((CAP, QD), F32),
        pltpu.VMEM((3, 4, CAP, 128), F32),
        pltpu.VMEM((2, 4, CAP, QD), BF16),
    ] + sum_scratch() + sum_scratch()
    vmem = pl.BlockSpec(memory_space=pltpu.VMEM)
    anywhere = pl.BlockSpec(memory_space=pl.ANY)
    fin, sel = pl.pallas_call(
        kernel,
        out_shape=[
            jax.ShapeDtypeStruct((2, 4, CAP, QD), BF16),
            jax.ShapeDtypeStruct((4 * CAP, residual.shape[0]), BF16),
        ],
        in_specs=[vmem] * 5 + [anywhere] * 2,
        out_specs=[vmem] * 2,
        scratch_shapes=scratch,
        compiler_params=pltpu.CompilerParams(
            collective_id=0, has_side_effects=True, vmem_limit_bytes=62 * 1024 * 1024
        ),
        cost_estimate=pl.CostEstimate(flops=10**10, bytes_accessed=10**7, transcendentals=10**6),
    )(
        chosen_count[None, :], chosen_pos[None, :], residual, cotangent, router_weight[None, :],
        weight_in.T, weight_out,
    )
    fin = fin.reshape(2, 4 * CAP, QD)
    n_steps = 1
    tokens = residual.shape[0]
    columns = QD // n_steps
    block = pl.BlockSpec((tokens, columns), lambda i: (0, i))
    return pl.pallas_call(
        place_kernel,
        grid=(n_steps,),
        out_shape=[jax.ShapeDtypeStruct(residual.shape, BF16)] * 2,
        in_specs=[
            pl.BlockSpec((4 * CAP, tokens), lambda i: (0, 0)),
            pl.BlockSpec((2, 4 * CAP, columns), lambda i: (0, 0, i)),
            block,
            block,
        ],
        out_specs=[block, block],
    )(sel, fin, residual, cotangent)


def solution(mesh):
    spec = P("seq", "mp")
    return jax.shard_map(
        local,
        mesh=mesh,
        in_specs=(spec, P("seq"), P("seq"), P("mp"), P("mp", "seq"), spec, spec),
        out_specs=(spec, spec),
        check_vma=False,
    )
```
